32 devices in a mesh: seq: 8 (over y, x, core), head: 4 (over z).
Axes of the slice: x: 2, y: 2, z: 4, core: 2. Of those that a mesh axis runs over, the one named last changes fastest.
Arguments:
- inputs: bfloat16 [4, 2048, 1536], P(None, 'seq'), may hold values from -6 to 6
- cotangent: bfloat16 [4, 2048, 1536], P(None, 'seq'), may hold values from -6 to 6
- tail_keys: bfloat16 [4, 1024, 1536], P(None, None, 'head'), may hold values from -6 to 6
- tail_values: bfloat16 [4, 1024, 1536], P(None, None, 'head'), may hold values from -6 to 6
- tail_forget: float32 [4, 1024, 24], P(None, None, 'head'), may hold values from -0.3 to -0.002
- gain_one: bfloat16 [1536], P('seq'), may hold values from 0.5 to 1.5
- gain_two: bfloat16 [1536], P('seq'), may hold values from 0.5 to 1.5
- w_query: bfloat16 [1536, 1536], P('seq', 'head'), may hold values from -0.15625 to 0.15625
- w_key: bfloat16 [1536, 1536], P('seq', 'head'), may hold values from -0.15625 to 0.15625
- w_value: bfloat16 [1536, 1536], P('seq', 'head'), may hold values from -0.15625 to 0.15625
- w_forget: bfloat16 [1536, 24], P('seq', 'head'), may hold values from -0.15625 to 0.15625
- forget_bias: float32 [24], replicated, may hold values from 1 to 8
- query_gain: bfloat16 [64], replicated, may hold values from 0.5 to 1.5
- key_gain: bfloat16 [64], replicated, may hold values from 0.5 to 1.5
- w_outgate: bfloat16 [1536, 1536], P('seq', 'head'), may hold values from -0.15625 to 0.15625
- w_out: bfloat16 [1536, 1536], P('head', 'seq'), may hold values from -0.625 to 0.625
- w_gate: bfloat16 [1536, 4096], P('seq', 'head'), may hold values from -0.15625 to 0.15625
- w_up: bfloat16 [1536, 4096], P('seq', 'head'), may hold values from -0.15625 to 0.15625
- w_down: bfloat16 [4096, 1536], P('head', 'seq'), may hold values from -0.09375 to 0.09375
Outputs:
- layer_out: bfloat16 [4, 2048, 1536], P(None, 'seq')
- input_grad: float32 [4, 2048, 1536], P(None, 'seq')
- grad_gain_one: float32 [1536], P('seq')
- grad_gain_two: float32 [1536], P('seq')
- grad_query: float32 [1536, 1536], P('seq', 'head')
- grad_key: float32 [1536, 1536], P('seq', 'head')
- grad_value: float32 [1536, 1536], P('seq', 'head')
- grad_forget: float32 [1536, 24], P('seq', 'head')
- grad_forget_bias: float32 [24], replicated
- grad_query_gain: float32 [64], replicated
- grad_key_gain: float32 [64], replicated
- grad_outgate: float32 [1536, 1536], P('seq', 'head')
- grad_out: float32 [1536, 1536], P('head', 'seq')
- grad_gate: float32 [1536, 4096], P('seq', 'head')
- grad_up: float32 [1536, 4096], P('seq', 'head')
- grad_down: float32 [4096, 1536], P('head', 'seq')
The draws below stay inside these ranges and needn't reach their ends.
All inputs are finite; a program needn't handle non-finite values.
Results may differ from the reference program's by a relative error of at most 0.025.
Values may be sent and summed in bfloat16 or wider, within the bound.
No kernel may reach another device: no remote copies, remote signals or barrier semaphores. Data moves between devices by JAX's collectives and lax.ppermute only.
A program may use at most 320 MiB of HBM per device.

```python
import jax
import jax.numpy as jnp
from jax import lax

HEADS = 24
HEAD_SIZE = 64
FF = 4096
D = 1536
MICRO = 4
TAIL = 1024
SEQLEN = 2048


def steps_of(key, shape, cuts, least, high):
    gain = 1.0
    for axis_at, parts in cuts:
        draws = jax.random.uniform(jax.random.fold_in(jax.random.fold_in(key, 6), axis_at), (parts,), jnp.float32, least / len(cuts), high / len(cuts))
        gain = gain * jnp.repeat(jnp.exp(draws), shape[axis_at] // parts).reshape((-1,) + (1,) * (len(shape) - 1 - axis_at))
    return gain


def gaussian(rng, shape, deviation, bound, split=(), held_as=jnp.bfloat16):
    values = jax.random.normal(rng, shape, jnp.float32) * deviation
    if len(split) > 0:
        values = steps_of(rng, shape, split, -0.22, 0.18) * values
    return jnp.clip(values, min=-bound, max=bound).astype(held_as)


def setup_inputs(seed: int = 0) -> dict:
    streams_of = jax.random.split(jax.random.key(seed), 20)
    inputs = gaussian(streams_of[0], (MICRO, SEQLEN, D), 1.0, 6.0, ((1, 8),))
    cotangent = gaussian(streams_of[1], (MICRO, SEQLEN, D), 1.0, 6.0, ((1, 8),))
    tail_keys = gaussian(streams_of[2], (MICRO, TAIL, D), 1.0, 6.0, ((2, 4),))
    tail_values = gaussian(streams_of[3], (MICRO, TAIL, D), 1.0, 6.0, ((2, 4),))
    tail_forget = jnp.clip(-0.3 + 0.298 * jax.random.uniform(streams_of[4], (MICRO, TAIL, HEADS), jnp.float32) ** steps_of(streams_of[4], (MICRO, TAIL, HEADS), ((2, 4),), -0.2, 0.2), -0.3, -0.002)
    gain_one = jnp.clip(1.0 + 0.1 * jax.random.normal(streams_of[5], (D,), jnp.float32), 0.5, 1.5).astype(jnp.bfloat16)
    gain_two = jnp.clip(1.0 + 0.1 * jax.random.normal(streams_of[6], (D,), jnp.float32), 0.5, 1.5).astype(jnp.bfloat16)
    w_query = gaussian(streams_of[7], (D, D), D ** -0.5, 0.15625, ((0, 8), (1, 4)))
    w_key = gaussian(streams_of[8], (D, D), D ** -0.5, 0.15625, ((0, 8), (1, 4)))
    w_value = gaussian(streams_of[9], (D, D), D ** -0.5, 0.15625, ((0, 8), (1, 4)))
    w_forget = gaussian(streams_of[10], (D, HEADS), D ** -0.5, 0.15625, ((0, 8), (1, 4)))
    forget_bias = jnp.clip(jax.random.uniform(streams_of[11], (HEADS,), jnp.float32, 1.0, 8.0), 1.0, 8.0)
    query_gain = jnp.clip(1.0 + 0.1 * jax.random.normal(streams_of[12], (HEAD_SIZE,), jnp.float32), 0.5, 1.5).astype(jnp.bfloat16)
    key_gain = jnp.clip(1.0 + 0.1 * jax.random.normal(streams_of[13], (HEAD_SIZE,), jnp.float32), 0.5, 1.5).astype(jnp.bfloat16)
    w_outgate = gaussian(streams_of[14], (D, D), D ** -0.5, 0.15625, ((0, 8), (1, 4)))
    w_out = gaussian(streams_of[15], (D, D), (D // 16) ** -0.5, 0.625, ((0, 4), (1, 8)))
    w_gate = gaussian(streams_of[16], (D, FF), D ** -0.5, 0.15625, ((0, 8), (1, 4)))
    w_up = gaussian(streams_of[17], (D, FF), D ** -0.5, 0.15625, ((0, 8), (1, 4)))
    w_down = gaussian(streams_of[18], (FF, D), FF ** -0.5, 0.09375, ((0, 4), (1, 8)))
    return {"inputs": inputs, "cotangent": cotangent, "tail_keys": tail_keys, "tail_values": tail_values, "tail_forget": tail_forget, "gain_one": gain_one, "gain_two": gain_two, "w_query": w_query, "w_key": w_key, "w_value": w_value, "w_forget": w_forget, "forget_bias": forget_bias, "query_gain": query_gain, "key_gain": key_gain, "w_outgate": w_outgate, "w_out": w_out, "w_gate": w_gate, "w_up": w_up, "w_down": w_down}


epsilon = 1e-06
highest = lax.Precision.HIGHEST

@jax.custom_vjp
def low(v):
    return lax.optimization_barrier(v.astype(jnp.bfloat16)).astype(jnp.float32)

@jax.custom_vjp
def low_back(v):
    return v

def low_keep(v):
    return (low(v), None)

def low_pass(kept, grad):
    return (grad,)

def back_keep(v):
    return (v, None)

def back_low(kept, grad):
    return (low(grad),)
low.defvjp(low_keep, low_pass)
low_back.defvjp(back_keep, back_low)

def matmul(left_side, right_side):
    return jnp.dot(left_side, right_side, precision=highest)

def rms_factor(values):
    return lax.rsqrt(lax.optimization_barrier(jnp.mean(values * values, axis=-1, keepdims=True)) + epsilon)

def head_normed(raw_rows, gain_row):
    shaped = raw_rows.reshape(raw_rows.shape[0], HEADS, HEAD_SIZE)
    return (shaped * rms_factor(shaped) * gain_row).reshape(raw_rows.shape)

def layer_forward(params, inputs, tail_key_rows, tail_value_rows, tail_decay):
    gain_one, gain_two, w_query, w_key, w_value, w_forget, forget_bias, query_gain, key_gain, w_outgate, w_out, w_gate, w_up, w_down = params
    length = inputs.shape[0]
    score_scale = HEAD_SIZE ** (-0.5)
    normed = low(inputs * rms_factor(inputs) * gain_one)
    query_raw = low_back(matmul(normed, w_query))
    key_raw = low_back(matmul(normed, w_key))
    value_rows = low(low_back(matmul(normed, w_value)))
    forget_logit = low_back(matmul(normed, w_forget) + forget_bias)
    gate_logit = low_back(matmul(normed, w_outgate))
    decay_sum = jnp.cumsum(jax.nn.log_sigmoid(forget_logit), axis=0)
    queries = low(head_normed(query_raw, query_gain))
    key_rows = low(head_normed(key_raw, key_gain))
    all_keys = jnp.concatenate([tail_key_rows, key_rows], 0).reshape(-1, HEADS, HEAD_SIZE)
    all_values = jnp.concatenate([tail_value_rows, value_rows], 0).reshape(-1, HEADS, HEAD_SIZE)
    all_decay = jnp.concatenate([tail_decay, decay_sum], 0)
    key_place = jnp.arange(all_keys.shape[0], dtype=jnp.int32) - TAIL
    query_rows = min(512, length)

    def attend(block_index):
        first_row = block_index * query_rows
        block_queries = lax.dynamic_slice_in_dim(queries, first_row, query_rows, 0).reshape(query_rows, HEADS, HEAD_SIZE)
        block_decay = lax.dynamic_slice_in_dim(decay_sum, first_row, query_rows, 0)
        scores = jnp.einsum('qhd,khd->qhk', block_queries, all_keys, precision=highest) * score_scale
        scores = low_back(scores + block_decay[:, :, None] - all_decay.T[None, :, :])
        query_place = first_row + jnp.arange(query_rows, dtype=jnp.int32)
        visible = key_place[None, :] <= query_place[:, None]
        scores = jnp.where(visible[:, None, :], scores, -jnp.inf)
        weights = low(jax.nn.softmax(scores, axis=-1))
        mixture = jnp.einsum('qhk,khd->qhd', weights, all_values, precision=highest)
        return mixture.reshape(query_rows, HEADS * HEAD_SIZE)
    attended = lax.map(jax.checkpoint(attend), jnp.arange(length // query_rows, dtype=jnp.int32))
    attended = low_back(attended.reshape(length, HEADS * HEAD_SIZE))
    gate_value = jax.nn.sigmoid(gate_logit)
    gated_rows = low(attended * gate_value)
    hidden = inputs + low_back(matmul(gated_rows, w_out))
    normed_two = low(hidden * rms_factor(hidden) * gain_two)
    gate_raw = low_back(matmul(normed_two, w_gate))
    up_raw = low_back(matmul(normed_two, w_up))
    activated = low(jax.nn.silu(gate_raw) * up_raw)
    return hidden + matmul(activated, w_down)

def reference(inputs, cotangent, tail_keys, tail_values, tail_forget, gain_one, gain_two, w_query, w_key, w_value, w_forget, forget_bias, query_gain, key_gain, w_outgate, w_out, w_gate, w_up, w_down):
    params = tuple((weight_arg.astype(jnp.float32) for weight_arg in (gain_one, gain_two, w_query, w_key, w_value, w_forget, forget_bias, query_gain, key_gain, w_outgate, w_out, w_gate, w_up, w_down)))
    tail_decays = jnp.cumsum(tail_forget, axis=1) - lax.optimization_barrier(jnp.sum(tail_forget, axis=1, keepdims=True))

    def one_micro(totals, slices):
        micro_in, micro_cot, micro_keys, micro_values, micro_decay = slices

        def forward(weights_all, layer_in):
            return layer_forward(weights_all, layer_in, micro_keys.astype(jnp.float32), micro_values.astype(jnp.float32), micro_decay)
        output, pullback = jax.vjp(forward, params, micro_in.astype(jnp.float32))
        weight_grads, input_grad = pullback(micro_cot.astype(jnp.float32))
        totals = jax.tree.map(jnp.add, totals, weight_grads)
        return (totals, (output.astype(jnp.bfloat16), input_grad))
    zero_grads = jax.tree.map(jnp.zeros_like, params)
    totals, (outputs, input_grads) = lax.scan(one_micro, zero_grads, (inputs, cotangent, tail_keys, tail_values, tail_decays))
    return (outputs, input_grads, totals[0], totals[1], totals[2], totals[3], totals[4], totals[5], totals[6], totals[7], totals[8], totals[9], totals[10], totals[11], totals[12], totals[13])
```

```python
import functools

import jax
import jax.numpy as jnp
from jax import lax
from jax.experimental import pallas as pl
from jax.experimental.pallas import tpu as pltpu
from jax.sharding import PartitionSpec as P

HEAD_SIZE = 64
LANES = 128
EPSILON = 1e-06
F32 = jnp.float32
BF16 = jnp.bfloat16
NN = (((1,), (0,)), ((), ()))
NT = (((1,), (1,)), ((), ()))
HIDE = -1e30
SCALE = HEAD_SIZE**-0.5
MIB = 1024 * 1024


def dot(left, right, dims=NN):
    return lax.dot_general(left, right, dims, preferred_element_type=F32)


def params(mib=48):
    return pltpu.CompilerParams(vmem_limit_bytes=mib * MIB)


def lanes_of(rows):
    return lax.broadcasted_iota(jnp.int32, (rows, LANES), 1)


def swap_halves(block):
    return pltpu.roll(block, HEAD_SIZE, 1)


def in_three(value):
    high = value.astype(BF16).astype(F32)
    rest = value - high
    middle = rest.astype(BF16).astype(F32)
    return high, middle, rest - middle


def at_lanes(lane, first, parts, base):
    for place, part in enumerate(parts):
        base = jnp.where(lane == first + place, part, base)
    return base


def triangle(rows, lower):
    down = lax.broadcasted_iota(jnp.int32, (rows, rows), 0)
    across = lax.broadcasted_iota(jnp.int32, (rows, rows), 1)
    return jnp.where(down >= across if lower else down <= across, 1.0, 0.0).astype(BF16)


def running_sum(tri, column, lane):
    spread = at_lanes(lane, 0, in_three(column), jnp.zeros(lane.shape, F32))
    sums = dot(tri, spread.astype(BF16))
    return sums[:, 0:1] + sums[:, 1:2] + sums[:, 2:3]


def forget_column(tail_block):
    return tail_block[:, 64:65] + tail_block[:, 65:66] + tail_block[:, 66:67]


def per_head(low, values):
    first = jnp.sum(jnp.where(low, values, 0.0), axis=-1, keepdims=True)
    second = jnp.sum(jnp.where(low, 0.0, values), axis=-1, keepdims=True)
    return jnp.where(low, first, second) * (1.0 / HEAD_SIZE)


def rms_factor(values):
    return lax.rsqrt(jnp.mean(values * values, axis=-1, keepdims=True) + EPSILON)


def merge_pair(low, first, second):
    return jnp.where(low, first, swap_halves(second))


def merge_swapped(low, first, second):
    return jnp.where(low, swap_halves(first), second)


def unpack_rows(low_half, first, second):
    top = jnp.where(low_half, first, swap_halves(second))
    bottom = jnp.where(low_half, swap_halves(first), second)
    return jnp.concatenate([top, bottom], axis=0)


def pack_rows(low_half, block):
    half = block.shape[0] // 2
    top, bottom = block[:half], block[half:]
    first = jnp.where(low_half, top, swap_halves(bottom))
    second = jnp.where(low_half, swap_halves(top), bottom)
    return first, second


def project_kernel(
    heads, x_ref, w_ref, bias_ref, gain_ref, gq_ref, gk_ref, a_ref, raw_ref, gl_ref, pay_ref
):
    x = x_ref[...].astype(F32)
    rows = x.shape[0]
    cols = gl_ref.shape[1]
    a = (x * rms_factor(x) * gain_ref[...]).astype(BF16)
    a_ref[...] = a
    proj = dot(a, w_ref[...])
    raw_ref[...] = proj[:, : 2 * cols]
    gl_ref[...] = proj[:, 3 * cols : 4 * cols]
    logit = proj[:, 4 * cols :] + bias_ref[...]
    lane = lanes_of(rows)
    low = lane < HEAD_SIZE
    for group in range(cols // LANES):
        at = group * LANES
        query = proj[:, at : at + LANES]
        key = proj[:, cols + at : cols + at + LANES]
        value = proj[:, 2 * cols + at : 2 * cols + at + LANES]
        query = query * lax.rsqrt(per_head(low, query * query) + EPSILON) * gq_ref[...]
        key = key * lax.rsqrt(per_head(low, key * key) + EPSILON) * gk_ref[...]
        for half in range(2):
            head = 2 * group + half
            if head >= heads:
                continue
            zl = at_lanes(lane, 64, in_three(logit[:, head : head + 1]), jnp.zeros(lane.shape, F32))
            if half == 0:
                both = merge_pair(low, query, key)
                rest = jnp.where(low, value, zl)
            else:
                both = merge_swapped(low, query, key)
                rest = jnp.where(low, swap_halves(value), zl)
            pay_ref[head, :, :LANES] = both.astype(BF16)
            pay_ref[head, :, LANES:] = rest.astype(BF16)


def project(heads, cols, x, weights, bias_row, gain_row, gq_row, gk_row, micros):
    total, width = x.shape
    rows = total // micros
    wide = weights.shape[1]
    whole = lambda m: (0, 0)
    part = lambda m: (m, 0)
    return pl.pallas_call(
        functools.partial(project_kernel, heads),
        grid=(micros,),
        in_specs=[
            pl.BlockSpec((rows, width), part),
            pl.BlockSpec((width, wide), whole),
            pl.BlockSpec((1, LANES), whole),
            pl.BlockSpec((1, width), whole),
            pl.BlockSpec((1, LANES), whole),
            pl.BlockSpec((1, LANES), whole),
        ],
        out_specs=[
            pl.BlockSpec((rows, width), part),
            pl.BlockSpec((rows, 2 * cols), part),
            pl.BlockSpec((rows, cols), part),
            pl.BlockSpec((heads, rows, 2 * LANES), lambda m: (m, 0, 0)),
        ],
        out_shape=[
            jax.ShapeDtypeStruct((total, width), BF16),
            jax.ShapeDtypeStruct((total, 2 * cols), F32),
            jax.ShapeDtypeStruct((total, cols), F32),
            jax.ShapeDtypeStruct((micros * heads, rows, 2 * LANES), BF16),
        ],
        compiler_params=params(),
        cost_estimate=pl.CostEstimate(
            flops=2 * total * width * wide,
            bytes_accessed=2 * width * wide + 10 * total * width,
            transcendentals=0,
        ),
        name="project",
    )(x, weights, bias_row, gain_row, gq_row, gk_row)


def attend_kernel(size, pay_ref, tk_ref, tv_ref, ap_ref, af_ref, q_ref, k_ref, v_ref):
    blocks, _, rows, _ = pay_ref.shape
    length = blocks * rows
    lane = lanes_of(rows)
    low = lane < HEAD_SIZE
    tri = triangle(rows, True)
    zero = jnp.zeros(lane.shape, F32)

    def build(b, carry):
        at = pl.ds(pl.multiple_of(b * rows, rows), rows)
        both = pay_ref[b, 0, :, :LANES].astype(F32)
        rest = pay_ref[b, 0, :, LANES:].astype(F32)
        logit = forget_column(rest)
        log_forget = jnp.minimum(logit, 0.0) - jnp.log1p(jnp.exp(-jnp.abs(logit)))
        decay = running_sum(tri, log_forget, lane) + carry
        high, middle, least = in_three(decay)
        query_side = at_lanes(lane, 64, (high, middle, least, 1.0, 1.0, 1.0), zero)
        key_side = at_lanes(lane, 64, (1.0, 1.0, 1.0, -high, -middle, -least), zero)
        value_side = at_lanes(lane, 64, (1.0, 1.0, 1.0), zero)
        q_ref[0, at, :] = jnp.where(low, both * SCALE, query_side).astype(BF16)
        k_ref[0, at, :] = jnp.where(low, swap_halves(both), key_side).astype(BF16)
        v_ref[0, at, :] = jnp.where(low, rest, value_side).astype(BF16)
        return decay[rows - 1 :, :]

    lax.fori_loop(0, blocks, build, jnp.zeros((1, 1), F32))

    tail_length = tk_ref.shape[1]
    visible = lax.broadcasted_iota(jnp.int32, (size, size), 0) >= lax.broadcasted_iota(
        jnp.int32, (size, size), 1
    )
    half_low = lanes_of(rows // 2) < HEAD_SIZE
    lane_here = lanes_of(size)

    def one_block(qi, carry):
        at = pl.ds(pl.multiple_of(qi * size, size), size)
        query = q_ref[0, at, :]

        def absorb(key, value, total, masked=False):
            scores = dot(query, key, NT)
            if masked:
                scores = jnp.where(visible, scores, HIDE)
            return total + dot(jnp.exp(scores).astype(BF16), value)

        total = jnp.zeros((size, LANES), F32)
        for t in range(tail_length // size):
            here = pl.ds(t * size, size)
            total = absorb(tk_ref[0, here, :], tv_ref[0, here, :], total)

        def earlier(ki, total):
            here = pl.ds(pl.multiple_of(ki * size, size), size)
            return absorb(k_ref[0, here, :], v_ref[0, here, :], total)

        total = lax.fori_loop(0, qi, earlier, total)
        total = absorb(k_ref[0, at, :], v_ref[0, at, :], total, True)
        weight = total[:, 64:65]
        mixture = total / weight
        af_ref[0, at, :] = mixture
        for piece in range(size // rows):
            block = mixture[piece * rows : (piece + 1) * rows]
            packed = jnp.where(
                half_low, block[: rows // 2], swap_halves(block[rows // 2 :])
            )
            ap_ref[qi * (size // rows) + piece, 0] = packed.astype(BF16)
        old = query.astype(F32)
        shifted = forget_column(old) - jnp.log(weight)
        q_ref[0, at, :] = at_lanes(lane_here, 64, in_three(shifted), old).astype(BF16)
        return carry

    lax.fori_loop(0, length // size, one_block, 0)


def attend(pay, tail_key, tail_value):
    blocks, pairs, rows, _ = pay.shape
    length = blocks * rows
    tail_length = tail_key.shape[1]
    size = min(512, length)
    pair = lambda j: (j, 0, 0)
    across = lambda j: (0, j, 0, 0)
    entries = length * (tail_length + length // 2) * pairs
    return pl.pallas_call(
        functools.partial(attend_kernel, size),
        grid=(pairs,),
        in_specs=[
            pl.BlockSpec((blocks, 1, rows, 2 * LANES), across),
            pl.BlockSpec((1, tail_length, LANES), pair),
            pl.BlockSpec((1, tail_length, LANES), pair),
        ],
        out_specs=[
            pl.BlockSpec((blocks, 1, rows // 2, LANES), across),
            pl.BlockSpec((1, length, LANES), pair),
            pl.BlockSpec((1, length, LANES), pair),
            pl.BlockSpec((1, length, LANES), pair),
            pl.BlockSpec((1, length, LANES), pair),
        ],
        out_shape=[
            jax.ShapeDtypeStruct((blocks, pairs, rows // 2, LANES), BF16),
            jax.ShapeDtypeStruct((pairs, length, LANES), F32),
            jax.ShapeDtypeStruct((pairs, length, LANES), BF16),
            jax.ShapeDtypeStruct((pairs, length, LANES), BF16),
            jax.ShapeDtypeStruct((pairs, length, LANES), BF16),
        ],
        compiler_params=params(),
        cost_estimate=pl.CostEstimate(
            flops=16 * LANES * entries, bytes_accessed=8 * pairs * length * LANES, transcendentals=entries
        ),
        name="attend",
    )(pay, tail_key, tail_value)


def attend_back_kernel(
    size,
    q_ref,
    k_ref,
    v_ref,
    tk_ref,
    tv_ref,
    af_ref,
    dap_ref,
    rest_ref,
    g_ref,
    da_ref,
    dqt_ref,
    sums_ref,
):
    blocks, _, rows, _ = rest_ref.shape
    length = blocks * rows
    lane = lanes_of(rows)
    low = lane < HEAD_SIZE
    zero = jnp.zeros(lane.shape, F32)

    def build(b, carry):
        at = pl.ds(pl.multiple_of(b * rows, rows), rows)
        packed = dap_ref[b, 0].astype(F32)
        grad = jnp.concatenate([packed, swap_halves(packed)], axis=0)
        grad = jnp.where(low, grad, 0.0)
        delta = jnp.sum(grad * af_ref[0, at, :], axis=-1, keepdims=True)
        da_ref[at, :] = at_lanes(lane, 64, in_three(-delta), grad).astype(BF16)
        return carry

    lax.fori_loop(0, blocks, build, 0)

    across = lax.broadcasted_iota(jnp.int32, (size, size), 1)
    down = lax.broadcasted_iota(jnp.int32, (size, size), 0)
    visible = across >= down
    count = length // size

    def block_at(i):
        return pl.ds(pl.multiple_of(i * size, size), size)

    def pieces(key, value, at, masked=False):
        scores = dot(key, q_ref[0, at, :], NT)
        if masked:
            scores = jnp.where(visible, scores, HIDE)
        prob = jnp.exp(scores)
        score_grad = prob * dot(value, da_ref[at, :], NT)
        return prob.astype(BF16), score_grad.astype(BF16)

    tail_length = tk_ref.shape[1]
    tail_count = tail_length // size

    def tail_block(qi, carry):
        at = block_at(qi)
        total = jnp.zeros((LANES, size), F32)
        for t in range(tail_count):
            key = tk_ref[0, pl.ds(t * size, size), :]
            _, score_grad = pieces(key, tv_ref[0, pl.ds(t * size, size), :], at)
            total = total + dot(key.T, score_grad)
        dqt_ref[:, at] = total
        return carry

    lax.fori_loop(0, count, tail_block, 0)
    lane_here = lanes_of(size)
    low_here = lane_here < HEAD_SIZE

    def key_block(ki, carry):
        own = block_at(ki)
        key = k_ref[0, own, :]
        value = v_ref[0, own, :]
        key_turned = key.T

        def one(at, sums, masked=False):
            key_sum, value_sum = sums
            prob, score_grad = pieces(key, value, at, masked)
            dqt_ref[:, at] += dot(key_turned, score_grad)
            return (
                key_sum + dot(score_grad, q_ref[0, at, :]),
                value_sum + dot(prob, da_ref[at, :]),
            )

        start = (jnp.zeros((size, LANES), F32), jnp.zeros((size, LANES), F32))
        sums = one(own, start, True)
        key_sum, value_sum = lax.fori_loop(
            ki + 1, count, lambda qi, sums: one(block_at(qi), sums), sums
        )
        sums_ref[own, :] = key_sum
        for piece in range(size // rows):
            here = slice(piece * rows, (piece + 1) * rows)
            g_ref[ki * (size // rows) + piece, 0, :, LANES:] = value_sum[here].astype(BF16)
        return carry

    lax.fori_loop(0, count, key_block, 0)

    tri = triangle(rows, False)

    def finish(i, carry):
        b = blocks - 1 - i
        at = pl.ds(pl.multiple_of(b * rows, rows), rows)
        query = dqt_ref[:, at].T
        key = sums_ref[at, :]
        decay_grad = query[:, 64:65] - key[:, 67:68]
        suffix = running_sum(tri, decay_grad, lane) + carry
        logit = forget_column(rest_ref[b, 0].astype(F32))
        forget_grad = suffix / (1.0 + jnp.exp(logit))
        both = jnp.where(low, query * SCALE, swap_halves(key))
        rest = jnp.where(low, g_ref[b, 0, :, LANES:].astype(F32), jnp.where(lane == 64, forget_grad, 0.0))
        g_ref[b, 0, :, :LANES] = both.astype(BF16)
        g_ref[b, 0, :, LANES:] = rest.astype(BF16)
        return suffix[0:1, :]

    lax.fori_loop(0, blocks, finish, jnp.zeros((1, 1), F32))


def attend_back(saved, tail_key, tail_value, mixture, packed_grad, pay):
    blocks, pairs, rows, _ = pay.shape
    length = blocks * rows
    tail_length = tail_key.shape[1]
    size = min(512, length)
    pair = lambda j: (j, 0, 0)
    across = lambda j: (0, j, 0, 0)
    entries = length * (tail_length + length // 2) * pairs
    return pl.pallas_call(
        functools.partial(attend_back_kernel, size),
        grid=(pairs,),
        in_specs=[
            pl.BlockSpec((1, length, LANES), pair),
            pl.BlockSpec((1, length, LANES), pair),
            pl.BlockSpec((1, length, LANES), pair),
            pl.BlockSpec((1, tail_length, LANES), pair),
            pl.BlockSpec((1, tail_length, LANES), pair),
            pl.BlockSpec((1, length, LANES), pair),
            pl.BlockSpec((blocks, 1, rows // 2, LANES), across),
            pl.BlockSpec((blocks, 1, rows, LANES), lambda j: (0, j, 0, 1)),
        ],
        out_specs=pl.BlockSpec((blocks, 1, rows, 2 * LANES), across),
        out_shape=jax.ShapeDtypeStruct((blocks, pairs, rows, 2 * LANES), BF16),
        scratch_shapes=[
            pltpu.VMEM((length, LANES), BF16),
            pltpu.VMEM((LANES, length), F32),
            pltpu.VMEM((length, LANES), F32),
        ],
        compiler_params=params(),
        cost_estimate=pl.CostEstimate(
            flops=40 * LANES * entries, bytes_accessed=10 * pairs * length * LANES, transcendentals=entries
        ),
        name="attend_back",
    )(*saved, tail_key, tail_value, mixture, packed_grad, pay)


def group_of(heads, ref, group, low_half):
    first = ref[2 * group].astype(F32)
    second = ref[2 * group + 1].astype(F32) if 2 * group + 1 < heads else jnp.zeros_like(first)
    return unpack_rows(low_half, first, second)


def gate_kernel(heads, ap_ref, gl_ref, o_ref):
    rows, cols = o_ref.shape
    half_low = lanes_of(rows // 2) < HEAD_SIZE
    for group in range(cols // LANES):
        at = slice(group * LANES, (group + 1) * LANES)
        mixture = group_of(heads, ap_ref, group, half_low)
        o_ref[:, at] = (mixture * jax.nn.sigmoid(gl_ref[:, at])).astype(BF16)


def gate(heads, packed, gl, micros):
    total, cols = gl.shape
    rows = total // micros
    return pl.pallas_call(
        functools.partial(gate_kernel, heads),
        grid=(micros,),
        in_specs=[
            pl.BlockSpec((heads, rows // 2, LANES), lambda m: (m, 0, 0)),
            pl.BlockSpec((rows, cols), lambda m: (m, 0)),
        ],
        out_specs=pl.BlockSpec((rows, cols), lambda m: (m, 0)),
        out_shape=jax.ShapeDtypeStruct((total, cols), BF16),
        compiler_params=params(),
        cost_estimate=pl.CostEstimate(
            flops=4 * total * cols, bytes_accessed=8 * total * cols, transcendentals=total * cols
        ),
        name="gate",
    )(packed, gl)


def feed_kernel(
    chunk,
    ff,
    x_ref,
    dy_ref,
    o_ref,
    w_ref,
    gain_ref,
    hid_ref,
    c_ref,
    u_ref,
    dgr_ref,
    dur_ref,
    out_ref,
    dc_ref,
    dg_ref,
    out_acc,
    dc_acc,
):
    parts, _, cols = o_ref.shape
    hidden = x_ref[...].astype(F32)
    for z in range(parts):
        hidden = hidden + dot(o_ref[z], w_ref[:, z * cols : (z + 1) * cols], NT)
    hid_ref[...] = hidden
    factor = rms_factor(hidden)
    c_ref[...] = (hidden * factor * gain_ref[...]).astype(BF16)
    out_acc[...] = jnp.zeros_like(out_acc)
    dc_acc[...] = jnp.zeros_like(dc_acc)

    def step(i, carry):
        at = pl.multiple_of(i * chunk, chunk)
        here = pl.ds(at, chunk)
        w_gate = w_ref[:, pl.ds(pl.multiple_of(parts * cols + at, LANES), chunk)]
        w_up = w_ref[:, pl.ds(pl.multiple_of(parts * cols + ff + at, LANES), chunk)]
        w_down = w_ref[:, pl.ds(pl.multiple_of(parts * cols + 2 * ff + at, LANES), chunk)]
        c = c_ref[...]
        gr = dot(c, w_gate)
        ur = dot(c, w_up)
        sig = jax.nn.sigmoid(gr)
        silu = gr * sig
        u = (silu * ur).astype(BF16)
        u_ref[:, here] = u
        out_acc[...] += dot(u, w_down, NT)
        du = dot(dy_ref[...], w_down)
        dgr = (du * ur * sig * (1.0 + gr * (1.0 - sig))).astype(BF16)
        dur = (du * silu).astype(BF16)
        dgr_ref[:, here] = dgr
        dur_ref[:, here] = dur
        dc_acc[...] += dot(dgr, w_gate, NT) + dot(dur, w_up, NT)
        return carry

    lax.fori_loop(0, ff // chunk, step, 0)
    out_ref[...] = out_acc[...].astype(BF16)
    dc = dc_acc[...]
    dc_ref[...] = dc.astype(BF16)

    @pl.when(pl.program_id(0) == 0)
    def _():
        dg_ref[...] = jnp.zeros_like(dg_ref)

    dg_ref[...] += jnp.sum(dc * hid_ref[...] * factor, axis=0, keepdims=True)


def feed(x, dy, o_all, weights, gain_row, ff, micros):
    total, width = x.shape
    rows = total // micros
    parts, _, cols = o_all.shape
    chunk = min(512, ff)
    whole = lambda m: (0, 0)
    part = lambda m: (m, 0)
    return pl.pallas_call(
        functools.partial(feed_kernel, chunk, ff),
        grid=(micros,),
        in_specs=[
            pl.BlockSpec((rows, width), part),
            pl.BlockSpec((rows, width), part),
            pl.BlockSpec((parts, rows, cols), lambda m: (0, m, 0)),
            pl.BlockSpec(weights.shape, whole, pipeline_mode=pl.Buffered(1)),
            pl.BlockSpec((1, width), whole),
        ],
        out_specs=[
            pl.BlockSpec((rows, width), part),
            pl.BlockSpec((rows, width), part),
            pl.BlockSpec((rows, ff), part),
            pl.BlockSpec((rows, ff), part),
            pl.BlockSpec((rows, ff), part),
            pl.BlockSpec((rows, width), part),
            pl.BlockSpec((rows, width), part),
            pl.BlockSpec((1, width), whole),
        ],
        out_shape=[
            jax.ShapeDtypeStruct((total, width), F32),
            jax.ShapeDtypeStruct((total, width), BF16),
            jax.ShapeDtypeStruct((total, ff), BF16),
            jax.ShapeDtypeStruct((total, ff), BF16),
            jax.ShapeDtypeStruct((total, ff), BF16),
            jax.ShapeDtypeStruct((total, width), BF16),
            jax.ShapeDtypeStruct((total, width), BF16),
            jax.ShapeDtypeStruct((1, width), F32),
        ],
        scratch_shapes=[pltpu.VMEM((rows, width), F32), pltpu.VMEM((rows, width), F32)],
        compiler_params=params(56),
        cost_estimate=pl.CostEstimate(
            flops=2 * total * width * (parts * cols + 6 * ff),
            bytes_accessed=2 * weights.size + 20 * total * width,
            transcendentals=total * ff,
        ),
        name="feed",
    )(x, dy, o_all, weights, gain_row)


def norm_back(source, factor, gain_row, upstream):
    scaled = upstream * gain_row
    inner = jnp.mean(scaled * source, axis=-1, keepdims=True)
    return factor * scaled - source * (factor * factor * factor) * inner


def hidden_back_kernel(
    heads, dc_ref, hid_ref, dy_ref, gain_ref, w_ref, gl_ref, ap_ref, dh_ref, dhb_ref, dgl_ref, dap_ref
):
    rows, cols = gl_ref.shape
    hidden = hid_ref[...]
    back = norm_back(hidden, rms_factor(hidden), gain_ref[...], dc_ref[...].astype(F32))
    dh = dy_ref[...].astype(F32) + back
    dh_ref[...] = dh
    dhb = dh.astype(BF16)
    dhb_ref[...] = dhb
    gated_grad = dot(dhb, w_ref[...])
    half_low = lanes_of(rows // 2) < HEAD_SIZE
    for group in range(cols // LANES):
        at = slice(group * LANES, (group + 1) * LANES)
        mixture = group_of(heads, ap_ref, group, half_low)
        gate_value = jax.nn.sigmoid(gl_ref[:, at])
        grad = gated_grad[:, at]
        dgl_ref[:, at] = (grad * mixture * gate_value * (1.0 - gate_value)).astype(BF16)
        first, second = pack_rows(half_low, grad * gate_value)
        dap_ref[2 * group] = first.astype(BF16)
        if 2 * group + 1 < heads:
            dap_ref[2 * group + 1] = second.astype(BF16)


def hidden_back(heads, dc, hidden, dy, gain_row, w_own, gl, packed, micros):
    total, width = dc.shape
    rows = total // micros
    cols = gl.shape[1]
    whole = lambda m: (0, 0)
    part = lambda m: (m, 0)
    cube = lambda m: (m, 0, 0)
    return pl.pallas_call(
        functools.partial(hidden_back_kernel, heads),
        grid=(micros,),
        in_specs=[
            pl.BlockSpec((rows, width), part),
            pl.BlockSpec((rows, width), part),
            pl.BlockSpec((rows, width), part),
            pl.BlockSpec((1, width), whole),
            pl.BlockSpec((width, cols), whole),
            pl.BlockSpec((rows, cols), part),
            pl.BlockSpec((heads, rows // 2, LANES), cube),
        ],
        out_specs=[
            pl.BlockSpec((rows, width), part),
            pl.BlockSpec((rows, width), part),
            pl.BlockSpec((rows, cols), part),
            pl.BlockSpec((heads, rows // 2, LANES), cube),
        ],
        out_shape=[
            jax.ShapeDtypeStruct((total, width), F32),
            jax.ShapeDtypeStruct((total, width), BF16),
            jax.ShapeDtypeStruct((total, cols), BF16),
            jax.ShapeDtypeStruct((micros * heads, rows // 2, LANES), BF16),
        ],
        compiler_params=params(),
        cost_estimate=pl.CostEstimate(
            flops=2 * total * width * cols, bytes_accessed=14 * total * width, transcendentals=total * cols
        ),
        name="hidden_back",
    )(dc, hidden, dy, gain_row, w_own, gl, packed)


def project_back_kernel(
    heads,
    g_ref,
    raw_ref,
    x_ref,
    dgl_ref,
    w_ref,
    gq_ref,
    gk_ref,
    grads_ref,
    da_ref,
    dg_ref,
    dgq_ref,
    dgk_ref,
    db_ref,
):
    rows, cols = dgl_ref.shape
    lane = lanes_of(rows)
    low = lane < HEAD_SIZE
    zero = jnp.zeros(lane.shape, F32)

    @pl.when(pl.program_id(0) == 0)
    def _():
        for ref in (dg_ref, dgq_ref, dgk_ref, db_ref):
            ref[...] = jnp.zeros_like(ref)

    def head_back(raw, upstream, gain_row, sum_ref):
        factor = lax.rsqrt(per_head(low, raw * raw) + EPSILON)
        scaled = upstream * gain_row
        inner = per_head(low, scaled * raw)
        sum_ref[...] += jnp.sum(upstream * raw * factor, axis=0, keepdims=True)
        return factor * scaled - raw * (factor * factor * factor) * inner

    forget = zero
    for group in range(cols // LANES):
        at = group * LANES
        here = slice(at, at + LANES)
        pair = (2 * group, 2 * group + 1)
        both = [g_ref[h, :, :LANES].astype(F32) if h < heads else zero for h in pair]
        rest = [g_ref[h, :, LANES:].astype(F32) if h < heads else zero for h in pair]
        query = head_back(raw_ref[:, here], merge_pair(low, *both), gq_ref[...], dgq_ref)
        key = head_back(
            raw_ref[:, cols + at : cols + at + LANES],
            merge_swapped(low, *both),
            gk_ref[...],
            dgk_ref,
        )
        grads_ref[:, here] = query.astype(BF16)
        grads_ref[:, cols + at : cols + at + LANES] = key.astype(BF16)
        value = merge_pair(low, *rest)
        grads_ref[:, 2 * cols + at : 2 * cols + at + LANES] = value.astype(BF16)
        for h, block in zip(pair, rest):
            if h < heads:
                forget = jnp.where(lane == h, block[:, 64:65], forget)
    grads_ref[:, 3 * cols : 4 * cols] = dgl_ref[...]
    grads_ref[:, 4 * cols :] = forget.astype(BF16)
    db_ref[...] += jnp.sum(forget, axis=0, keepdims=True)
    da = dot(grads_ref[...], w_ref[...], NT)
    da_ref[...] = da.astype(BF16)
    x = x_ref[...].astype(F32)
    dg_ref[...] += jnp.sum(da * x * rms_factor(x), axis=0, keepdims=True)


def project_back(heads, returned, raw, x, dgl, weights, gq_row, gk_row, micros):
    total, width = x.shape
    rows = total // micros
    cols = dgl.shape[1]
    wide = weights.shape[1]
    whole = lambda m: (0, 0)
    part = lambda m: (m, 0)
    return pl.pallas_call(
        functools.partial(project_back_kernel, heads),
        grid=(micros,),
        in_specs=[
            pl.BlockSpec((heads, rows, 2 * LANES), lambda m: (m, 0, 0)),
            pl.BlockSpec((rows, 2 * cols), part),
            pl.BlockSpec((rows, width), part),
            pl.BlockSpec((rows, cols), part),
            pl.BlockSpec((width, wide), whole),
            pl.BlockSpec((1, LANES), whole),
            pl.BlockSpec((1, LANES), whole),
        ],
        out_specs=[
            pl.BlockSpec((rows, wide), part),
            pl.BlockSpec((rows, width), part),
            pl.BlockSpec((1, width), whole),
            pl.BlockSpec((1, LANES), whole),
            pl.BlockSpec((1, LANES), whole),
            pl.BlockSpec((1, LANES), whole),
        ],
        out_shape=[
            jax.ShapeDtypeStruct((total, wide), BF16),
            jax.ShapeDtypeStruct((total, width), BF16),
            jax.ShapeDtypeStruct((1, width), F32),
            jax.ShapeDtypeStruct((1, LANES), F32),
            jax.ShapeDtypeStruct((1, LANES), F32),
            jax.ShapeDtypeStruct((1, LANES), F32),
        ],
        compiler_params=params(),
        cost_estimate=pl.CostEstimate(
            flops=2 * total * width * wide,
            bytes_accessed=2 * width * wide + 12 * total * width,
            transcendentals=0,
        ),
        name="project_back",
    )(returned, raw, x, dgl, weights, gq_row, gk_row)


def input_back_kernel(da_ref, x_ref, dh_ref, gain_ref, out_ref):
    x = x_ref[...].astype(F32)
    out_ref[...] = dh_ref[...] + norm_back(
        x, rms_factor(x), gain_ref[...], da_ref[...].astype(F32)
    )


def input_back(da, x, dh, gain_row, micros):
    total, width = x.shape
    rows = total // micros
    part = lambda m: (m, 0)
    block = pl.BlockSpec((rows, width), part)
    return pl.pallas_call(
        input_back_kernel,
        grid=(micros,),
        in_specs=[block, block, block, pl.BlockSpec((1, width), lambda m: (0, 0))],
        out_specs=block,
        out_shape=jax.ShapeDtypeStruct((total, width), F32),
        compiler_params=params(),
        cost_estimate=pl.CostEstimate(
            flops=10 * total * width, bytes_accessed=12 * total * width, transcendentals=0
        ),
        name="input_back",
    )(da, x, dh, gain_row)


def pad_to(array, size, axis):
    missing = size - array.shape[axis]
    if missing == 0:
        return array
    widths = [(0, missing if i == axis else 0) for i in range(array.ndim)]
    return jnp.pad(array, widths)


def turned_product(left, right):
    return lax.dot_general(
        left, right, (((0,), (0,)), ((), ())), preferred_element_type=F32
    ).astype(BF16)


def shards(
    inputs,
    cotangent,
    tail_keys,
    tail_values,
    tail_forget,
    gain_one,
    gain_two,
    w_query,
    w_key,
    w_value,
    w_forget,
    forget_bias,
    query_gain,
    key_gain,
    w_outgate,
    w_out,
    w_gate,
    w_up,
    w_down,
):
    micros, rows, width = inputs.shape
    total = micros * rows
    own_cols = w_query.shape[1]
    heads = w_forget.shape[1]
    ff = w_gate.shape[1]
    seq_count = lax.axis_size("seq")
    head_count = lax.axis_size("head")
    seq_rank = lax.axis_index("seq")
    head_rank = lax.axis_index("head")
    cols = -(-own_cols // LANES) * LANES
    pair_total = micros * heads
    pairs = -(-pair_total // seq_count)
    padded_pairs = pairs * seq_count
    tail_length = tail_keys.shape[1]

    x = inputs.reshape(total, width)
    dy = cotangent.reshape(total, width)

    small = jnp.concatenate([w_forget, gain_one[:, None], gain_two[:, None]], axis=1)
    first_shard = jnp.concatenate(
        [pad_to(w, cols, 1) for w in (w_query, w_key, w_value, w_outgate)]
        + [pad_to(small, LANES, 1)],
        axis=1,
    )
    first = lax.all_gather(first_shard, "seq", axis=0, tiled=True)
    out_all = lax.all_gather(pad_to(w_out.T, cols, 1), "head", axis=1, tiled=True)
    second_shard = jnp.concatenate([out_all, w_gate, w_up, w_down.T], axis=1)
    second = lax.all_gather(second_shard, "seq", axis=0, tiled=True)
    out_own = lax.dynamic_slice_in_dim(second, head_rank * cols, cols, 1)
    gain_one_row = first[:, 4 * cols + heads].astype(F32)[None, :]
    gain_two_row = first[:, 4 * cols + heads + 1].astype(F32)[None, :]
    bias_here = lax.dynamic_slice_in_dim(forget_bias, head_rank * heads, heads, 0)
    bias_row = pad_to(bias_here[None, :], LANES, 1)
    gq_row = jnp.tile(query_gain.astype(F32), 2)[None, :]
    gk_row = jnp.tile(key_gain.astype(F32), 2)[None, :]

    tail_key_parts, tail_value_parts = [], []
    for j in range(pairs):
        p = jnp.minimum(seq_rank * pairs + j, pair_total - 1)
        m, h = p // heads, p % heads
        tail_of = lambda array, wide: lax.dynamic_slice(
            array, (m, 0, h * wide), (1, tail_length, wide)
        )[0]
        forget = tail_of(tail_forget, 1)
        decay = jnp.cumsum(forget, axis=0) - jnp.sum(forget, axis=0, keepdims=True)
        high = lax.reduce_precision(decay, 8, 7)
        middle = lax.reduce_precision(decay - high, 8, 7)
        least = decay - high - middle
        ones = jnp.ones((tail_length, 3), BF16)
        parts = jnp.concatenate([-high, -middle, -least], axis=1).astype(BF16)
        tail_key_parts.append(
            pad_to(jnp.concatenate([tail_of(tail_keys, HEAD_SIZE), ones, parts], axis=1), LANES, 1)
        )
        tail_value_parts.append(
            pad_to(jnp.concatenate([tail_of(tail_values, HEAD_SIZE), ones], axis=1), LANES, 1)
        )
    tail_key = jnp.stack(tail_key_parts)
    tail_value = jnp.stack(tail_value_parts)

    def to_owners(array):
        array = pad_to(array, padded_pairs, 0)
        array = array.reshape((seq_count, pairs) + array.shape[1:])
        return lax.all_to_all(array, "seq", 0, 0, tiled=True)

    def from_owners(array):
        array = lax.all_to_all(array, "seq", 0, 0, tiled=True)
        return array.reshape((padded_pairs,) + array.shape[2:])[:pair_total]

    a, raw, gl, pay = project(
        heads, cols, x, first, bias_row, gain_one_row, gq_row, gk_row, micros
    )
    pay = to_owners(pay)
    packed, mixture, *saved = attend(pay, tail_key, tail_value)
    packed = from_owners(packed)
    o = gate(heads, packed, gl, micros)
    o_all = lax.all_gather(o, "head", axis=0)
    hidden, c, u, dgr, dur, out_part, dc_part, dgain_two = feed(
        x, dy, o_all, second, gain_two_row, ff, micros
    )
    dc = lax.psum(dc_part, "head")
    out_sum = lax.psum(out_part, "head")
    layer_out = (hidden + out_sum.astype(F32)).astype(BF16)
    dh, dhb, dgl, dap = hidden_back(heads, dc, hidden, dy, gain_two_row, out_own, gl, packed, micros)
    dap = to_owners(dap)
    returned = attend_back(saved, tail_key, tail_value, mixture, dap, pay)
    returned = from_owners(returned)
    grads, da_part, dgain_one, dgq, dgk, dbias = project_back(
        heads, returned, raw, x, dgl, first, gq_row, gk_row, micros
    )
    da = lax.psum(da_part, "head")
    input_grad = input_back(da, x, dh, gain_one_row, micros)

    def scattered(grad):
        return lax.psum_scatter(grad, "seq", scatter_dimension=0, tiled=True).astype(F32)

    grad_gate = scattered(turned_product(c, dgr))
    grad_up = scattered(turned_product(c, dur))
    grad_down = scattered(turned_product(dy, u)).T
    grad_out = scattered(turned_product(dhb, o))[:, :own_cols].T
    grad_first = scattered(turned_product(a, grads))

    bias_full = lax.dynamic_update_slice_in_dim(
        jnp.zeros(forget_bias.shape, F32), dbias[0, :heads], head_rank * heads, 0
    )
    fold = lambda row: row[0, :HEAD_SIZE] + row[0, HEAD_SIZE:]
    gains, bias_total, gq_total, gk_total = lax.psum(
        (jnp.concatenate([dgain_one, dgain_two], axis=0), bias_full, fold(dgq), fold(dgk)),
        ("seq", "head"),
    )
    own_rows = gain_one.shape[0]
    gains = lax.dynamic_slice_in_dim(gains, seq_rank * own_rows, own_rows, 1)
    shape = inputs.shape
    return (
        layer_out.reshape(shape),
        input_grad.reshape(shape),
        gains[0],
        gains[1],
        grad_first[:, :own_cols],
        grad_first[:, cols : cols + own_cols],
        grad_first[:, 2 * cols : 2 * cols + own_cols],
        grad_first[:, 4 * cols : 4 * cols + heads],
        bias_total,
        gq_total,
        gk_total,
        grad_first[:, 3 * cols : 3 * cols + own_cols],
        grad_out,
        grad_gate,
        grad_up,
        grad_down,
    )


def solution(mesh):
    by_rows = P("seq", "head")
    by_cols = P("head", "seq")
    placed = (
        P(None, "seq", None),
        P(None, "seq", None),
        P(None, None, "head"),
        P(None, None, "head"),
        P(None, None, "head"),
        P("seq"),
        P("seq"),
        by_rows,
        by_rows,
        by_rows,
        by_rows,
        P(),
        P(),
        P(),
        by_rows,
        by_cols,
        by_rows,
        by_rows,
        by_cols,
    )
    return jax.shard_map(
        shards,
        mesh=mesh,
        in_specs=placed,
        out_specs=(
            P(None, "seq", None),
            P(None, "seq", None),
            P("seq"),
            P("seq"),
            by_rows,
            by_rows,
            by_rows,
            by_rows,
            P(),
            P(),
            P(),
            by_rows,
            by_cols,
            by_rows,
            by_rows,
            by_cols,
        ),
        check_vma=False,
    )
```

```python
import functools

import jax
import jax.numpy as jnp
from jax import lax
from jax.experimental import pallas as pl
from jax.experimental.pallas import tpu as pltpu
from jax.sharding import PartitionSpec as P

HEAD_SIZE = 64
LANES = 128
EPSILON = 1e-06
F32 = jnp.float32
BF16 = jnp.bfloat16
NN = (((1,), (0,)), ((), ()))
NT = (((1,), (1,)), ((), ()))
HIDE = -1e30
SCALE = HEAD_SIZE**-0.5
STRIP = 64
MIB = 1024 * 1024


def dot(left, right, dims=NN):
    return lax.dot_general(left, right, dims, preferred_element_type=F32)


def params():
    return pltpu.CompilerParams(vmem_limit_bytes=60 * MIB)


def linked(kernel, inputs, extra, outputs):
    def body(*refs):
        token = refs[inputs + extra + outputs]
        token[...] = jnp.zeros_like(token)
        kernel(
            *refs[:inputs],
            *refs[inputs + extra : inputs + extra + outputs],
            *refs[inputs + extra + outputs + 1 :],
        )

    return body


class Order:
    def __init__(self):
        self.tokens = []

    def call(self, kernel, name, grid, ins, outs, us, scratch=(), before=(), scalars=(), after=()):
        arrays = list(scalars) + [array for array, _ in ins]
        extra = list(before) + list(after) + self.tokens
        count = len(arrays)
        whole = lambda *at: (0, 0)
        out_specs = [spec for _, _, spec in outs] + [pl.BlockSpec((8, LANES), whole)]
        out_shape = [jax.ShapeDtypeStruct(shape, kind) for shape, kind, _ in outs]
        out_shape.append(jax.ShapeDtypeStruct((8, LANES), F32))
        *results, token = pl.pallas_call(
            linked(kernel, count, len(extra), len(outs)),
            grid_spec=pltpu.PrefetchScalarGridSpec(
                num_scalar_prefetch=len(scalars),
                grid=grid,
                in_specs=[spec for _, spec in ins] + [pl.BlockSpec(memory_space=pl.ANY)] * len(extra),
                out_specs=out_specs,
                scratch_shapes=list(scratch),
            ),
            out_shape=out_shape,
            input_output_aliases={count + i: i for i in range(len(before))},
            compiler_params=params(),
            cost_estimate=pl.CostEstimate(flops=int(us * 0.45e9), bytes_accessed=0, transcendentals=0),
            name=name,
        )(*arrays, *extra)
        self.tokens = [token]
        return results


def lanes_of(rows):
    return lax.broadcasted_iota(jnp.int32, (rows, LANES), 1)


def swap_halves(block):
    return pltpu.roll(block, HEAD_SIZE, 1)


def in_three(value):
    high = value.astype(BF16).astype(F32)
    rest = value - high
    middle = rest.astype(BF16).astype(F32)
    return high, middle, rest - middle


def at_lanes(lane, first, parts, base):
    for place, part in enumerate(parts):
        base = jnp.where(lane == first + place, part, base)
    return base


def triangle(rows, lower):
    down = lax.broadcasted_iota(jnp.int32, (rows, rows), 0)
    across = lax.broadcasted_iota(jnp.int32, (rows, rows), 1)
    return jnp.where(down >= across if lower else down <= across, 1.0, 0.0).astype(BF16)


def running_sum(tri, column, lane):
    spread = at_lanes(lane, 0, in_three(column), jnp.zeros(lane.shape, F32))
    sums = dot(tri, spread.astype(BF16))
    return sums[:, 0:1] + sums[:, 1:2] + sums[:, 2:3]


def forget_column(tail_block):
    return tail_block[:, 64:65] + tail_block[:, 65:66] + tail_block[:, 66:67]


def per_head(low, values):
    first = jnp.sum(jnp.where(low, values, 0.0), axis=-1, keepdims=True)
    second = jnp.sum(jnp.where(low, 0.0, values), axis=-1, keepdims=True)
    return jnp.where(low, first, second) * (1.0 / HEAD_SIZE)


def rms_factor(values):
    return lax.rsqrt(jnp.mean(values * values, axis=-1, keepdims=True) + EPSILON)


def merge_pair(low, first, second):
    return jnp.where(low, first, swap_halves(second))


def merge_swapped(low, first, second):
    return jnp.where(low, swap_halves(first), second)


def unpack_rows(low_half, first, second):
    strip = low_half.shape[0]
    rows = []
    for at in range(0, first.shape[0], strip):
        one, two = first[at : at + strip], second[at : at + strip]
        rows.append(jnp.where(low_half, one, swap_halves(two)))
        rows.append(jnp.where(low_half, swap_halves(one), two))
    return jnp.concatenate(rows, axis=0)


def pack_rows(low_half, block):
    strip = low_half.shape[0]
    first, second = [], []
    for at in range(0, block.shape[0], 2 * strip):
        top, bottom = block[at : at + strip], block[at + strip : at + 2 * strip]
        first.append(jnp.where(low_half, top, swap_halves(bottom)))
        second.append(jnp.where(low_half, swap_halves(top), bottom))
    return jnp.concatenate(first, axis=0), jnp.concatenate(second, axis=0)


def project_kernel(
    heads, idle, x_ref, w_ref, bias_ref, gain_ref, gq_ref, gk_ref, a_ref, raw_ref, gl_ref, pay_ref
):
    x = x_ref[...].astype(F32)
    rows = x.shape[0]
    cols = gl_ref.shape[1]
    a = (x * rms_factor(x) * gain_ref[...]).astype(BF16)
    a_ref[...] = a
    proj = dot(a, w_ref[...])
    raw_ref[...] = proj[:, : 2 * cols]
    gl_ref[...] = proj[:, 3 * cols : 4 * cols]
    logit = proj[:, 4 * cols :] + bias_ref[...]
    lane = lanes_of(rows)
    low = lane < HEAD_SIZE
    for group in range(cols // LANES):
        at = group * LANES
        query = proj[:, at : at + LANES]
        key = proj[:, cols + at : cols + at + LANES]
        value = proj[:, 2 * cols + at : 2 * cols + at + LANES]
        query = query * lax.rsqrt(per_head(low, query * query) + EPSILON) * gq_ref[...]
        key = key * lax.rsqrt(per_head(low, key * key) + EPSILON) * gk_ref[...]
        for half in range(2):
            head = 2 * group + half
            if head >= heads:
                continue
            zl = at_lanes(lane, 64, in_three(logit[:, head : head + 1]), jnp.zeros(lane.shape, F32))
            if half == 0:
                both = merge_pair(low, query, key)
                rest = jnp.where(low, value, zl)
            else:
                both = merge_swapped(low, query, key)
                rest = jnp.where(low, swap_halves(value), zl)
            pair = pl.program_id(0) * heads + head
            owner, place = lax.rem(pair, pay_ref.shape[0]), lax.div(pair, pay_ref.shape[0])
            pay_ref[owner, place, :, :LANES] = both.astype(BF16)
            pay_ref[owner, place, :, LANES:] = rest.astype(BF16)

    @pl.when(pl.program_id(0) == 0)
    def _():
        for pair in idle:
            owner, place = pair % pay_ref.shape[0], pair // pay_ref.shape[0]
            pay_ref[owner, place] = jnp.zeros(pay_ref.shape[2:], BF16)


def project(order, heads, cols, owners, x, weights, bias_row, gain_row, gq_row, gk_row, micros, after):
    total, width = x.shape
    rows = total // micros
    wide = weights.shape[1]
    whole = lambda m: (0, 0)
    part = lambda m: (m, 0)
    row = pl.BlockSpec((1, LANES), whole)
    pairs = -(-micros * heads // owners)
    idle = range(micros * heads, pairs * owners)
    sent = (owners, pairs, rows, 2 * LANES)
    return order.call(
        functools.partial(project_kernel, heads, idle),
        "project",
        (micros,),
        [
            (x, pl.BlockSpec((rows, width), part)),
            (weights, pl.BlockSpec((width, wide), whole)),
            (bias_row, row),
            (gain_row, pl.BlockSpec((1, width), whole)),
            (gq_row, row),
            (gk_row, row),
        ],
        [
            ((total, width), BF16, pl.BlockSpec((rows, width), part)),
            ((total, 2 * cols), F32, pl.BlockSpec((rows, 2 * cols), part)),
            ((total, cols), F32, pl.BlockSpec((rows, cols), part)),
            (sent, BF16, pl.BlockSpec(sent, lambda m: (0, 0, 0, 0))),
        ],
        13,
        after=after,
    )


def attend_kernel(size, pay_ref, tk_ref, tv_ref, ap_ref, af_ref, q_ref, k_ref, v_ref):
    blocks, _, rows, _ = pay_ref.shape
    length = blocks * rows
    lane = lanes_of(rows)
    low = lane < HEAD_SIZE
    tri = triangle(rows, True)
    zero = jnp.zeros(lane.shape, F32)

    def build(b, carry):
        at = pl.ds(pl.multiple_of(b * rows, rows), rows)
        both = pay_ref[b, 0, :, :LANES].astype(F32)
        rest = pay_ref[b, 0, :, LANES:].astype(F32)
        logit = forget_column(rest)
        log_forget = jnp.minimum(logit, 0.0) - jnp.log1p(jnp.exp(-jnp.abs(logit)))
        decay = running_sum(tri, log_forget, lane) + carry
        high, middle, least = in_three(decay)
        query_side = at_lanes(lane, 64, (high, middle, least, 1.0, 1.0, 1.0), zero)
        key_side = at_lanes(lane, 64, (1.0, 1.0, 1.0, -high, -middle, -least), zero)
        value_side = at_lanes(lane, 64, (1.0, 1.0, 1.0), zero)
        q_ref[0, at, :] = jnp.where(low, both * SCALE, query_side).astype(BF16)
        k_ref[0, at, :] = jnp.where(low, swap_halves(both), key_side).astype(BF16)
        v_ref[0, at, :] = jnp.where(low, rest, value_side).astype(BF16)
        return decay[rows - 1 :, :]

    lax.fori_loop(0, blocks, build, jnp.zeros((1, 1), F32))

    tail_length = tk_ref.shape[1]
    visible = lax.broadcasted_iota(jnp.int32, (size, size), 0) >= lax.broadcasted_iota(
        jnp.int32, (size, size), 1
    )
    half_low = lanes_of(STRIP) < HEAD_SIZE
    lane_here = lanes_of(size)

    def one_block(qi, carry):
        at = pl.ds(pl.multiple_of(qi * size, size), size)
        query = q_ref[0, at, :]

        def absorb(key, value, total, masked=False):
            scores = dot(query, key, NT)
            if masked:
                scores = jnp.where(visible, scores, HIDE)
            return total + dot(jnp.exp(scores).astype(BF16), value)

        total = jnp.zeros((size, LANES), F32)
        for t in range(tail_length // size):
            here = pl.ds(t * size, size)
            total = absorb(tk_ref[0, here, :], tv_ref[0, here, :], total)

        def earlier(ki, total):
            here = pl.ds(pl.multiple_of(ki * size, size), size)
            return absorb(k_ref[0, here, :], v_ref[0, here, :], total)

        total = lax.fori_loop(0, qi, earlier, total)
        total = absorb(k_ref[0, at, :], v_ref[0, at, :], total, True)
        weight = total[:, 64:65]
        mixture = total / weight
        af_ref[0, at, :] = mixture
        for piece in range(size // rows):
            block = mixture[piece * rows : (piece + 1) * rows]
            packed, _ = pack_rows(half_low, block)
            ap_ref[qi * (size // rows) + piece, 0] = packed.astype(BF16)
        old = query.astype(F32)
        shifted = forget_column(old) - jnp.log(weight)
        q_ref[0, at, :] = at_lanes(lane_here, 64, in_three(shifted), old).astype(BF16)
        return carry

    lax.fori_loop(0, length // size, one_block, 0)


def attend(order, pay, tail_key, tail_value):
    blocks, pairs, rows, _ = pay.shape
    length = blocks * rows
    tail_length = tail_key.shape[1]
    size = min(512, length)
    pair = lambda j: (j, 0, 0)
    across = lambda j: (0, j, 0, 0)
    tail = pl.BlockSpec((1, tail_length, LANES), pair)
    whole = pl.BlockSpec((1, length, LANES), pair)
    return order.call(
        functools.partial(attend_kernel, size),
        "attend",
        (pairs,),
        [
            (pay, pl.BlockSpec((blocks, 1, rows, 2 * LANES), across)),
            (tail_key, tail),
            (tail_value, tail),
        ],
        [
            (
                (blocks, pairs, rows // 2, LANES),
                BF16,
                pl.BlockSpec((blocks, 1, rows // 2, LANES), across),
            ),
            ((pairs, length, LANES), F32, whole),
            ((pairs, length, LANES), BF16, whole),
            ((pairs, length, LANES), BF16, whole),
            ((pairs, length, LANES), BF16, whole),
        ],
        17 * pairs,
    )


def attend_back_kernel(
    size,
    q_ref,
    k_ref,
    v_ref,
    tk_ref,
    tv_ref,
    af_ref,
    dap_ref,
    rest_ref,
    g_ref,
    da_ref,
    dqt_ref,
    sums_ref,
):
    blocks, _, rows, _ = rest_ref.shape
    length = blocks * rows
    lane = lanes_of(rows)
    low = lane < HEAD_SIZE
    zero = jnp.zeros(lane.shape, F32)

    def build(b, carry):
        at = pl.ds(pl.multiple_of(b * rows, rows), rows)
        packed = dap_ref[b, 0].astype(F32)
        strips = []
        for strip in range(0, packed.shape[0], STRIP):
            strips += [packed[strip : strip + STRIP], swap_halves(packed[strip : strip + STRIP])]
        grad = jnp.where(low, jnp.concatenate(strips, axis=0), 0.0)
        delta = jnp.sum(grad * af_ref[0, at, :], axis=-1, keepdims=True)
        da_ref[at, :] = at_lanes(lane, 64, in_three(-delta), grad).astype(BF16)
        return carry

    lax.fori_loop(0, blocks, build, 0)

    across = lax.broadcasted_iota(jnp.int32, (size, size), 1)
    down = lax.broadcasted_iota(jnp.int32, (size, size), 0)
    visible = across >= down
    count = length // size

    def block_at(i):
        return pl.ds(pl.multiple_of(i * size, size), size)

    def pieces(key, value, at, masked=False):
        scores = dot(key, q_ref[0, at, :], NT)
        if masked:
            scores = jnp.where(visible, scores, HIDE)
        prob = jnp.exp(scores)
        score_grad = prob * dot(value, da_ref[at, :], NT)
        return prob.astype(BF16), score_grad.astype(BF16)

    tail_length = tk_ref.shape[1]
    tail_count = tail_length // size

    def tail_block(qi, carry):
        at = block_at(qi)
        total = jnp.zeros((LANES, size), F32)
        for t in range(tail_count):
            key = tk_ref[0, pl.ds(t * size, size), :]
            _, score_grad = pieces(key, tv_ref[0, pl.ds(t * size, size), :], at)
            total = total + dot(key.T, score_grad)
        dqt_ref[:, at] = total
        return carry

    lax.fori_loop(0, count, tail_block, 0)
    lane_here = lanes_of(size)
    low_here = lane_here < HEAD_SIZE

    def key_block(ki, carry):
        own = block_at(ki)
        key = k_ref[0, own, :]
        value = v_ref[0, own, :]
        key_turned = key.T

        def one(at, sums, masked=False):
            key_sum, value_sum = sums
            prob, score_grad = pieces(key, value, at, masked)
            dqt_ref[:, at] += dot(key_turned, score_grad)
            return (
                key_sum + dot(score_grad, q_ref[0, at, :]),
                value_sum + dot(prob, da_ref[at, :]),
            )

        start = (jnp.zeros((size, LANES), F32), jnp.zeros((size, LANES), F32))
        sums = one(own, start, True)
        key_sum, value_sum = lax.fori_loop(
            ki + 1, count, lambda qi, sums: one(block_at(qi), sums), sums
        )
        sums_ref[own, :] = key_sum
        for piece in range(size // rows):
            here = slice(piece * rows, (piece + 1) * rows)
            g_ref[ki * (size // rows) + piece, 0, :, LANES:] = value_sum[here].astype(BF16)
        return carry

    lax.fori_loop(0, count, key_block, 0)

    tri = triangle(rows, False)

    def finish(i, carry):
        b = blocks - 1 - i
        at = pl.ds(pl.multiple_of(b * rows, rows), rows)
        query = dqt_ref[:, at].T
        key = sums_ref[at, :]
        decay_grad = query[:, 64:65] - key[:, 67:68]
        suffix = running_sum(tri, decay_grad, lane) + carry
        logit = forget_column(rest_ref[b, 0].astype(F32))
        forget_grad = suffix / (1.0 + jnp.exp(logit))
        both = jnp.where(low, query * SCALE, swap_halves(key))
        rest = jnp.where(low, g_ref[b, 0, :, LANES:].astype(F32), jnp.where(lane == 64, forget_grad, 0.0))
        g_ref[b, 0, :, :LANES] = both.astype(BF16)
        g_ref[b, 0, :, LANES:] = rest.astype(BF16)
        return suffix[0:1, :]

    lax.fori_loop(0, blocks, finish, jnp.zeros((1, 1), F32))


def attend_back(order, saved, tail_key, tail_value, mixture, packed_grad, pay, place, grad_place):
    blocks, _, rows, _ = pay.shape
    length = blocks * rows
    tail_length = tail_key.shape[1]
    size = min(512, length)
    pair = lambda j: (place, 0, 0)
    tail = pl.BlockSpec((1, tail_length, LANES), pair)
    whole = pl.BlockSpec((1, length, LANES), pair)
    grad = pl.BlockSpec((blocks, 1, rows // 2, LANES), lambda j: (0, grad_place, 0, 0))
    sent = (blocks, 1, rows, 2 * LANES)
    return order.call(
        functools.partial(attend_back_kernel, size),
        "attend_back",
        (1,),
        [(array, whole) for array in saved]
        + [
            (tail_key, tail),
            (tail_value, tail),
            (mixture, whole),
            (packed_grad, grad),
            (pay, pl.BlockSpec((blocks, 1, rows, LANES), lambda j: (0, place, 0, 1))),
        ],
        [(sent, BF16, pl.BlockSpec(sent, lambda j: (0, 0, 0, 0)))],
        22,
        scratch=[
            pltpu.VMEM((length, LANES), BF16),
            pltpu.VMEM((LANES, length), F32),
            pltpu.VMEM((length, LANES), F32),
        ],
    )[0]


def group_of(heads, ref, first_pair, group, low_half):
    owners = ref.shape[0]

    def packed(head):
        if head >= heads:
            return jnp.zeros(ref.shape[2:], F32)
        pair = first_pair + head
        if isinstance(pair, int):
            return ref[pair % owners, pair // owners].astype(F32)
        return ref[lax.rem(pair, owners), lax.div(pair, owners)].astype(F32)

    return unpack_rows(low_half, packed(2 * group), packed(2 * group + 1))


def gate_kernel(heads, first, ap_ref, gl_ref, o_ref, sent_ref):
    rows, cols = o_ref.shape
    half_low = lanes_of(STRIP) < HEAD_SIZE
    pair = (first + pl.program_id(0)) * heads
    for group in range(cols // LANES):
        at = slice(group * LANES, (group + 1) * LANES)
        mixture = group_of(heads, ap_ref, pair, group, half_low)
        gated = (mixture * jax.nn.sigmoid(gl_ref[:, at])).astype(BF16)
        o_ref[:, at] = gated
        for z in range(sent_ref.shape[0]):
            sent_ref[z, :, at] = gated


def gate(order, heads, packed, gl, rows, first, count, copies, before):
    total, cols = gl.shape
    here = pl.BlockSpec((rows, cols), lambda i: (first + i, 0))
    return order.call(
        functools.partial(gate_kernel, heads, first),
        "gate",
        (count,),
        [(packed, pl.BlockSpec(packed.shape, lambda i: (0, 0, 0, 0))), (gl, here)],
        [
            ((total, cols), BF16, here),
            (
                (copies, count * rows, cols),
                BF16,
                pl.BlockSpec((copies, rows, cols), lambda i: (0, i, 0)),
            ),
        ],
        2 * count,
        before=before,
    )


def pack_kernel(*refs):
    out_ref, at = refs[-1], 0
    for ref in refs[:-1]:
        wide = ref.shape[1]
        out_ref[:, at : at + wide] = ref[...]
        at += wide


def pack(order, arrays):
    rows = arrays[0].shape[0]
    wide = sum(array.shape[1] for array in arrays)
    whole = lambda i: (0, 0)
    return order.call(
        pack_kernel,
        "pack",
        (1,),
        [(array, pl.BlockSpec(array.shape, whole)) for array in arrays],
        [((rows, wide), BF16, pl.BlockSpec((rows, wide), whole))],
        2,
    )[0]


def feed_kernel(
    parts,
    own,
    rank_ref,
    x_ref,
    dy_ref,
    wo_ref,
    wg_ref,
    wu_ref,
    wd_ref,
    wg_far_ref,
    wu_far_ref,
    wd_far_ref,
    gain_ref,
    *refs,
):
    o_ref, c_ref, u_ref, dgu_ref, hid_ref, out_ref, dc_ref, out_acc, dc_acc = refs
    step = pl.program_id(0)
    last = pl.num_programs(0) - 1

    def attended():
        return dot(o_ref[0], wo_ref[...], NT)

    @pl.when(step == 0)
    def _():
        hid_ref[...] = x_ref[...].astype(F32) + attended()

    @pl.when((step > 0) & (step < parts))
    def _():
        hid_ref[...] += attended()

    @pl.when(step == parts - 1)
    def _():
        hidden = hid_ref[...]
        c_ref[...] = (hidden * rms_factor(hidden) * gain_ref[...]).astype(BF16)
        out_acc[...] = jnp.zeros_like(out_acc)
        dc_acc[...] = jnp.zeros_like(dc_acc)

    def chunk(w_gate, w_up, w_down):
        c = c_ref[...]
        gr = dot(c, w_gate[...])
        ur = dot(c, w_up[...])
        sig = jax.nn.sigmoid(gr)
        silu = gr * sig
        u = (silu * ur).astype(BF16)
        du = dot(dy_ref[...], w_down[...])
        dgr = (du * ur * sig * (1.0 + gr * (1.0 - sig))).astype(BF16)
        dur = (du * silu).astype(BF16)
        out_acc[...] += dot(u, w_down[...], NT)
        dc_acc[...] += dot(dgr, w_gate[...], NT) + dot(dur, w_up[...], NT)
        return u, dgr, dur

    @pl.when((step >= parts) & (step < parts + own))
    def _():
        u, dgr, dur = chunk(wg_ref, wu_ref, wd_ref)
        wide = u.shape[1]
        u_ref[...] = u
        dgu_ref[:, :wide] = dgr
        dgu_ref[:, wide:] = dur

    @pl.when(step >= parts + own)
    def _():
        chunk(wg_far_ref, wu_far_ref, wd_far_ref)

    @pl.when(step == last)
    def _():
        out_ref[...] = out_acc[...].astype(BF16)
        dc_ref[...] = dc_acc[...].astype(BF16)


def feed(order, rank, x, dy, o_all, near, far, gain_row, ff, chunk, group, before):
    parts, rows, cols = o_all.shape
    total, width = x.shape
    own = ff // chunk
    offset = parts * cols // chunk
    others = (far.shape[1] - parts * cols) // (3 * ff)
    steps = parts + (1 + others) * own
    whole = lambda i, rank: (0, 0)
    here = lambda i, rank: (group, 0)
    early = lambda i: jnp.minimum(i, parts - 1)
    mine = lambda i: jnp.clip(i - parts, 0, own - 1)

    def near_strip(k):
        return pl.BlockSpec((width, chunk), lambda i, rank: (0, k * own + mine(i)))

    def far_strip(k):
        def place(i, rank):
            s = jnp.maximum(i - parts - own, 0)
            return (0, offset + (s // own * 3 + k) * own + s % own)

        return pl.BlockSpec((width, chunk), place)

    wide = pl.BlockSpec((rows, width), whole)
    return order.call(
        functools.partial(feed_kernel, parts, own),
        "feed",
        (steps,),
        [
            (x, pl.BlockSpec((rows, width), here)),
            (dy, pl.BlockSpec((rows, width), here)),
            (far, pl.BlockSpec((width, cols), lambda i, rank: (0, early(i)))),
            (near, near_strip(0)),
            (near, near_strip(1)),
            (near, near_strip(2)),
            (far, far_strip(0)),
            (far, far_strip(1)),
            (far, far_strip(2)),
            (gain_row, pl.BlockSpec((1, width), whole)),
        ]
        + [(o_all, pl.BlockSpec((1, rows, cols), lambda i, rank: (rank[0] ^ early(i), 0, 0)))],
        [
            ((total, width), BF16, pl.BlockSpec((rows, width), here)),
            ((total, ff), BF16, pl.BlockSpec((rows, chunk), lambda i, rank: (group, mine(i)))),
            (
                (total, 2 * ff),
                BF16,
                pl.BlockSpec((rows, 2 * chunk), lambda i, rank: (group, mine(i))),
            ),
            ((rows, width), F32, wide),
            ((rows, width), BF16, wide),
            ((rows, width), BF16, wide),
        ],
        37,
        scratch=[pltpu.VMEM((rows, width), F32), pltpu.VMEM((rows, width), F32)],
        before=before,
        scalars=(rank,),
    )


def norm_back(source, factor, gain_row, upstream):
    scaled = upstream * gain_row
    inner = jnp.mean(scaled * source, axis=-1, keepdims=True)
    return factor * scaled - source * (factor * factor * factor) * inner


def hidden_back_kernel(
    heads,
    pair,
    dc_ref,
    dc_other_ref,
    hid_ref,
    dy_ref,
    gain_ref,
    w_ref,
    gl_ref,
    ap_ref,
    dhb_ref,
    dgl_ref,
    dh_ref,
    dap_ref,
    dg_ref,
):
    rows, cols = gl_ref.shape
    hidden = hid_ref[...]
    factor = rms_factor(hidden)
    dc = dc_ref[...].astype(F32) + dc_other_ref[...].astype(F32)
    dh = dy_ref[...].astype(F32) + norm_back(hidden, factor, gain_ref[...], dc)
    dg_ref[0] = jnp.sum(dc * hidden * factor, axis=0, keepdims=True)
    dh_ref[...] = dh
    dhb = dh.astype(BF16)
    dhb_ref[...] = dhb
    gated_grad = dot(dhb, w_ref[...])
    half_low = lanes_of(STRIP) < HEAD_SIZE
    for group in range(cols // LANES):
        at = slice(group * LANES, (group + 1) * LANES)
        mixture = group_of(heads, ap_ref, pair, group, half_low)
        gate_value = jax.nn.sigmoid(gl_ref[:, at])
        grad = gated_grad[:, at]
        dgl_ref[:, at] = (grad * mixture * gate_value * (1.0 - gate_value)).astype(BF16)
        first, second = pack_rows(half_low, grad * gate_value)
        dap_ref[2 * group] = first.astype(BF16)
        if 2 * group + 1 < heads:
            dap_ref[2 * group + 1] = second.astype(BF16)


def hidden_back(order, heads, dc, dc_other, hidden, dy, gain_row, weights, gl, packed, rows, micro, place, before):
    total, cols = gl.shape
    width = dc.shape[1]
    half = rows // 2
    whole = lambda i: (0, 0)
    here = lambda i: (2 * micro + i, 0)
    part = pl.BlockSpec((half, width), lambda i: (2 * place + i, 0))
    strips = pl.BlockSpec((heads, half // 2, LANES), lambda i: (0, i, 0))
    return order.call(
        functools.partial(hidden_back_kernel, heads, micro * heads),
        "hidden_back",
        (2,),
        [
            (dc, part),
            (dc_other, part),
            (hidden, part),
            (dy, pl.BlockSpec((half, width), here)),
            (gain_row, pl.BlockSpec((1, width), whole)),
            (weights, pl.BlockSpec((width, cols), whole)),
            (gl, pl.BlockSpec((half, cols), here)),
            (packed, pl.BlockSpec(packed.shape[:2] + (half // 2, LANES), lambda i: (0, 0, i, 0))),
        ],
        [
            ((total, width), BF16, pl.BlockSpec((half, width), here)),
            ((total, cols), BF16, pl.BlockSpec((half, cols), here)),
            ((rows, width), F32, pl.BlockSpec((half, width), lambda i: (i, 0))),
            ((heads, half, LANES), BF16, strips),
            ((2, 1, width), F32, pl.BlockSpec((1, 1, width), lambda i: (i, 0, 0))),
        ],
        4,
        before=before,
    )


def project_back_kernel(
    heads,
    upper_ref,
    g_ref,
    raw_ref,
    x_ref,
    dgl_ref,
    w_ref,
    gq_ref,
    gk_ref,
    grads_ref,
    *refs,
):
    *da_refs, sums_ref, all_ref = refs
    rows, cols = dgl_ref.shape
    width = x_ref.shape[1]
    lane = lanes_of(rows)
    low = lane < HEAD_SIZE
    zero = jnp.zeros(lane.shape, F32)
    sums = [jnp.zeros((1, LANES), F32), jnp.zeros((1, LANES), F32)]

    def head_back(raw, upstream, gain_row, which):
        factor = lax.rsqrt(per_head(low, raw * raw) + EPSILON)
        scaled = upstream * gain_row
        inner = per_head(low, scaled * raw)
        sums[which] += jnp.sum(upstream * raw * factor, axis=0, keepdims=True)
        return factor * scaled - raw * (factor * factor * factor) * inner

    forget = zero
    for group in range(cols // LANES):
        at = group * LANES
        here = slice(at, at + LANES)
        pair = (2 * group, 2 * group + 1)
        both = [g_ref[h, :, :LANES].astype(F32) if h < heads else zero for h in pair]
        rest = [g_ref[h, :, LANES:].astype(F32) if h < heads else zero for h in pair]
        query = head_back(raw_ref[:, here], merge_pair(low, *both), gq_ref[...], 0)
        key = head_back(
            raw_ref[:, cols + at : cols + at + LANES],
            merge_swapped(low, *both),
            gk_ref[...],
            1,
        )
        all_ref[:, here] = query.astype(BF16)
        all_ref[:, cols + at : cols + at + LANES] = key.astype(BF16)
        value = merge_pair(low, *rest)
        all_ref[:, 2 * cols + at : 2 * cols + at + LANES] = value.astype(BF16)
        for h, block in zip(pair, rest):
            if h < heads:
                forget = jnp.where(lane == h, block[:, 64:65], forget)
    all_ref[:, 3 * cols : 4 * cols] = dgl_ref[...]
    all_ref[:, 4 * cols :] = forget.astype(BF16)
    grads_ref[:, : 3 * cols] = all_ref[:, : 3 * cols]
    grads_ref[:, 3 * cols :] = all_ref[:, 4 * cols :]
    da = dot(all_ref[...], w_ref[...], NT)
    if len(da_refs) == 1:
        da_refs[0][...] = da.astype(BF16)
    else:
        is_kept = pl.program_id(0) == upper_ref[0]
        for ref, chosen in zip(da_refs, (is_kept, jnp.logical_not(is_kept))):

            @pl.when(chosen)
            def _(ref=ref):
                ref[...] = da.astype(BF16)

    x = x_ref[...].astype(F32)
    sums_ref[0, :, :width] = jnp.sum(da * x * rms_factor(x), axis=0, keepdims=True)
    sums_ref[0, :, width : width + LANES] = sums[0]
    sums_ref[0, :, width + LANES : width + 2 * LANES] = sums[1]
    sums_ref[0, :, width + 2 * LANES :] = jnp.sum(forget, axis=0, keepdims=True)


def project_back(order, heads, upper, returned, raw, x, dgl, weights, gq_row, gk_row, rows, micro, halves, before, after):
    total, cols = dgl.shape
    width, wide = weights.shape
    half = rows // 2
    whole = lambda i, upper: (0, 0)
    here = lambda i, upper: (2 * micro + i, 0)
    row = pl.BlockSpec((1, LANES), whole)
    sums = width + 3 * LANES
    if halves:
        da = [((half, width), BF16, pl.BlockSpec((half, width), whole))] * 2
    else:
        da = [((rows, width), BF16, pl.BlockSpec((half, width), lambda i, upper: (i, 0)))]
    return order.call(
        functools.partial(project_back_kernel, heads),
        "project_back",
        (2,),
        [
            (returned, pl.BlockSpec((heads, half, 2 * LANES), lambda i, upper: (0, i, 0))),
            (raw, pl.BlockSpec((half, 2 * cols), here)),
            (x, pl.BlockSpec((half, width), here)),
            (dgl, pl.BlockSpec((half, cols), here)),
            (weights, pl.BlockSpec((width, wide), whole)),
            (gq_row, row),
            (gk_row, row),
        ],
        [((total, wide - cols), BF16, pl.BlockSpec((half, wide - cols), here))]
        + da
        + [((2, 1, sums), F32, pl.BlockSpec((1, 1, sums), lambda i, upper: (i, 0, 0)))],
        6,
        scratch=[pltpu.VMEM((half, wide), BF16)],
        before=before,
        scalars=(upper,),
        after=after,
    )


def input_back_kernel(rank_ref, x_ref, dh_ref, gain_ref, own_ref, *refs):
    *passed, out_ref = refs
    rank, count = rank_ref[0], len(passed) + 1
    da = own_ref[...].astype(F32)
    for t, ref in enumerate(passed):
        taken = jnp.where(pl.program_id(0) == 0, rank == t + 1, rank == count - 2 - t)
        da = jnp.where(taken, ref[...].astype(F32), da)
    x = x_ref[...].astype(F32)
    out_ref[...] = dh_ref[...] + norm_back(x, rms_factor(x), gain_ref[...], da)


def input_back(order, rank, summed, x, dh, gain_row, micro, before):
    total, width = x.shape
    rows = dh.shape[0]
    half = rows // 2
    here = pl.BlockSpec((half, width), lambda i, rank: (2 * micro + i, 0))
    one = pl.BlockSpec((half, width), lambda i, rank: (i, 0))
    passing = pl.BlockSpec((half, width), lambda i, rank: (0, 0))
    return order.call(
        input_back_kernel,
        "input_back",
        (2,),
        [(x, here), (dh, one), (gain_row, pl.BlockSpec((1, width), lambda i, rank: (0, 0)))]
        + [(block, one if len(summed) == 1 else passing) for block in summed],
        [((total, width), F32, here)],
        4,
        before=before,
        scalars=(rank,),
    )


def layer_out_kernel(hid_ref, part_ref, other_ref, out_ref):
    total = hid_ref[...] + (part_ref[...].astype(F32) + other_ref[...].astype(F32))
    out_ref[...] = total.astype(BF16)


def layer_output(order, hidden, part, other, group, total, before):
    rows, width = hidden.shape
    tiles = 4
    tile = rows // tiles
    one = pl.BlockSpec((tile, width), lambda i: (i, 0))
    return order.call(
        layer_out_kernel,
        "layer_out",
        (tiles,),
        [(hidden, one), (part, one), (other, one)],
        [((total, width), BF16, pl.BlockSpec((tile, width), lambda i: (tiles * group + i, 0)))],
        4,
        before=before,
    )


def pad_to(array, size, axis):
    missing = size - array.shape[axis]
    if missing == 0:
        return array
    widths = [(0, missing if i == axis else 0) for i in range(array.ndim)]
    return jnp.pad(array, widths)


def turned_kernel(*refs):
    out_ref, at = refs[-1], 0
    for left_ref, right_ref in zip(refs[:-1:2], refs[1:-1:2]):
        wide = right_ref.shape[1]
        product = lax.dot_general(
            left_ref[...], right_ref[...], (((0,), (0,)), ((), ())), preferred_element_type=F32
        )
        out_ref[:, at : at + wide] = product.astype(BF16)
        at += wide


def turned_products(order, pairs, us):
    height = pairs[0][0].shape[1]
    tile = 256
    ins, wide = [], 0
    for left, right in pairs:
        ins.append((left, pl.BlockSpec((left.shape[0], tile), lambda i: (0, i))))
        ins.append((right, pl.BlockSpec(right.shape, lambda i: (0, 0))))
        wide += right.shape[1]
    return order.call(
        turned_kernel,
        "turned_products",
        (height // tile,),
        ins,
        [((height, wide), BF16, pl.BlockSpec((tile, wide), lambda i: (i, 0)))],
        us,
    )[0]


def line_steps(count):
    return [((t - 1, t), (count - t, count - 1 - t)) for t in range(1, count)]


def line_sum(kept, sent, axis):
    count = lax.axis_size(axis)
    steps = line_steps(count)
    moving = sent
    for t, hops in enumerate(steps):
        arrived = lax.ppermute(moving, axis, hops)
        moving = arrived + (sent if t + 2 <= count // 2 else kept)
    passed = [moving]
    for hops in steps:
        passed.append(lax.ppermute(passed[-1], axis, hops))
    return passed


def exchanged(array, axis, flip):
    count = lax.axis_size(axis)
    return lax.ppermute(array, axis, [(i, i ^ flip) for i in range(count)])


def to_all(array, axis):
    return lax.all_to_all(array, axis, 0, 0, tiled=True)


def small_sum(row):
    for axis in ("seq", "head"):
        flip = 1
        while flip < lax.axis_size(axis):
            row = row + exchanged(row, axis, flip)
            flip *= 2
    return row


def shards(
    inputs,
    cotangent,
    tail_keys,
    tail_values,
    tail_forget,
    gain_one,
    gain_two,
    w_query,
    w_key,
    w_value,
    w_forget,
    forget_bias,
    query_gain,
    key_gain,
    w_outgate,
    w_out,
    w_gate,
    w_up,
    w_down,
):
    micros, rows, width = inputs.shape
    total = micros * rows
    own_cols = w_query.shape[1]
    heads = w_forget.shape[1]
    ff = w_gate.shape[1]
    seq_count = lax.axis_size("seq")
    head_count = lax.axis_size("head")
    seq_rank = lax.axis_index("seq")
    head_rank = lax.axis_index("head")
    cols = -(-own_cols // LANES) * LANES
    pair_total = micros * heads
    pairs = -(-pair_total // seq_count)
    padded_pairs = pairs * seq_count
    tail_length = tail_keys.shape[1]

    x = inputs.reshape(total, width)
    dy = cotangent.reshape(total, width)

    small = jnp.concatenate([w_forget, gain_one[:, None], gain_two[:, None]], axis=1)
    first_shard = jnp.concatenate(
        [pad_to(w, cols, 1) for w in (w_query, w_key, w_value, w_outgate)]
        + [pad_to(small, LANES, 1)],
        axis=1,
    )
    first = lax.all_gather(first_shard, "seq", axis=0, tiled=True)
    near_shard = jnp.concatenate([w_gate, w_up, w_down.T], axis=1)
    near = lax.all_gather(near_shard, "seq", axis=0, tiled=True)
    split = 3 * ff // 2
    outs, units, early = [pad_to(w_out.T, cols, 1)], [(near_shard[:, :split], near_shard[:, split:])], []
    flip = 1
    while flip < head_count:
        outs.append(exchanged(jnp.concatenate(outs, axis=1), "head", flip))
        early.append(outs[-1])
        if flip > 1:
            units += [tuple(exchanged(part, "head", flip) for part in unit) for unit in units]
            early += [first_part for first_part, _ in units[len(units) // 2 :]]
        flip *= 2
    far_parts = outs + [part for unit in units[1:] for part in unit]
    rank = head_rank.astype(jnp.int32)[None]
    upper = (rank >= head_count // 2).astype(jnp.int32)
    order = Order()
    gain_one_row = first[:, 4 * cols + heads].astype(F32)[None, :]
    gain_two_row = first[:, 4 * cols + heads + 1].astype(F32)[None, :]
    bias_here = lax.dynamic_slice_in_dim(forget_bias, head_rank * heads, heads, 0)
    bias_row = pad_to(bias_here[None, :], LANES, 1)
    gq_row = jnp.tile(query_gain.astype(F32), 2)[None, :]
    gk_row = jnp.tile(key_gain.astype(F32), 2)[None, :]

    tail_key_parts, tail_value_parts = [], []
    for j in range(pairs):
        p = jnp.minimum(j * seq_count + seq_rank, pair_total - 1)
        m, h = p // heads, p % heads
        tail_of = lambda array, wide: lax.dynamic_slice(
            array, (m, 0, h * wide), (1, tail_length, wide)
        )[0]
        forget = tail_of(tail_forget, 1)
        decay = jnp.cumsum(forget, axis=0) - jnp.sum(forget, axis=0, keepdims=True)
        high = lax.reduce_precision(decay, 8, 7)
        middle = lax.reduce_precision(decay - high, 8, 7)
        least = decay - high - middle
        ones = jnp.ones((tail_length, 3), BF16)
        parts = jnp.concatenate([-high, -middle, -least], axis=1).astype(BF16)
        tail_key_parts.append(
            pad_to(jnp.concatenate([tail_of(tail_keys, HEAD_SIZE), ones, parts], axis=1), LANES, 1)
        )
        tail_value_parts.append(
            pad_to(jnp.concatenate([tail_of(tail_values, HEAD_SIZE), ones], axis=1), LANES, 1)
        )
    tail_key, tail_value = jnp.stack(tail_key_parts), jnp.stack(tail_value_parts)

    def pairs_of(stages, first_micro, count):
        low, high = first_micro * heads, (first_micro + count) * heads
        taken = []
        for j, stage in enumerate(stages):
            start, stop = max(low - j * seq_count, 0), min(high - j * seq_count, seq_count)
            if start < stop:
                taken.append(stage[start:stop, 0])
        return jnp.concatenate(taken, axis=0)

    def stage_of(blocks, j):
        low, high = j * seq_count, min((j + 1) * seq_count, pair_total)
        taken = []
        for m in range(low // heads, (high - 1) // heads + 1):
            taken.append(blocks[m][max(low - m * heads, 0) : min(high - m * heads, heads)])
        return pad_to(jnp.concatenate(taken, axis=0), seq_count, 0)[:, None]

    def ready(stages):
        return len(stages) * seq_count // heads if len(stages) < pairs else micros

    a, raw, gl, pay = project(
        order, heads, cols, seq_count, x, first, bias_row, gain_one_row, gq_row, gk_row, micros, early
    )
    pay = to_all(pay, "seq")
    far = lax.all_gather(pack(order, far_parts), "seq", axis=0, tiled=True)
    packed, mixture, *saved = attend(order, pay, tail_key, tail_value)
    packed = to_all(packed, "seq")

    size = 2 if micros % 2 == 0 else 1
    groups = micros // size
    gated, o_alls = (), []
    for g in range(groups):
        *gated, sent = gate(order, heads, packed, gl, rows, g * size, size, head_count, gated)
        o_alls.append(to_all(sent, "head"))
    o = gated[0]

    chunk = min(512, ff)
    hiddens, out_parts, dc_parts, dc_others = [], [], [], []
    dhs, daps, gains_two = [], [], []
    fed, backed, returned_stages = (), (), []

    def back_to_heads(m):
        nonlocal backed
        g = m // size
        *backed, dh, dap, gain = hidden_back(
            order,
            heads,
            dc_parts[g],
            dc_others[g],
            hiddens[g],
            dy,
            gain_two_row,
            far,
            gl,
            packed,
            rows,
            m,
            m % size,
            backed,
        )
        dhs.append(dh)
        daps.append(dap)
        gains_two.append(gain)

    for g in range(groups):
        *fed, hidden, out_part, dc_part = feed(
            order,
            rank,
            x,
            dy,
            o_alls[g],
            near,
            far,
            gain_two_row,
            ff,
            chunk,
            g,
            fed,
        )
        hiddens.append(hidden)
        out_parts.append(out_part)
        dc_parts.append(dc_part)
        dc_others.append(exchanged(dc_part, "head", 1))
        if g > 0:
            for m in range((g - 1) * size, g * size):
                back_to_heads(m)
    c, u, dgu = fed

    def scattered(grad):
        return lax.psum_scatter(grad, "seq", scatter_dimension=0, tiled=True)

    unit_grads = scattered(turned_products(order, [(c, dgu), (dy, u)], 13))

    grads, da_sums, gains_one = (), [], []
    last_group = (groups - 1) * size
    da_group = []

    after = ()

    def back_to_input():
        nonlocal grads, da_group, after
        for m in range(len(gains_one), ready(returned_stages)):
            by_line = m >= last_group
            *out, gain = project_back(
                order,
                heads,
                upper,
                pairs_of(returned_stages, m, 1),
                raw,
                x,
                backed[1],
                first,
                gq_row,
                gk_row,
                rows,
                m,
                by_line,
                grads,
                after,
            )
            grads, da = out[:1], out[1:]
            gains_one.append(gain)
            after = ()
            if by_line:
                da_sums.append(line_sum(*da, "head"))
            else:
                da_group += da
                if len(da_group) == size:
                    total_da = lax.psum(jnp.concatenate(da_group, axis=0), "head")
                    da_sums.extend([total_da[i * rows : (i + 1) * rows]] for i in range(size))
                    da_group = []

    layer_out = ()

    def put_out(g):
        nonlocal layer_out
        other = exchanged(out_parts[g], "head", 1)
        layer_out = layer_output(order, hiddens[g], out_parts[g], other, g, total, layer_out)

    sent_grads = []
    for j in range(pairs):
        needed = (min((j + 1) * seq_count, pair_total) - 1) // heads
        if needed >= len(daps):
            for m in range(len(daps), micros):
                back_to_heads(m)
            mixed_grads = scattered(turned_products(order, [(backed[0], o), (a, backed[1])], 8))
        if j == len(sent_grads):
            here = [k for k in range(j, pairs) if (min((k + 1) * seq_count, pair_total) - 1) // heads < len(daps)]
            stages = jnp.concatenate([stage_of(daps, k) for k in here], axis=1)
            stages = to_all(stages, "seq")
            sent_grads += [(stages, k - j) for k in here]
        returned = attend_back(
            order, saved, tail_key, tail_value, mixture, sent_grads[j][0], pay, j, sent_grads[j][1]
        )
        returned_stages.append(to_all(returned, "seq"))
    put_out(0)
    after = (unit_grads,)
    last_stage = returned_stages.pop()
    back_to_input()
    for g in range(1, groups):
        put_out(g)
    returned_stages.append(last_stage)
    after = (mixed_grads,)
    back_to_input()
    head_grads = turned_products(order, [(a, grads[0])], 9)

    input_grad = ()
    for m in range(micros):
        input_grad = input_back(order, rank, da_sums[m], x, dhs[m], gain_one_row, m, input_grad)

    head_grads = head_grads.reshape(seq_count, -1, head_grads.shape[1])
    head_grads = jnp.sum(to_all(head_grads, "seq").astype(F32), axis=0)
    unit_grads, mixed_grads = unit_grads.astype(F32), mixed_grads.astype(F32)
    strips = [unit_grads[:, i * chunk : (i + 1) * chunk] for i in range(2 * ff // chunk)]
    grad_gate = jnp.concatenate(strips[0::2], axis=1)
    grad_up = jnp.concatenate(strips[1::2], axis=1)
    grad_down = unit_grads[:, 2 * ff :].T
    grad_out = mixed_grads[:, :own_cols].T

    one_sums = jnp.sum(jnp.concatenate(gains_one, axis=0), axis=0)
    two_sums = jnp.sum(jnp.concatenate(gains_two, axis=0), axis=0) * (1.0 / head_count)
    bias_full = lax.dynamic_update_slice(
        jnp.zeros((1, forget_bias.shape[0]), F32),
        one_sums[:, width + 2 * LANES : width + 2 * LANES + heads],
        (0, head_rank * heads),
    )
    sums = small_sum(jnp.concatenate([one_sums[:, : width + 2 * LANES], two_sums, bias_full], axis=1))[0]
    gq_total = sums[width : width + HEAD_SIZE] + sums[width + HEAD_SIZE : width + LANES]
    gk_total = sums[width + LANES : width + LANES + HEAD_SIZE] + sums[width + LANES + HEAD_SIZE : width + 2 * LANES]
    bias_total = sums[2 * width + 2 * LANES :]
    input_grad, layer_out = input_grad[0], layer_out[0]
    own_rows = gain_one.shape[0]
    own = lambda at: lax.dynamic_slice_in_dim(sums[at : at + width], seq_rank * own_rows, own_rows, 0)
    shape = inputs.shape
    return (
        layer_out.reshape(shape),
        input_grad.reshape(shape),
        own(0),
        own(width + 2 * LANES),
        head_grads[:, :own_cols],
        head_grads[:, cols : cols + own_cols],
        head_grads[:, 2 * cols : 2 * cols + own_cols],
        head_grads[:, 3 * cols : 3 * cols + heads],
        bias_total,
        gq_total,
        gk_total,
        mixed_grads[:, cols : cols + own_cols],
        grad_out,
        grad_gate,
        grad_up,
        grad_down,
    )


def solution(mesh):
    by_rows = P("seq", "head")
    by_cols = P("head", "seq")
    placed = (
        P(None, "seq", None),
        P(None, "seq", None),
        P(None, None, "head"),
        P(None, None, "head"),
        P(None, None, "head"),
        P("seq"),
        P("seq"),
        by_rows,
        by_rows,
        by_rows,
        by_rows,
        P(),
        P(),
        P(),
        by_rows,
        by_cols,
        by_rows,
        by_rows,
        by_cols,
    )
    return jax.shard_map(
        shards,
        mesh=mesh,
        in_specs=placed,
        out_specs=(
            P(None, "seq", None),
            P(None, "seq", None),
            P("seq"),
            P("seq"),
            by_rows,
            by_rows,
            by_rows,
            by_rows,
            P(),
            P(),
            P(),
            by_rows,
            by_cols,
            by_rows,
            by_rows,
            by_cols,
        ),
        check_vma=False,
    )
```

```python
import functools

import jax
import jax.numpy as jnp
from jax import lax
from jax.experimental import pallas as pl
from jax.experimental.pallas import tpu as pltpu
from jax.sharding import PartitionSpec as P

HEAD_SIZE = 64
LANES = 128
EPSILON = 1e-06
F32 = jnp.float32
BF16 = jnp.bfloat16
NN = (((1,), (0,)), ((), ()))
NT = (((1,), (1,)), ((), ()))
HIDE = -1e30
SCALE = HEAD_SIZE**-0.5
STRIP = 64
MIB = 1024 * 1024


def dot(left, right, dims=NN):
    return lax.dot_general(left, right, dims, preferred_element_type=F32)


def params():
    return pltpu.CompilerParams(vmem_limit_bytes=60 * MIB)


def linked(kernel, inputs, extra, outputs, carried):
    def body(*refs):
        first = inputs + extra
        token = refs[first + outputs + carried]
        token[...] = jnp.zeros_like(token)
        kernel(*refs[:inputs], *refs[first : first + outputs], *refs[first + outputs + carried + 1 :])

    return body


class Order:
    def __init__(self):
        self.tokens = []

    def call(
        self, kernel, name, grid, ins, outs, us, scratch=(), before=(), scalars=(), after=(), carry=()
    ):
        arrays = list(scalars) + [array for array, _ in ins]
        extra = list(before) + list(carry) + list(after) + self.tokens
        count = len(arrays)
        whole = lambda *at: (0, 0)
        anywhere = pl.BlockSpec(memory_space=pl.ANY)
        out_specs = [spec for _, _, spec in outs] + [anywhere] * len(carry)
        out_specs.append(pl.BlockSpec((8, LANES), whole))
        out_shape = [jax.ShapeDtypeStruct(shape, kind) for shape, kind, _ in outs]
        out_shape += [jax.ShapeDtypeStruct(array.shape, array.dtype) for array in carry]
        out_shape.append(jax.ShapeDtypeStruct((8, LANES), F32))
        aliases = {count + i: i for i in range(len(before))}
        for i in range(len(carry)):
            aliases[count + len(before) + i] = len(outs) + i
        *results, token = pl.pallas_call(
            linked(kernel, count, len(extra), len(outs), len(carry)),
            grid_spec=pltpu.PrefetchScalarGridSpec(
                num_scalar_prefetch=len(scalars),
                grid=grid,
                in_specs=[spec for _, spec in ins] + [anywhere] * len(extra),
                out_specs=out_specs,
                scratch_shapes=list(scratch),
            ),
            out_shape=out_shape,
            input_output_aliases=aliases,
            compiler_params=params(),
            cost_estimate=pl.CostEstimate(flops=int(us * 0.3e9), bytes_accessed=0, transcendentals=0),
            name=name,
        )(*arrays, *extra)
        self.tokens = [token]
        return results


def lanes_of(rows):
    return lax.broadcasted_iota(jnp.int32, (rows, LANES), 1)


def swap_halves(block):
    return pltpu.roll(block, HEAD_SIZE, 1)


def in_three(value):
    high = value.astype(BF16).astype(F32)
    rest = value - high
    middle = rest.astype(BF16).astype(F32)
    return high, middle, rest - middle


def at_lanes(lane, first, parts, base):
    for place, part in enumerate(parts):
        base = jnp.where(lane == first + place, part, base)
    return base


def triangle(rows, lower):
    down = lax.broadcasted_iota(jnp.int32, (rows, rows), 0)
    across = lax.broadcasted_iota(jnp.int32, (rows, rows), 1)
    return jnp.where(down >= across if lower else down <= across, 1.0, 0.0).astype(BF16)


def running_sum(tri, column, lane):
    spread = at_lanes(lane, 0, in_three(column), jnp.zeros(lane.shape, F32))
    sums = dot(tri, spread.astype(BF16))
    return sums[:, 0:1] + sums[:, 1:2] + sums[:, 2:3]


def forget_column(tail_block):
    return tail_block[:, 64:65] + tail_block[:, 65:66] + tail_block[:, 66:67]


def per_head(low, values):
    first = jnp.sum(jnp.where(low, values, 0.0), axis=-1, keepdims=True)
    second = jnp.sum(jnp.where(low, 0.0, values), axis=-1, keepdims=True)
    return jnp.where(low, first, second) * (1.0 / HEAD_SIZE)


def rms_factor(values):
    return lax.rsqrt(jnp.mean(values * values, axis=-1, keepdims=True) + EPSILON)


def merge_pair(low, first, second):
    return jnp.where(low, first, swap_halves(second))


def merge_swapped(low, first, second):
    return jnp.where(low, swap_halves(first), second)


def put_pair(refs, pair, block, column=0, start=0):
    owners = refs[0].shape[0]
    owner, place = lax.rem(pair, owners), lax.div(pair, owners)
    width = block.shape[1]
    for ref in refs:
        stop = start + ref.shape[1]

        @pl.when((place >= start) & (place < stop))
        def _(ref=ref, start=start):
            ref[owner, place - start, :, column : column + width] = block

        start = stop


def unpack_rows(low_half, first, second):
    strip = low_half.shape[0]
    rows = []
    for at in range(0, first.shape[0], strip):
        one, two = first[at : at + strip], second[at : at + strip]
        rows.append(jnp.where(low_half, one, swap_halves(two)))
        rows.append(jnp.where(low_half, swap_halves(one), two))
    return jnp.concatenate(rows, axis=0)


def pack_rows(low_half, block):
    strip = low_half.shape[0]
    first, second = [], []
    for at in range(0, block.shape[0], 2 * strip):
        top, bottom = block[at : at + strip], block[at + strip : at + 2 * strip]
        first.append(jnp.where(low_half, top, swap_halves(bottom)))
        second.append(jnp.where(low_half, swap_halves(top), bottom))
    return jnp.concatenate(first, axis=0), jnp.concatenate(second, axis=0)


def project_kernel(
    heads, idle, x_ref, w_ref, bias_ref, gain_ref, gq_ref, gk_ref, a_ref, raw_ref, gl_ref, *pay_refs
):
    x = x_ref[...].astype(F32)
    rows = x.shape[0]
    cols = gl_ref.shape[1]
    a = (x * rms_factor(x) * gain_ref[...]).astype(BF16)
    a_ref[...] = a
    proj = dot(a, w_ref[...])
    raw_ref[...] = proj[:, : 2 * cols]
    gl_ref[...] = proj[:, 3 * cols : 4 * cols]
    logit = proj[:, 4 * cols :] + bias_ref[...]
    lane = lanes_of(rows)
    low = lane < HEAD_SIZE
    for group in range(cols // LANES):
        at = group * LANES
        query = proj[:, at : at + LANES]
        key = proj[:, cols + at : cols + at + LANES]
        value = proj[:, 2 * cols + at : 2 * cols + at + LANES]
        query = query * lax.rsqrt(per_head(low, query * query) + EPSILON) * gq_ref[...]
        key = key * lax.rsqrt(per_head(low, key * key) + EPSILON) * gk_ref[...]
        for half in range(2):
            head = 2 * group + half
            if head >= heads:
                continue
            zl = at_lanes(lane, 64, in_three(logit[:, head : head + 1]), jnp.zeros(lane.shape, F32))
            if half == 0:
                both = merge_pair(low, query, key)
                rest = jnp.where(low, value, zl)
            else:
                both = merge_swapped(low, query, key)
                rest = jnp.where(low, swap_halves(value), zl)
            pair = pl.program_id(0) * heads + head
            put_pair(pay_refs, pair, both.astype(BF16))
            put_pair(pay_refs, pair, rest.astype(BF16), LANES)

    @pl.when(pl.program_id(0) == 0)
    def _():
        for pair in idle:
            put_pair(pay_refs, pair, jnp.zeros((rows, 2 * LANES), BF16))


def project(order, heads, cols, owners, x, weights, bias_row, gain_row, gq_row, gk_row, micros, after):
    total, width = x.shape
    rows = total // micros
    wide = weights.shape[1]
    whole = lambda m: (0, 0)
    part = lambda m: (m, 0)
    row = pl.BlockSpec((1, LANES), whole)
    pairs = -(-micros * heads // owners)
    idle = range(micros * heads, pairs * owners)
    parts = [pairs - 1, 1] if pairs > 1 else [1]
    sent = [(owners, part, rows, 2 * LANES) for part in parts]
    return order.call(
        functools.partial(project_kernel, heads, idle),
        "project",
        (micros,),
        [
            (x, pl.BlockSpec((rows, width), part)),
            (weights, pl.BlockSpec((width, wide), whole)),
            (bias_row, row),
            (gain_row, pl.BlockSpec((1, width), whole)),
            (gq_row, row),
            (gk_row, row),
        ],
        [
            ((total, width), BF16, pl.BlockSpec((rows, width), part)),
            ((total, 2 * cols), F32, pl.BlockSpec((rows, 2 * cols), part)),
            ((total, cols), F32, pl.BlockSpec((rows, cols), part)),
        ]
        + [(shape, BF16, pl.BlockSpec(shape, lambda m: (0, 0, 0, 0))) for shape in sent],
        13,
        after=after,
    )


def attend_kernel(size, pay_ref, tk_ref, tv_ref, ap_ref, af_ref, q_ref, k_ref, v_ref):
    blocks, _, rows, _ = pay_ref.shape
    length = blocks * rows
    lane = lanes_of(rows)
    low = lane < HEAD_SIZE
    tri = triangle(rows, True)
    zero = jnp.zeros(lane.shape, F32)

    def build(b, carry):
        at = pl.ds(pl.multiple_of(b * rows, rows), rows)
        both = pay_ref[b, 0, :, :LANES].astype(F32)
        rest = pay_ref[b, 0, :, LANES:].astype(F32)
        logit = forget_column(rest)
        log_forget = jnp.minimum(logit, 0.0) - jnp.log1p(jnp.exp(-jnp.abs(logit)))
        decay = running_sum(tri, log_forget, lane) + carry
        high, middle, least = in_three(decay)
        query_side = at_lanes(lane, 64, (high, middle, least, 1.0, 1.0, 1.0), zero)
        key_side = at_lanes(lane, 64, (1.0, 1.0, 1.0, -high, -middle, -least), zero)
        value_side = at_lanes(lane, 64, (1.0, 1.0, 1.0), zero)
        q_ref[0, at, :] = jnp.where(low, both * SCALE, query_side).astype(BF16)
        k_ref[0, at, :] = jnp.where(low, swap_halves(both), key_side).astype(BF16)
        v_ref[0, at, :] = jnp.where(low, rest, value_side).astype(BF16)
        return decay[rows - 1 :, :]

    lax.fori_loop(0, blocks, build, jnp.zeros((1, 1), F32))

    tail_length = tk_ref.shape[1]
    visible = lax.broadcasted_iota(jnp.int32, (size, size), 0) >= lax.broadcasted_iota(
        jnp.int32, (size, size), 1
    )
    half_low = lanes_of(STRIP) < HEAD_SIZE
    lane_here = lanes_of(size)

    def one_block(qi):
        at = pl.ds(qi * size, size)
        query = q_ref[0, at, :]

        def absorb(key, value, total, masked=False):
            scores = dot(query, key, NT)
            if masked:
                scores = jnp.where(visible, scores, HIDE)
            return total + dot(jnp.exp(scores).astype(BF16), value)

        total = jnp.zeros((size, LANES), F32)
        for t in range(tail_length // size):
            here = pl.ds(t * size, size)
            total = absorb(tk_ref[0, here, :], tv_ref[0, here, :], total)

        for ki in range(qi):
            here = pl.ds(ki * size, size)
            total = absorb(k_ref[0, here, :], v_ref[0, here, :], total)
        total = absorb(k_ref[0, at, :], v_ref[0, at, :], total, True)
        weight = total[:, 64:65]
        mixture = total / weight
        af_ref[0, at, :] = mixture
        for piece in range(size // rows):
            block = mixture[piece * rows : (piece + 1) * rows]
            packed, _ = pack_rows(half_low, block)
            ap_ref[qi * (size // rows) + piece, 0] = packed.astype(BF16)
        old = query.astype(F32)
        shifted = forget_column(old) - jnp.log(weight)
        q_ref[0, at, :] = at_lanes(lane_here, 64, in_three(shifted), old).astype(BF16)

    for qi in range(length // size):
        one_block(qi)


def attend(order, pay, tail_key, tail_value, first):
    blocks, pairs, rows, _ = pay.shape
    length = blocks * rows
    tail_length = tail_key.shape[1]
    size = min(512, length)
    pair = lambda j: (j, 0, 0)
    across = lambda j: (0, j, 0, 0)
    tail = pl.BlockSpec((1, tail_length, LANES), lambda j: (first + j, 0, 0))
    whole = pl.BlockSpec((1, length, LANES), pair)
    return order.call(
        functools.partial(attend_kernel, size),
        "attend",
        (pairs,),
        [
            (pay, pl.BlockSpec((blocks, 1, rows, 2 * LANES), across)),
            (tail_key, tail),
            (tail_value, tail),
        ],
        [
            (
                (blocks, pairs, rows // 2, LANES),
                BF16,
                pl.BlockSpec((blocks, 1, rows // 2, LANES), across),
            ),
            ((pairs, length, LANES), F32, whole),
            ((pairs, length, LANES), BF16, whole),
            ((pairs, length, LANES), BF16, whole),
            ((pairs, length, LANES), BF16, whole),
        ],
        17 * pairs,
    )


def attend_back_kernel(
    size,
    q_ref,
    k_ref,
    v_ref,
    tk_ref,
    tv_ref,
    af_ref,
    dap_ref,
    rest_ref,
    g_ref,
    da_ref,
    dqt_ref,
    sums_ref,
):
    blocks, _, rows, _ = rest_ref.shape
    length = blocks * rows
    lane = lanes_of(rows)
    low = lane < HEAD_SIZE
    zero = jnp.zeros(lane.shape, F32)

    def build(b, carry):
        at = pl.ds(pl.multiple_of(b * rows, rows), rows)
        packed = dap_ref[b, 0].astype(F32)
        strips = []
        for strip in range(0, packed.shape[0], STRIP):
            strips += [packed[strip : strip + STRIP], swap_halves(packed[strip : strip + STRIP])]
        grad = jnp.where(low, jnp.concatenate(strips, axis=0), 0.0)
        delta = jnp.sum(grad * af_ref[0, at, :], axis=-1, keepdims=True)
        da_ref[at, :] = at_lanes(lane, 64, in_three(-delta), grad).astype(BF16)
        return carry

    lax.fori_loop(0, blocks, build, 0)

    across = lax.broadcasted_iota(jnp.int32, (size, size), 1)
    down = lax.broadcasted_iota(jnp.int32, (size, size), 0)
    visible = across >= down
    count = length // size

    def block_at(i):
        return pl.ds(i * size, size)

    def pieces(key, value, at, masked=False):
        scores = dot(key, q_ref[0, at, :], NT)
        if masked:
            scores = jnp.where(visible, scores, HIDE)
        prob = jnp.exp(scores)
        score_grad = prob * dot(value, da_ref[at, :], NT)
        return prob.astype(BF16), score_grad.astype(BF16)

    tail_length = tk_ref.shape[1]
    tail_count = tail_length // size

    for qi in range(count):
        at = block_at(qi)
        total = jnp.zeros((LANES, size), F32)
        for t in range(tail_count):
            key = tk_ref[0, pl.ds(t * size, size), :]
            _, score_grad = pieces(key, tv_ref[0, pl.ds(t * size, size), :], at)
            total = total + dot(key.T, score_grad)
        dqt_ref[:, at] = total

    lane_here = lanes_of(size)
    low_here = lane_here < HEAD_SIZE

    for ki in range(count):
        own = block_at(ki)
        key = k_ref[0, own, :]
        value = v_ref[0, own, :]
        key_turned = key.T

        def one(at, sums, masked=False, key=key, value=value, key_turned=key_turned):
            key_sum, value_sum = sums
            prob, score_grad = pieces(key, value, at, masked)
            dqt_ref[:, at] += dot(key_turned, score_grad)
            return (
                key_sum + dot(score_grad, q_ref[0, at, :]),
                value_sum + dot(prob, da_ref[at, :]),
            )

        start = (jnp.zeros((size, LANES), F32), jnp.zeros((size, LANES), F32))
        sums = one(own, start, True)
        for qi in range(ki + 1, count):
            sums = one(block_at(qi), sums)
        key_sum, value_sum = sums
        sums_ref[own, :] = key_sum
        for piece in range(size // rows):
            here = slice(piece * rows, (piece + 1) * rows)
            g_ref[ki * (size // rows) + piece, 0, :, LANES:] = value_sum[here].astype(BF16)

    tri = triangle(rows, False)

    def finish(i, carry):
        b = blocks - 1 - i
        at = pl.ds(pl.multiple_of(b * rows, rows), rows)
        query = dqt_ref[:, at].T
        key = sums_ref[at, :]
        decay_grad = query[:, 64:65] - key[:, 67:68]
        suffix = running_sum(tri, decay_grad, lane) + carry
        logit = forget_column(rest_ref[b, 0].astype(F32))
        forget_grad = suffix / (1.0 + jnp.exp(logit))
        both = jnp.where(low, query * SCALE, swap_halves(key))
        rest = jnp.where(low, g_ref[b, 0, :, LANES:].astype(F32), jnp.where(lane == 64, forget_grad, 0.0))
        g_ref[b, 0, :, :LANES] = both.astype(BF16)
        g_ref[b, 0, :, LANES:] = rest.astype(BF16)
        return suffix[0:1, :]

    lax.fori_loop(0, blocks, finish, jnp.zeros((1, 1), F32))


def attend_back(
    order, saved, tail_key, tail_value, mixture, packed_grad, pay, place, saved_place, grad_place, carry, after
):
    blocks, _, rows, _ = pay.shape
    length = blocks * rows
    tail_length = tail_key.shape[1]
    size = min(512, length)
    pair = lambda j: (place, 0, 0)
    tail = pl.BlockSpec((1, tail_length, LANES), pair)
    whole = pl.BlockSpec((1, length, LANES), lambda j: (saved_place, 0, 0))
    grad = pl.BlockSpec((blocks, 1, rows // 2, LANES), lambda j: (0, grad_place, 0, 0))
    sent = (blocks, 1, rows, 2 * LANES)
    return order.call(
        functools.partial(attend_back_kernel, size),
        "attend_back",
        (1,),
        [(array, whole) for array in saved]
        + [
            (tail_key, tail),
            (tail_value, tail),
            (mixture, whole),
            (packed_grad, grad),
            (pay, pl.BlockSpec((blocks, 1, rows, LANES), lambda j: (0, saved_place, 0, 1))),
        ],
        [(sent, BF16, pl.BlockSpec(sent, lambda j: (0, 0, 0, 0)))],
        22,
        scratch=[
            pltpu.VMEM((length, LANES), BF16),
            pltpu.VMEM((LANES, length), F32),
            pltpu.VMEM((length, LANES), F32),
        ],
        carry=carry,
        after=after,
    )


def group_of(heads, ref, first_pair, group, low_half):
    owners = ref.shape[0]

    def packed(head):
        if head >= heads:
            return jnp.zeros(ref.shape[2:], F32)
        pair = first_pair + head
        if isinstance(pair, int):
            return ref[pair % owners, pair // owners].astype(F32)
        return ref[lax.rem(pair, owners), lax.div(pair, owners)].astype(F32)

    return unpack_rows(low_half, packed(2 * group), packed(2 * group + 1))


def gate_kernel(heads, first, ap_ref, gl_ref, o_ref, sent_ref):
    rows, cols = o_ref.shape
    half_low = lanes_of(STRIP) < HEAD_SIZE
    pair = (first + pl.program_id(0)) * heads
    for group in range(cols // LANES):
        at = slice(group * LANES, (group + 1) * LANES)
        mixture = group_of(heads, ap_ref, pair, group, half_low)
        gated = (mixture * jax.nn.sigmoid(gl_ref[:, at])).astype(BF16)
        o_ref[:, at] = gated
        for z in range(sent_ref.shape[0]):
            sent_ref[z, :, at] = gated


def gate(order, heads, packed, gl, rows, first, count, copies, before):
    total, cols = gl.shape
    here = pl.BlockSpec((rows, cols), lambda i: (first + i, 0))
    return order.call(
        functools.partial(gate_kernel, heads, first),
        "gate",
        (count,),
        [(packed, pl.BlockSpec(packed.shape, lambda i: (0, 0, 0, 0))), (gl, here)],
        [
            ((total, cols), BF16, here),
            (
                (copies, count * rows, cols),
                BF16,
                pl.BlockSpec((copies, rows, cols), lambda i: (0, i, 0)),
            ),
        ],
        2 * count,
        before=before,
    )


def pack_kernel(*refs):
    out_ref, at = refs[-1], 0
    for ref in refs[:-1]:
        wide = ref.shape[1]
        out_ref[:, at : at + wide] = ref[...]
        at += wide


def pack(order, arrays):
    rows = arrays[0].shape[0]
    wide = sum(array.shape[1] for array in arrays)
    whole = lambda i: (0, 0)
    return order.call(
        pack_kernel,
        "pack",
        (1,),
        [(array, pl.BlockSpec(array.shape, whole)) for array in arrays],
        [((rows, wide), BF16, pl.BlockSpec((rows, wide), whole))],
        2,
    )[0]


def feed_kernel(
    parts,
    own,
    rank_ref,
    x_ref,
    dy_ref,
    wo_ref,
    wg_ref,
    wu_ref,
    wd_ref,
    wg_far_ref,
    wu_far_ref,
    wd_far_ref,
    gain_ref,
    *refs,
):
    o_ref, c_ref, u_ref, dgu_ref, hid_ref, out_ref, dc_ref, out_acc, dc_acc = refs
    step = pl.program_id(0)
    last = pl.num_programs(0) - 1

    def attended():
        return dot(o_ref[0], wo_ref[...], NT)

    @pl.when(step == 0)
    def _():
        hid_ref[...] = x_ref[...].astype(F32) + attended()

    @pl.when((step > 0) & (step < parts))
    def _():
        hid_ref[...] += attended()

    @pl.when(step == parts - 1)
    def _():
        hidden = hid_ref[...]
        c_ref[...] = (hidden * rms_factor(hidden) * gain_ref[...]).astype(BF16)
        out_acc[...] = jnp.zeros_like(out_acc)
        dc_acc[...] = jnp.zeros_like(dc_acc)

    def chunk(w_gate, w_up, w_down):
        c = c_ref[...]
        gr = dot(c, w_gate[...])
        ur = dot(c, w_up[...])
        sig = jax.nn.sigmoid(gr)
        silu = gr * sig
        u = (silu * ur).astype(BF16)
        du = dot(dy_ref[...], w_down[...])
        dgr = (du * ur * sig * (1.0 + gr * (1.0 - sig))).astype(BF16)
        dur = (du * silu).astype(BF16)
        out_acc[...] += dot(u, w_down[...], NT)
        dc_acc[...] += dot(dgr, w_gate[...], NT) + dot(dur, w_up[...], NT)
        return u, dgr, dur

    @pl.when((step >= parts) & (step < parts + own))
    def _():
        u, dgr, dur = chunk(wg_ref, wu_ref, wd_ref)
        wide = u.shape[1]
        u_ref[...] = u
        dgu_ref[:, :wide] = dgr
        dgu_ref[:, wide:] = dur

    @pl.when(step >= parts + own)
    def _():
        chunk(wg_far_ref, wu_far_ref, wd_far_ref)

    @pl.when(step == last)
    def _():
        out_ref[...] = out_acc[...].astype(BF16)
        dc_ref[...] = dc_acc[...].astype(BF16)


def feed(order, rank, x, dy, o_all, near, far, gain_row, ff, chunk, group, before):
    parts, rows, cols = o_all.shape
    total, width = x.shape
    own = ff // chunk
    offset = parts * cols // chunk
    others = (far.shape[1] - parts * cols) // (3 * ff)
    steps = parts + (1 + others) * own
    whole = lambda i, rank: (0, 0)
    here = lambda i, rank: (group, 0)
    early = lambda i: jnp.minimum(i, parts - 1)
    mine = lambda i: jnp.clip(i - parts, 0, own - 1)

    def near_strip(k):
        return pl.BlockSpec((width, chunk), lambda i, rank: (0, k * own + mine(i)))

    def far_strip(k):
        def place(i, rank):
            s = jnp.maximum(i - parts - own, 0)
            return (0, offset + (s // own * 3 + k) * own + s % own)

        return pl.BlockSpec((width, chunk), place)

    wide = pl.BlockSpec((rows, width), whole)
    return order.call(
        functools.partial(feed_kernel, parts, own),
        "feed",
        (steps,),
        [
            (x, pl.BlockSpec((rows, width), here)),
            (dy, pl.BlockSpec((rows, width), here)),
            (far, pl.BlockSpec((width, cols), lambda i, rank: (0, early(i)))),
            (near, near_strip(0)),
            (near, near_strip(1)),
            (near, near_strip(2)),
            (far, far_strip(0)),
            (far, far_strip(1)),
            (far, far_strip(2)),
            (gain_row, pl.BlockSpec((1, width), whole)),
        ]
        + [(o_all, pl.BlockSpec((1, rows, cols), lambda i, rank: (rank[0] ^ early(i), 0, 0)))],
        [
            ((total, width), BF16, pl.BlockSpec((rows, width), here)),
            ((total, ff), BF16, pl.BlockSpec((rows, chunk), lambda i, rank: (group, mine(i)))),
            (
                (total, 2 * ff),
                BF16,
                pl.BlockSpec((rows, 2 * chunk), lambda i, rank: (group, mine(i))),
            ),
            ((rows, width), F32, wide),
            ((rows, width), BF16, wide),
            ((rows, width), BF16, wide),
        ],
        37,
        scratch=[pltpu.VMEM((rows, width), F32), pltpu.VMEM((rows, width), F32)],
        before=before,
        scalars=(rank,),
    )


def norm_back(source, factor, gain_row, upstream):
    scaled = upstream * gain_row
    inner = jnp.mean(scaled * source, axis=-1, keepdims=True)
    return factor * scaled - source * (factor * factor * factor) * inner


def hidden_back_kernel(
    heads,
    first,
    start,
    with_old,
    dc_ref,
    dc_other_ref,
    hid_ref,
    dy_ref,
    gain_ref,
    w_ref,
    gl_ref,
    ap_ref,
    *refs,
):
    if with_old:
        old_ref, *refs = refs
    dhb_ref, dgl_ref, dh_ref, dg_ref, *dap_refs = refs
    rows, cols = gl_ref.shape
    pair = (first + pl.program_id(0)) * heads
    if with_old:

        @pl.when(pl.program_id(0) == 0)
        def _():
            dap_refs[0][...] = old_ref[...]

    hidden = hid_ref[...]
    factor = rms_factor(hidden)
    dc = dc_ref[...].astype(F32) + dc_other_ref[...].astype(F32)
    dh = dy_ref[...].astype(F32) + norm_back(hidden, factor, gain_ref[...], dc)
    dg_ref[0] = jnp.sum(dc * hidden * factor, axis=0, keepdims=True)
    dh_ref[...] = dh
    dhb = dh.astype(BF16)
    dhb_ref[...] = dhb
    gated_grad = dot(dhb, w_ref[...])
    half_low = lanes_of(STRIP) < HEAD_SIZE
    for group in range(cols // LANES):
        at = slice(group * LANES, (group + 1) * LANES)
        mixture = group_of(heads, ap_ref, pair, group, half_low)
        gate_value = jax.nn.sigmoid(gl_ref[:, at])
        grad = gated_grad[:, at]
        dgl_ref[:, at] = (grad * mixture * gate_value * (1.0 - gate_value)).astype(BF16)
        for half, packed in enumerate(pack_rows(half_low, grad * gate_value)):
            if 2 * group + half < heads:
                put_pair(dap_refs, pair + 2 * group + half, packed.astype(BF16), start=start)


def hidden_back(
    order, heads, dc, dc_other, hidden, dy, gain_row, weights, gl, packed, rows, first, places, old, before, carry
):
    total, cols = gl.shape
    group, width = dc.shape
    count = group // rows
    whole = lambda i: (0, 0)
    here = lambda i: (first + i, 0)
    part = pl.BlockSpec((rows, width), lambda i: (i, 0))
    every = lambda shape: pl.BlockSpec(shape, lambda i: (0,) * len(shape))
    sent = [(packed.shape[0], stop - start, rows // 2, LANES) for start, stop in places]
    return order.call(
        functools.partial(hidden_back_kernel, heads, first, places[0][0], bool(old)),
        "hidden_back",
        (count,),
        [
            (dc, part),
            (dc_other, part),
            (hidden, part),
            (dy, pl.BlockSpec((rows, width), here)),
            (gain_row, pl.BlockSpec((1, width), whole)),
            (weights, pl.BlockSpec((width, cols), whole)),
            (gl, pl.BlockSpec((rows, cols), here)),
            (packed, every(packed.shape)),
        ]
        + [(array, every(array.shape)) for array in old],
        [
            ((total, width), BF16, pl.BlockSpec((rows, width), here)),
            ((total, cols), BF16, pl.BlockSpec((rows, cols), here)),
            ((group, width), F32, part),
            ((count, 1, width), F32, pl.BlockSpec((1, 1, width), lambda i: (i, 0, 0))),
        ]
        + [(shape, BF16, every(shape)) for shape in sent],
        4 * count,
        before=before,
        carry=carry,
    )


def project_back_kernel(
    heads,
    upper_ref,
    g_ref,
    raw_ref,
    x_ref,
    dgl_ref,
    w_ref,
    gq_ref,
    gk_ref,
    grads_ref,
    *refs,
):
    *da_refs, sums_ref, all_ref, da_ref = refs
    rows, cols = dgl_ref.shape
    width = x_ref.shape[1]
    lane = lanes_of(rows)
    low = lane < HEAD_SIZE
    zero = jnp.zeros(lane.shape, F32)
    sums = [jnp.zeros((1, LANES), F32), jnp.zeros((1, LANES), F32)]

    def head_back(raw, upstream, gain_row, which):
        factor = lax.rsqrt(per_head(low, raw * raw) + EPSILON)
        scaled = upstream * gain_row
        inner = per_head(low, scaled * raw)
        sums[which] += jnp.sum(upstream * raw * factor, axis=0, keepdims=True)
        return factor * scaled - raw * (factor * factor * factor) * inner

    forget = zero
    for group in range(cols // LANES):
        at = group * LANES
        here = slice(at, at + LANES)
        pair = (2 * group, 2 * group + 1)
        both = [g_ref[h, :, :LANES].astype(F32) if h < heads else zero for h in pair]
        rest = [g_ref[h, :, LANES:].astype(F32) if h < heads else zero for h in pair]
        query = head_back(raw_ref[:, here], merge_pair(low, *both), gq_ref[...], 0)
        key = head_back(
            raw_ref[:, cols + at : cols + at + LANES],
            merge_swapped(low, *both),
            gk_ref[...],
            1,
        )
        all_ref[:, here] = query.astype(BF16)
        all_ref[:, cols + at : cols + at + LANES] = key.astype(BF16)
        value = merge_pair(low, *rest)
        all_ref[:, 2 * cols + at : 2 * cols + at + LANES] = value.astype(BF16)
        for h, block in zip(pair, rest):
            if h < heads:
                forget = jnp.where(lane == h, block[:, 64:65], forget)
    all_ref[:, 3 * cols : 4 * cols] = dgl_ref[...]
    all_ref[:, 4 * cols :] = forget.astype(BF16)
    grads_ref[:, : 3 * cols] = all_ref[:, : 3 * cols]
    grads_ref[:, 3 * cols :] = all_ref[:, 4 * cols :]
    da = dot(all_ref[...], w_ref[...], NT)
    if len(da_refs) == 1:
        da_refs[0][...] = da.astype(BF16)
    else:
        da_ref[...] = da
        half = rows // 2
        upper = upper_ref[0]
        for ref, part in zip(da_refs, (upper, 1 - upper)):
            ref[0] = da_ref[pl.ds(pl.multiple_of(part * half, half), half), :].astype(BF16)

    x = x_ref[...].astype(F32)
    sums_ref[0, :, :width] = jnp.sum(da * x * rms_factor(x), axis=0, keepdims=True)
    sums_ref[0, :, width : width + LANES] = sums[0]
    sums_ref[0, :, width + LANES : width + 2 * LANES] = sums[1]
    sums_ref[0, :, width + 2 * LANES :] = jnp.sum(forget, axis=0, keepdims=True)


def project_back(
    order, heads, upper, returned, raw, x, dgl, weights, gq_row, gk_row, rows, first, count, halves, before, after, carry
):
    total, cols = dgl.shape
    width, wide = weights.shape
    half = rows // 2
    whole = lambda i, upper: (0, 0)
    here = lambda i, upper: (first + i, 0)
    row = pl.BlockSpec((1, LANES), whole)
    sums = width + 3 * LANES
    if halves:
        da = [((count, half, width), BF16, pl.BlockSpec((1, half, width), lambda i, upper: (i, 0, 0)))] * 2
    else:
        da = [((count * rows, width), BF16, pl.BlockSpec((rows, width), lambda i, upper: (i, 0)))]
    return order.call(
        functools.partial(project_back_kernel, heads),
        "project_back",
        (count,),
        [
            (returned, pl.BlockSpec((heads, rows, 2 * LANES), lambda i, upper: (i, 0, 0))),
            (raw, pl.BlockSpec((rows, 2 * cols), here)),
            (x, pl.BlockSpec((rows, width), here)),
            (dgl, pl.BlockSpec((rows, cols), here)),
            (weights, pl.BlockSpec((width, wide), whole)),
            (gq_row, row),
            (gk_row, row),
        ],
        [((total, wide - cols), BF16, pl.BlockSpec((rows, wide - cols), here))]
        + da
        + [((count, 1, sums), F32, pl.BlockSpec((1, 1, sums), lambda i, upper: (i, 0, 0)))],
        6 * count,
        scratch=[pltpu.VMEM((rows, wide), BF16), pltpu.VMEM((rows, width), F32)],
        before=before,
        scalars=(upper,),
        after=after,
        carry=carry,
    )


def input_back_kernel(rank_ref, x_ref, dh_ref, gain_ref, own_ref, *refs):
    *passed, out_ref = refs
    rank, count = rank_ref[0], len(passed) + 1
    da = own_ref[...].astype(F32)
    for t, ref in enumerate(passed):
        taken = jnp.where(pl.program_id(0) == 0, rank == t + 1, rank == count - 2 - t)
        da = jnp.where(taken, ref[...].astype(F32), da)
    x = x_ref[...].astype(F32)
    out_ref[...] = dh_ref[...] + norm_back(x, rms_factor(x), gain_ref[...], da)


def input_back(order, rank, summed, place, x, dh, dh_place, gain_row, rows, micro, before, after):
    total, width = x.shape
    half = rows // 2
    here = pl.BlockSpec((half, width), lambda i, rank: (2 * micro + i, 0))
    one = pl.BlockSpec((half, width), lambda i, rank: (2 * place + i, 0))
    mine = pl.BlockSpec((half, width), lambda i, rank: (2 * dh_place + i, 0))
    passing = pl.BlockSpec((half, width), lambda i, rank: (0, 0))
    return order.call(
        input_back_kernel,
        "input_back",
        (2,),
        [(x, here), (dh, mine), (gain_row, pl.BlockSpec((1, width), lambda i, rank: (0, 0)))]
        + [(block, one if len(summed) == 1 else passing) for block in summed],
        [((total, width), F32, here)],
        4,
        before=before,
        scalars=(rank,),
        after=after,
    )


def layer_out_kernel(hid_ref, part_ref, other_ref, out_ref):
    total = hid_ref[...] + (part_ref[...].astype(F32) + other_ref[...].astype(F32))
    out_ref[...] = total.astype(BF16)


def layer_output(order, hidden, part, other, group, total, before, after):
    rows, width = hidden.shape
    tiles = 4
    tile = rows // tiles
    one = pl.BlockSpec((tile, width), lambda i: (i, 0))
    return order.call(
        layer_out_kernel,
        "layer_out",
        (tiles,),
        [(hidden, one), (part, one), (other, one)],
        [((total, width), BF16, pl.BlockSpec((tile, width), lambda i: (tiles * group + i, 0)))],
        4,
        before=before,
        after=after,
    )


def pad_to(array, size, axis):
    missing = size - array.shape[axis]
    if missing == 0:
        return array
    widths = [(0, missing if i == axis else 0) for i in range(array.ndim)]
    return jnp.pad(array, widths)


def turned_kernel(*refs):
    out_ref, at = refs[-1], 0
    for left_ref, right_ref in zip(refs[:-1:2], refs[1:-1:2]):
        wide = right_ref.shape[1]
        product = lax.dot_general(
            left_ref[...], right_ref[...], (((0,), (0,)), ((), ())), preferred_element_type=F32
        )
        out_ref[:, at : at + wide] = product.astype(BF16)
        at += wide


def turned_products(order, pairs, us):
    height = pairs[0][0].shape[1]
    tile = 256
    ins, wide = [], 0
    for left, right in pairs:
        ins.append((left, pl.BlockSpec((left.shape[0], tile), lambda i: (0, i))))
        ins.append((right, pl.BlockSpec(right.shape, lambda i: (0, 0))))
        wide += right.shape[1]
    return order.call(
        turned_kernel,
        "turned_products",
        (height // tile,),
        ins,
        [((height, wide), BF16, pl.BlockSpec((tile, wide), lambda i: (i, 0)))],
        us,
    )[0]


def owned_kernel(own, left_ref, right_ref, sums_ref, out_ref):
    product = lax.dot_general(
        left_ref[...], right_ref[...], (((0,), (0,)), ((), ())), preferred_element_type=F32
    ).astype(BF16)
    for i in range(out_ref.shape[0]):
        out_ref[i, :own] = product[i * own : (i + 1) * own]
        out_ref[i, own:] = sums_ref[i]


def owned_product(order, left, right, sums, us):
    rows, height = left.shape
    owners, extra, wide = sums.shape
    own = height // owners
    step = 1
    while own * step % LANES:
        step += 1
    return order.call(
        functools.partial(owned_kernel, own),
        "owned_product",
        (owners // step,),
        [
            (left, pl.BlockSpec((rows, own * step), lambda i: (0, i))),
            (right, pl.BlockSpec((rows, wide), lambda i: (0, 0))),
            (sums, pl.BlockSpec((step, extra, wide), lambda i: (i, 0, 0))),
        ],
        [((owners, own + extra, wide), BF16, pl.BlockSpec((step, own + extra, wide), lambda i: (i, 0, 0)))],
        us,
    )[0]


def line_steps(count):
    return [((t - 1, t), (count - t, count - 1 - t)) for t in range(1, count)]


def line_sum(kept, sent, axis):
    count = lax.axis_size(axis)
    steps = line_steps(count)
    moving = sent
    for t, hops in enumerate(steps):
        arrived = lax.ppermute(moving, axis, hops)
        moving = arrived + (sent if t + 2 <= count // 2 else kept)
    passed = [moving]
    for hops in steps:
        passed.append(lax.ppermute(passed[-1], axis, hops))
    return passed


def exchanged(array, axis, flip):
    count = lax.axis_size(axis)
    return lax.ppermute(array, axis, [(i, i ^ flip) for i in range(count)])


def to_all(array, axis):
    return lax.all_to_all(array, axis, 0, 0, tiled=True)


def small_sum(row, axis):
    flip = 1
    while flip < lax.axis_size(axis):
        row = row + exchanged(row, axis, flip)
        flip *= 2
    return row


def shards(
    inputs,
    cotangent,
    tail_keys,
    tail_values,
    tail_forget,
    gain_one,
    gain_two,
    w_query,
    w_key,
    w_value,
    w_forget,
    forget_bias,
    query_gain,
    key_gain,
    w_outgate,
    w_out,
    w_gate,
    w_up,
    w_down,
):
    micros, rows, width = inputs.shape
    total = micros * rows
    own_cols = w_query.shape[1]
    heads = w_forget.shape[1]
    ff = w_gate.shape[1]
    seq_count = lax.axis_size("seq")
    head_count = lax.axis_size("head")
    seq_rank = lax.axis_index("seq")
    head_rank = lax.axis_index("head")
    cols = -(-own_cols // LANES) * LANES
    pair_total = micros * heads
    pairs = -(-pair_total // seq_count)
    padded_pairs = pairs * seq_count
    tail_length = tail_keys.shape[1]

    x = inputs.reshape(total, width)
    dy = cotangent.reshape(total, width)

    small = jnp.concatenate([w_forget, gain_one[:, None], gain_two[:, None]], axis=1)
    first_shard = jnp.concatenate(
        [pad_to(w, cols, 1) for w in (w_query, w_key, w_value, w_outgate)]
        + [pad_to(small, LANES, 1)],
        axis=1,
    )
    first = lax.all_gather(first_shard, "seq", axis=0, tiled=True)
    near_shard = jnp.concatenate([w_gate, w_up, w_down.T], axis=1)
    near = lax.all_gather(near_shard, "seq", axis=0, tiled=True)
    split = 3 * ff // 2
    outs, units, early = [pad_to(w_out.T, cols, 1)], [(near_shard[:, :split], near_shard[:, split:])], []
    flip = 1
    while flip < head_count:
        outs.append(exchanged(jnp.concatenate(outs, axis=1), "head", flip))
        if flip == 1:
            early.append(outs[-1])
        else:
            units += [tuple(exchanged(part, "head", flip) for part in unit) for unit in units]
        flip *= 2
    far_parts = outs + [part for unit in units[1:] for part in unit]
    rank = head_rank.astype(jnp.int32)[None]
    upper = (rank >= head_count // 2).astype(jnp.int32)
    order = Order()
    gain_one_row = first[:, 4 * cols + heads].astype(F32)[None, :]
    gain_two_row = first[:, 4 * cols + heads + 1].astype(F32)[None, :]
    bias_here = lax.dynamic_slice_in_dim(forget_bias, head_rank * heads, heads, 0)
    bias_row = pad_to(bias_here[None, :], LANES, 1)
    gq_row = jnp.tile(query_gain.astype(F32), 2)[None, :]
    gk_row = jnp.tile(key_gain.astype(F32), 2)[None, :]

    tail_key_parts, tail_value_parts = [], []
    for j in range(pairs):
        p = jnp.minimum(j * seq_count + seq_rank, pair_total - 1)
        m, h = p // heads, p % heads
        tail_of = lambda array, wide: lax.dynamic_slice(
            array, (m, 0, h * wide), (1, tail_length, wide)
        )[0]
        forget = tail_of(tail_forget, 1)
        decay = jnp.cumsum(forget, axis=0) - jnp.sum(forget, axis=0, keepdims=True)
        high = lax.reduce_precision(decay, 8, 7)
        middle = lax.reduce_precision(decay - high, 8, 7)
        least = decay - high - middle
        ones = jnp.ones((tail_length, 3), BF16)
        parts = jnp.concatenate([-high, -middle, -least], axis=1).astype(BF16)
        tail_key_parts.append(
            pad_to(jnp.concatenate([tail_of(tail_keys, HEAD_SIZE), ones, parts], axis=1), LANES, 1)
        )
        tail_value_parts.append(
            pad_to(jnp.concatenate([tail_of(tail_values, HEAD_SIZE), ones], axis=1), LANES, 1)
        )
    tail_key, tail_value = jnp.stack(tail_key_parts), jnp.stack(tail_value_parts)

    def pairs_of(stages, first_micro, count):
        low, high = first_micro * heads, (first_micro + count) * heads
        taken = []
        for j, stage in enumerate(stages):
            start, stop = max(low - j * seq_count, 0), min(high - j * seq_count, seq_count)
            if start < stop:
                taken.append(stage[start:stop, 0])
        return jnp.concatenate(taken, axis=0)

    a, raw, gl, *pays = project(
        order, heads, cols, seq_count, x, first, bias_row, gain_one_row, gq_row, gk_row, micros, early
    )
    pays = [to_all(pay, "seq") for pay in pays]
    far = lax.all_gather(pack(order, far_parts), "seq", axis=0, tiled=True)
    kept, returned = [], []
    at = 0
    for pay in pays:
        packed, *saved = attend(order, pay, tail_key, tail_value, at)
        kept += [(saved, pay, place) for place in range(pay.shape[1])]
        returned.append(to_all(packed, "seq"))
        at = len(kept)
    packed = jnp.concatenate(returned, axis=1)

    size = 2 if micros % 2 == 0 else 1
    groups = micros // size
    chunk = min(512, ff)
    gated, o_alls = (), []
    for g in range(groups):
        enough = (g + 1) * size * heads <= (pairs - 1) * seq_count
        *gated, sent = gate(
            order, heads, returned[0] if enough else packed, gl, rows, g * size, size, head_count, gated
        )
        o_alls.append(to_all(sent, "head"))
    o = gated[0]

    hiddens, out_parts, dc_parts, dc_others = [], [], [], []
    dhs, gains_two = [], []
    late = ()
    early_places = size * heads // seq_count if groups > 1 else 0
    fed, backed = (), ()

    def back_to_heads(g):
        nonlocal backed, late
        places = [(early_places, pairs)]
        if g == 0 and early_places > 0:
            places = [(0, early_places)] + places
        dhb, dgl, dh, gain, *sent, out_parts[g] = hidden_back(
            order,
            heads,
            dc_parts[g],
            dc_others[g],
            hiddens[g],
            dy,
            gain_two_row,
            far,
            gl,
            packed,
            rows,
            g * size,
            places,
            late,
            backed,
            (out_parts[g],),
        )
        backed, late = (dhb, dgl), (sent[-1],)
        dhs.append(dh)
        gains_two.append(gain)
        return sent[0]

    def scattered(grad):
        return lax.psum_scatter(grad, "seq", scatter_dimension=0, tiled=True)

    for g in range(groups):
        *fed, hidden, out_part, dc_part = feed(
            order, rank, x, dy, o_alls[g], near, far, gain_two_row, ff, chunk, g, fed
        )
        hiddens.append(hidden)
        out_parts.append(out_part)
        dc_parts.append(dc_part)
        dc_others.append(exchanged(dc_part, "head", 1))
        if g > 0:
            early_grads = back_to_heads(g - 1)
    c, u, dgu = fed
    unit_grads = scattered(turned_products(order, [(c, dgu), (dy, u)], 13))

    layer_out = ()

    def put_out(g, after=()):
        nonlocal layer_out
        other = exchanged(out_parts[g], "head", 1)
        layer_out = layer_output(order, hiddens[g], out_parts[g], other, g, total, layer_out, after)

    if early_places > 0:
        early_grads = to_all(early_grads, "seq")
    returned = []
    mixed = ()
    for j in range(pairs):
        if j == early_places:
            back_to_heads(groups - 1)
            mixed = (turned_products(order, [(backed[0], o), (a, backed[1])], 8),)
            late_grads = to_all(late[0], "seq")
        sent = (early_grads, j) if j < early_places else (late_grads, j - early_places)
        saved, pay, place = kept[j]
        waited = tuple(returned[: j - 1]) if j >= 2 else ()
        grad, *mixed = attend_back(
            order, saved[1:], tail_key, tail_value, saved[0], sent[0], pay, j, place, sent[1], mixed, waited
        )
        returned.append(to_all(grad, "seq"))

    put_out(0, tuple(returned[:-1]))

    grads, da_sums, gains_one = (), [], []
    for g in range(groups):
        last = g == groups - 1
        results = project_back(
            order,
            heads,
            upper,
            pairs_of(returned, g * size, size),
            raw,
            x,
            backed[1],
            first,
            gq_row,
            gk_row,
            rows,
            g * size,
            size,
            last,
            grads,
            (unit_grads,) if g == 0 else (),
            mixed,
        )
        count = 2 if last else 1
        grads, da, gain, mixed = results[:1], results[1 : 1 + count], results[1 + count], results[2 + count :]
        gains_one.append(gain)
        if last:
            da_sums += [(line_sum(da[0][i], da[1][i], "head"), 0) for i in range(size)]
        else:
            total_da = lax.psum(da[0], "head")
            da_sums += [([total_da], i) for i in range(size)]
        if g == 0:
            mixed_grads = scattered(mixed[0])
            mixed = ()
            for out in range(1, groups):
                put_out(out)

    one_sums = jnp.sum(jnp.concatenate(gains_one, axis=0), axis=0)
    two_sums = jnp.sum(jnp.concatenate(gains_two, axis=0), axis=0) * (1.0 / head_count)
    own_rows = gain_one.shape[0]
    shared = pad_to(one_sums[:, width:], 3 * LANES, 1)
    owned_sums = jnp.concatenate(
        [
            one_sums[:, :width].reshape(seq_count, own_rows),
            two_sums.reshape(seq_count, own_rows),
            jnp.broadcast_to(shared, (seq_count, 3 * LANES)),
        ],
        axis=1,
    ).astype(BF16)
    owned_sums = jnp.pad(owned_sums[:, None], ((0, 0), (0, 15), (0, grads[0].shape[1] - owned_sums.shape[1])))
    head_grads = owned_product(order, a, grads[0], owned_sums, 9)

    head_grads = jnp.sum(to_all(head_grads, "seq").astype(F32), axis=0)
    sums = head_grads[own_rows : own_rows + 1]
    head_grads = head_grads[:own_rows]
    unit_grads, mixed_grads = unit_grads.astype(F32), mixed_grads.astype(F32)
    strips = [unit_grads[:, i * chunk : (i + 1) * chunk] for i in range(2 * ff // chunk)]
    grad_gate = jnp.concatenate(strips[0::2], axis=1)
    grad_up = jnp.concatenate(strips[1::2], axis=1)
    grad_down = unit_grads[:, 2 * ff :].T
    grad_out = mixed_grads[:, :own_cols].T

    gain_lanes = 2 * own_rows
    bias_at = gain_lanes + 2 * LANES
    bias_full = lax.dynamic_update_slice(
        jnp.zeros((1, forget_bias.shape[0]), F32), sums[:, bias_at : bias_at + heads], (0, head_rank * heads)
    )
    sums = small_sum(jnp.concatenate([sums[:, :bias_at], bias_full], axis=1), "head")[0]
    halves = sums[gain_lanes:bias_at].reshape(4, HEAD_SIZE)
    gq_total, gk_total = halves[0] + halves[1], halves[2] + halves[3]
    bias_total = sums[bias_at:]

    input_grad = ()
    for m in range(micros):
        summed, place = da_sums[m]
        input_grad = input_back(
            order, rank, summed, place, x, dhs[m // size], m % size, gain_one_row, rows, m, input_grad, ()
        )

    input_grad, layer_out = input_grad[0], layer_out[0]
    shape = inputs.shape
    return (
        layer_out.reshape(shape),
        input_grad.reshape(shape),
        sums[:own_rows],
        sums[own_rows:gain_lanes],
        head_grads[:, :own_cols],
        head_grads[:, cols : cols + own_cols],
        head_grads[:, 2 * cols : 2 * cols + own_cols],
        head_grads[:, 3 * cols : 3 * cols + heads],
        bias_total,
        gq_total,
        gk_total,
        mixed_grads[:, cols : cols + own_cols],
        grad_out,
        grad_gate,
        grad_up,
        grad_down,
    )


def solution(mesh):
    by_rows = P("seq", "head")
    by_cols = P("head", "seq")
    placed = (
        P(None, "seq", None),
        P(None, "seq", None),
        P(None, None, "head"),
        P(None, None, "head"),
        P(None, None, "head"),
        P("seq"),
        P("seq"),
        by_rows,
        by_rows,
        by_rows,
        by_rows,
        P(),
        P(),
        P(),
        by_rows,
        by_cols,
        by_rows,
        by_rows,
        by_cols,
    )
    return jax.shard_map(
        shards,
        mesh=mesh,
        in_specs=placed,
        out_specs=(
            P(None, "seq", None),
            P(None, "seq", None),
            P("seq"),
            P("seq"),
            by_rows,
            by_rows,
            by_rows,
            by_rows,
            P(),
            P(),
            P(),
            by_rows,
            by_cols,
            by_rows,
            by_rows,
            by_cols,
        ),
        check_vma=False,
    )
```

```python
import functools

import jax
import jax.numpy as jnp
from jax import lax
from jax.experimental import pallas as pl
from jax.experimental.pallas import tpu as pltpu
from jax.sharding import PartitionSpec as P

HEAD_SIZE = 64
LANES = 128
EPSILON = 1e-06
F32 = jnp.float32
BF16 = jnp.bfloat16
NN = (((1,), (0,)), ((), ()))
NT = (((1,), (1,)), ((), ()))
HIDE = -1e30
SCALE = HEAD_SIZE**-0.5
STRIP = 64
MIB = 1024 * 1024


def dot(left, right, dims=NN):
    return lax.dot_general(left, right, dims, preferred_element_type=F32)


def params():
    return pltpu.CompilerParams(vmem_limit_bytes=60 * MIB)


def linked(kernel, inputs, extra, outputs, carried):
    def body(*refs):
        first = inputs + extra
        token = refs[first + outputs + carried]
        token[...] = jnp.zeros_like(token)
        kernel(*refs[:inputs], *refs[first : first + outputs], *refs[first + outputs + carried + 1 :])

    return body


class Order:
    def __init__(self):
        self.tokens = []

    def call(
        self, kernel, name, grid, ins, outs, us, scratch=(), before=(), scalars=(), after=(), carry=()
    ):
        arrays = list(scalars) + [array for array, _ in ins]
        extra = list(before) + list(carry) + list(after) + self.tokens
        count = len(arrays)
        whole = lambda *at: (0, 0)
        anywhere = pl.BlockSpec(memory_space=pl.ANY)
        out_specs = [spec for _, _, spec in outs] + [anywhere] * len(carry)
        out_specs.append(pl.BlockSpec((8, LANES), whole))
        out_shape = [jax.ShapeDtypeStruct(shape, kind) for shape, kind, _ in outs]
        out_shape += [jax.ShapeDtypeStruct(array.shape, array.dtype) for array in carry]
        out_shape.append(jax.ShapeDtypeStruct((8, LANES), F32))
        aliases = {count + i: i for i in range(len(before))}
        for i in range(len(carry)):
            aliases[count + len(before) + i] = len(outs) + i
        *results, token = pl.pallas_call(
            linked(kernel, count, len(extra), len(outs), len(carry)),
            grid_spec=pltpu.PrefetchScalarGridSpec(
                num_scalar_prefetch=len(scalars),
                grid=grid,
                in_specs=[spec for _, spec in ins] + [anywhere] * len(extra),
                out_specs=out_specs,
                scratch_shapes=list(scratch),
            ),
            out_shape=out_shape,
            input_output_aliases=aliases,
            compiler_params=params(),
            cost_estimate=pl.CostEstimate(flops=int(us * 8e9), bytes_accessed=0, transcendentals=0),
            name=name,
        )(*arrays, *extra)
        self.tokens = [token]
        return results


def lanes_of(rows):
    return lax.broadcasted_iota(jnp.int32, (rows, LANES), 1)


def swap_halves(block):
    return pltpu.roll(block, HEAD_SIZE, 1)


def in_three(value):
    high = value.astype(BF16).astype(F32)
    rest = value - high
    middle = rest.astype(BF16).astype(F32)
    return high, middle, rest - middle


def at_lanes(lane, first, parts, base):
    for place, part in enumerate(parts):
        base = jnp.where(lane == first + place, part, base)
    return base


def triangle(rows, lower):
    down = lax.broadcasted_iota(jnp.int32, (rows, rows), 0)
    across = lax.broadcasted_iota(jnp.int32, (rows, rows), 1)
    return jnp.where(down >= across if lower else down <= across, 1.0, 0.0).astype(BF16)


def running_sum(tri, column, lane):
    spread = at_lanes(lane, 0, in_three(column), jnp.zeros(lane.shape, F32))
    sums = dot(tri, spread.astype(BF16))
    return sums[:, 0:1] + sums[:, 1:2] + sums[:, 2:3]


def forget_column(tail_block):
    return tail_block[:, 64:65] + tail_block[:, 65:66] + tail_block[:, 66:67]


def per_head(low, values):
    first = jnp.sum(jnp.where(low, values, 0.0), axis=-1, keepdims=True)
    second = jnp.sum(jnp.where(low, 0.0, values), axis=-1, keepdims=True)
    return jnp.where(low, first, second) * (1.0 / HEAD_SIZE)


def rms_factor(values):
    return lax.rsqrt(jnp.mean(values * values, axis=-1, keepdims=True) + EPSILON)


def merge_pair(low, first, second):
    return jnp.where(low, first, swap_halves(second))


def merge_swapped(low, first, second):
    return jnp.where(low, swap_halves(first), second)


def put_pair(refs, pair, block, column=0, start=0):
    owners = refs[0].shape[0]
    owner, place = lax.rem(pair, owners), lax.div(pair, owners)
    width = block.shape[1]
    for ref in refs:
        stop = start + ref.shape[1]

        @pl.when((place >= start) & (place < stop))
        def _(ref=ref, start=start):
            ref[owner, place - start, :, column : column + width] = block

        start = stop


def unpack_rows(low_half, first, second):
    strip = low_half.shape[0]
    rows = []
    for at in range(0, first.shape[0], strip):
        one, two = first[at : at + strip], second[at : at + strip]
        rows.append(jnp.where(low_half, one, swap_halves(two)))
        rows.append(jnp.where(low_half, swap_halves(one), two))
    return jnp.concatenate(rows, axis=0)


def pack_rows(low_half, block):
    strip = low_half.shape[0]
    first, second = [], []
    for at in range(0, block.shape[0], 2 * strip):
        top, bottom = block[at : at + strip], block[at + strip : at + 2 * strip]
        first.append(jnp.where(low_half, top, swap_halves(bottom)))
        second.append(jnp.where(low_half, swap_halves(top), bottom))
    return jnp.concatenate(first, axis=0), jnp.concatenate(second, axis=0)


def project_kernel(
    heads, idle, x_ref, w_ref, bias_ref, gain_ref, gq_ref, gk_ref, a_ref, raw_ref, gl_ref, *pay_refs
):
    x = x_ref[...].astype(F32)
    rows = x.shape[0]
    cols = gl_ref.shape[1]
    a = (x * rms_factor(x) * gain_ref[...]).astype(BF16)
    a_ref[...] = a
    proj = dot(a, w_ref[...])
    raw_ref[...] = proj[:, : 2 * cols]
    gl_ref[...] = proj[:, 3 * cols : 4 * cols]
    logit = proj[:, 4 * cols :] + bias_ref[...]
    lane = lanes_of(rows)
    low = lane < HEAD_SIZE
    for group in range(cols // LANES):
        at = group * LANES
        query = proj[:, at : at + LANES]
        key = proj[:, cols + at : cols + at + LANES]
        value = proj[:, 2 * cols + at : 2 * cols + at + LANES]
        query = query * lax.rsqrt(per_head(low, query * query) + EPSILON) * gq_ref[...]
        key = key * lax.rsqrt(per_head(low, key * key) + EPSILON) * gk_ref[...]
        for half in range(2):
            head = 2 * group + half
            if head >= heads:
                continue
            zl = at_lanes(lane, 64, in_three(logit[:, head : head + 1]), jnp.zeros(lane.shape, F32))
            if half == 0:
                both = merge_pair(low, query, key)
                rest = jnp.where(low, value, zl)
            else:
                both = merge_swapped(low, query, key)
                rest = jnp.where(low, swap_halves(value), zl)
            pair = pl.program_id(0) * heads + head
            put_pair(pay_refs, pair, both.astype(BF16))
            put_pair(pay_refs, pair, rest.astype(BF16), LANES)

    @pl.when(pl.program_id(0) == 0)
    def _():
        for pair in idle:
            put_pair(pay_refs, pair, jnp.zeros((rows, 2 * LANES), BF16))


def project(order, heads, cols, owners, x, weights, bias_row, gain_row, gq_row, gk_row, micros, after):
    total, width = x.shape
    rows = total // micros
    wide = weights.shape[1]
    whole = lambda m: (0, 0)
    part = lambda m: (m, 0)
    row = pl.BlockSpec((1, LANES), whole)
    pairs = -(-micros * heads // owners)
    idle = range(micros * heads, pairs * owners)
    parts = [1] * pairs
    sent = [(owners, part, rows, 2 * LANES) for part in parts]
    return order.call(
        functools.partial(project_kernel, heads, idle),
        "project",
        (micros,),
        [
            (x, pl.BlockSpec((rows, width), part)),
            (weights, pl.BlockSpec((width, wide), whole)),
            (bias_row, row),
            (gain_row, pl.BlockSpec((1, width), whole)),
            (gq_row, row),
            (gk_row, row),
        ],
        [
            ((total, width), BF16, pl.BlockSpec((rows, width), part)),
            ((total, 2 * cols), F32, pl.BlockSpec((rows, 2 * cols), part)),
            ((total, cols), F32, pl.BlockSpec((rows, cols), part)),
        ]
        + [(shape, BF16, pl.BlockSpec(shape, lambda m: (0, 0, 0, 0))) for shape in sent],
        13,
        after=after,
    )


def attend_kernel(size, pay_ref, tk_ref, tv_ref, ap_ref, af_ref, q_ref, k_ref, v_ref):
    blocks, _, rows, _ = pay_ref.shape
    length = blocks * rows
    lane = lanes_of(rows)
    low = lane < HEAD_SIZE
    tri = triangle(rows, True)
    zero = jnp.zeros(lane.shape, F32)

    def build(b, carry):
        at = pl.ds(pl.multiple_of(b * rows, rows), rows)
        both = pay_ref[b, 0, :, :LANES].astype(F32)
        rest = pay_ref[b, 0, :, LANES:].astype(F32)
        logit = forget_column(rest)
        log_forget = jnp.minimum(logit, 0.0) - jnp.log1p(jnp.exp(-jnp.abs(logit)))
        decay = running_sum(tri, log_forget, lane) + carry
        high, middle, least = in_three(decay)
        query_side = at_lanes(lane, 64, (high, middle, least, 1.0, 1.0, 1.0), zero)
        key_side = at_lanes(lane, 64, (1.0, 1.0, 1.0, -high, -middle, -least), zero)
        value_side = at_lanes(lane, 64, (1.0, 1.0, 1.0), zero)
        q_ref[0, at, :] = jnp.where(low, both * SCALE, query_side).astype(BF16)
        k_ref[0, at, :] = jnp.where(low, swap_halves(both), key_side).astype(BF16)
        v_ref[0, at, :] = jnp.where(low, rest, value_side).astype(BF16)
        return decay[rows - 1 :, :]

    lax.fori_loop(0, blocks, build, jnp.zeros((1, 1), F32))

    tail_length = tk_ref.shape[1]
    visible = lax.broadcasted_iota(jnp.int32, (size, size), 0) >= lax.broadcasted_iota(
        jnp.int32, (size, size), 1
    )
    half_low = lanes_of(STRIP) < HEAD_SIZE
    lane_here = lanes_of(size)

    def one_block(qi):
        at = pl.ds(qi * size, size)
        query = q_ref[0, at, :]

        def absorb(key, value, total, masked=False):
            scores = dot(query, key, NT)
            if masked:
                scores = jnp.where(visible, scores, HIDE)
            return total + dot(jnp.exp(scores).astype(BF16), value)

        total = jnp.zeros((size, LANES), F32)
        for t in range(tail_length // size):
            here = pl.ds(t * size, size)
            total = absorb(tk_ref[0, here, :], tv_ref[0, here, :], total)

        for ki in range(qi):
            here = pl.ds(ki * size, size)
            total = absorb(k_ref[0, here, :], v_ref[0, here, :], total)
        total = absorb(k_ref[0, at, :], v_ref[0, at, :], total, True)
        weight = total[:, 64:65]
        mixture = total / weight
        af_ref[0, at, :] = mixture
        for piece in range(size // rows):
            block = mixture[piece * rows : (piece + 1) * rows]
            packed, _ = pack_rows(half_low, block)
            ap_ref[qi * (size // rows) + piece, 0] = packed.astype(BF16)
        old = query.astype(F32)
        shifted = forget_column(old) - jnp.log(weight)
        q_ref[0, at, :] = at_lanes(lane_here, 64, in_three(shifted), old).astype(BF16)

    for qi in range(length // size):
        one_block(qi)


def attend(order, pay, tail_key, tail_value, first, out_places, out_place, before):
    blocks, pairs, rows, _ = pay.shape
    length = blocks * rows
    tail_length = tail_key.shape[1]
    size = min(512, length)
    pair = lambda j: (j, 0, 0)
    across = lambda j: (0, j, 0, 0)
    tail = pl.BlockSpec((1, tail_length, LANES), lambda j: (first + j, 0, 0))
    whole = pl.BlockSpec((1, length, LANES), pair)
    return order.call(
        functools.partial(attend_kernel, size),
        "attend",
        (pairs,),
        [
            (pay, pl.BlockSpec((blocks, 1, rows, 2 * LANES), across)),
            (tail_key, tail),
            (tail_value, tail),
        ],
        [
            (
                (blocks, out_places, rows // 2, LANES),
                BF16,
                pl.BlockSpec((blocks, 1, rows // 2, LANES), lambda j: (0, out_place, 0, 0)),
            ),
            ((pairs, length, LANES), F32, whole),
            ((pairs, length, LANES), BF16, whole),
            ((pairs, length, LANES), BF16, whole),
            ((pairs, length, LANES), BF16, whole),
        ],
        14 * pairs,
        before=before,
    )


def attend_back_kernel(
    size,
    q_ref,
    k_ref,
    v_ref,
    tk_ref,
    tv_ref,
    af_ref,
    dap_ref,
    rest_ref,
    g_ref,
    da_ref,
    dqt_ref,
    sums_ref,
):
    blocks, _, rows, _ = rest_ref.shape
    length = blocks * rows
    lane = lanes_of(rows)
    low = lane < HEAD_SIZE
    zero = jnp.zeros(lane.shape, F32)

    def build(b, carry):
        at = pl.ds(pl.multiple_of(b * rows, rows), rows)
        packed = dap_ref[b, 0].astype(F32)
        strips = []
        for strip in range(0, packed.shape[0], STRIP):
            strips += [packed[strip : strip + STRIP], swap_halves(packed[strip : strip + STRIP])]
        grad = jnp.where(low, jnp.concatenate(strips, axis=0), 0.0)
        delta = jnp.sum(grad * af_ref[0, at, :], axis=-1, keepdims=True)
        da_ref[at, :] = at_lanes(lane, 64, in_three(-delta), grad).astype(BF16)
        return carry

    lax.fori_loop(0, blocks, build, 0)

    across = lax.broadcasted_iota(jnp.int32, (size, size), 1)
    down = lax.broadcasted_iota(jnp.int32, (size, size), 0)
    visible = across >= down
    count = length // size

    def block_at(i):
        return pl.ds(i * size, size)

    def pieces(key, value, at, masked=False):
        scores = dot(key, q_ref[0, at, :], NT)
        if masked:
            scores = jnp.where(visible, scores, HIDE)
        prob = jnp.exp(scores)
        score_grad = prob * dot(value, da_ref[at, :], NT)
        return prob.astype(BF16), score_grad.astype(BF16)

    tail_length = tk_ref.shape[1]
    tail_count = tail_length // size

    for qi in range(count):
        at = block_at(qi)
        total = jnp.zeros((LANES, size), F32)
        for t in range(tail_count):
            key = tk_ref[0, pl.ds(t * size, size), :]
            _, score_grad = pieces(key, tv_ref[0, pl.ds(t * size, size), :], at)
            total = total + dot(key.T, score_grad)
        dqt_ref[:, at] = total

    lane_here = lanes_of(size)
    low_here = lane_here < HEAD_SIZE

    for ki in range(count):
        own = block_at(ki)
        key = k_ref[0, own, :]
        value = v_ref[0, own, :]
        key_turned = key.T

        def one(at, sums, masked=False, key=key, value=value, key_turned=key_turned):
            key_sum, value_sum = sums
            prob, score_grad = pieces(key, value, at, masked)
            dqt_ref[:, at] += dot(key_turned, score_grad)
            return (
                key_sum + dot(score_grad, q_ref[0, at, :]),
                value_sum + dot(prob, da_ref[at, :]),
            )

        start = (jnp.zeros((size, LANES), F32), jnp.zeros((size, LANES), F32))
        sums = one(own, start, True)
        for qi in range(ki + 1, count):
            sums = one(block_at(qi), sums)
        key_sum, value_sum = sums
        sums_ref[own, :] = key_sum
        for piece in range(size // rows):
            here = slice(piece * rows, (piece + 1) * rows)
            g_ref[ki * (size // rows) + piece, 0, :, LANES:] = value_sum[here].astype(BF16)

    tri = triangle(rows, False)

    def finish(i, carry):
        b = blocks - 1 - i
        at = pl.ds(pl.multiple_of(b * rows, rows), rows)
        query = dqt_ref[:, at].T
        key = sums_ref[at, :]
        decay_grad = query[:, 64:65] - key[:, 67:68]
        suffix = running_sum(tri, decay_grad, lane) + carry
        logit = forget_column(rest_ref[b, 0].astype(F32))
        forget_grad = suffix / (1.0 + jnp.exp(logit))
        both = jnp.where(low, query * SCALE, swap_halves(key))
        rest = jnp.where(low, g_ref[b, 0, :, LANES:].astype(F32), jnp.where(lane == 64, forget_grad, 0.0))
        g_ref[b, 0, :, :LANES] = both.astype(BF16)
        g_ref[b, 0, :, LANES:] = rest.astype(BF16)
        return suffix[0:1, :]

    lax.fori_loop(0, blocks, finish, jnp.zeros((1, 1), F32))


def attend_back(
    order, saved, tail_key, tail_value, mixture, packed_grad, pay, place, saved_place, grad_place, out_places, out_place, before, carry, after
):
    blocks, _, rows, _ = pay.shape
    length = blocks * rows
    tail_length = tail_key.shape[1]
    size = min(512, length)
    pair = lambda j: (place, 0, 0)
    tail = pl.BlockSpec((1, tail_length, LANES), pair)
    whole = pl.BlockSpec((1, length, LANES), lambda j: (saved_place, 0, 0))
    grad = pl.BlockSpec((blocks, 1, rows // 2, LANES), lambda j: (0, grad_place, 0, 0))
    sent = (blocks, out_places, rows, 2 * LANES)
    out = pl.BlockSpec((blocks, 1, rows, 2 * LANES), lambda j: (0, out_place, 0, 0))
    return order.call(
        functools.partial(attend_back_kernel, size),
        "attend_back",
        (1,),
        [(array, whole) for array in saved]
        + [
            (tail_key, tail),
            (tail_value, tail),
            (mixture, whole),
            (packed_grad, grad),
            (pay, pl.BlockSpec((blocks, 1, rows, LANES), lambda j: (0, saved_place, 0, 1))),
        ],
        [(sent, BF16, out)],
        22,
        scratch=[
            pltpu.VMEM((length, LANES), BF16),
            pltpu.VMEM((LANES, length), F32),
            pltpu.VMEM((length, LANES), F32),
        ],
        before=before,
        carry=carry,
        after=after,
    )


def take_pair(refs, pair):
    owners = refs[0].shape[0]
    owner, place = lax.rem(pair, owners), lax.div(pair, owners)
    block, start = None, 0
    for ref in refs:
        here = ref[owner, jnp.clip(place - start, 0, ref.shape[1] - 1)]
        block = here if block is None else jnp.where(place >= start, here, block)
        start += ref.shape[1]
    return block


def group_of(heads, ref, first_pair, group, low_half):
    owners = ref.shape[0]

    def packed(head):
        if head >= heads:
            return jnp.zeros(ref.shape[2:], F32)
        pair = first_pair + head
        if isinstance(pair, int):
            return ref[pair % owners, pair // owners].astype(F32)
        return ref[lax.rem(pair, owners), lax.div(pair, owners)].astype(F32)

    return unpack_rows(low_half, packed(2 * group), packed(2 * group + 1))


def gate_kernel(heads, first, ap_ref, gl_ref, o_ref, sent_ref):
    rows, cols = o_ref.shape
    half_low = lanes_of(STRIP) < HEAD_SIZE
    pair = (first + pl.program_id(0)) * heads
    for group in range(cols // LANES):
        at = slice(group * LANES, (group + 1) * LANES)
        mixture = group_of(heads, ap_ref, pair, group, half_low)
        gated = (mixture * jax.nn.sigmoid(gl_ref[:, at])).astype(BF16)
        o_ref[:, at] = gated
        for z in range(sent_ref.shape[0]):
            sent_ref[z, :, at] = gated


def gate(order, heads, packed, gl, rows, first, count, copies, before):
    total, cols = gl.shape
    here = pl.BlockSpec((rows, cols), lambda i: (first + i, 0))
    return order.call(
        functools.partial(gate_kernel, heads, first),
        "gate",
        (count,),
        [(packed, pl.BlockSpec(packed.shape, lambda i: (0, 0, 0, 0))), (gl, here)],
        [
            ((total, cols), BF16, here),
            (
                (copies, count * rows, cols),
                BF16,
                pl.BlockSpec((copies, rows, cols), lambda i: (0, i, 0)),
            ),
        ],
        2 * count,
        before=before,
    )


def pack_kernel(*refs):
    out_ref, at = refs[-1], 0
    for ref in refs[:-1]:
        wide = ref.shape[1]
        out_ref[:, at : at + wide] = ref[...]
        at += wide


def pack(order, arrays):
    rows = arrays[0].shape[0]
    wide = sum(array.shape[1] for array in arrays)
    whole = lambda i: (0, 0)
    return order.call(
        pack_kernel,
        "pack",
        (1,),
        [(array, pl.BlockSpec(array.shape, whole)) for array in arrays],
        [((rows, wide), BF16, pl.BlockSpec((rows, wide), whole))],
        2,
    )[0]


def feed_kernel(
    parts,
    own,
    rank_ref,
    x_ref,
    dy_ref,
    wo_ref,
    wg_ref,
    wu_ref,
    wd_ref,
    wg_far_ref,
    wu_far_ref,
    wd_far_ref,
    gain_ref,
    *refs,
):
    o_ref, c_ref, u_ref, dgu_ref, hid_ref, out_ref, dc_ref, out_acc, dc_acc = refs
    step = pl.program_id(0)
    last = pl.num_programs(0) - 1

    def attended():
        return dot(o_ref[0], wo_ref[...], NT)

    @pl.when(step == 0)
    def _():
        hid_ref[...] = x_ref[...].astype(F32) + attended()

    @pl.when((step > 0) & (step < parts))
    def _():
        hid_ref[...] += attended()

    @pl.when(step == parts - 1)
    def _():
        hidden = hid_ref[...]
        c_ref[...] = (hidden * rms_factor(hidden) * gain_ref[...]).astype(BF16)
        out_acc[...] = jnp.zeros_like(out_acc)
        dc_acc[...] = jnp.zeros_like(dc_acc)

    def chunk(w_gate, w_up, w_down):
        c = c_ref[...]
        gr = dot(c, w_gate[...])
        ur = dot(c, w_up[...])
        sig = jax.nn.sigmoid(gr)
        silu = gr * sig
        u = (silu * ur).astype(BF16)
        du = dot(dy_ref[...], w_down[...])
        dgr = (du * ur * sig * (1.0 + gr * (1.0 - sig))).astype(BF16)
        dur = (du * silu).astype(BF16)
        out_acc[...] += dot(u, w_down[...], NT)
        dc_acc[...] += dot(dgr, w_gate[...], NT) + dot(dur, w_up[...], NT)
        return u, dgr, dur

    @pl.when((step >= parts) & (step < parts + own))
    def _():
        u, dgr, dur = chunk(wg_ref, wu_ref, wd_ref)
        wide = u.shape[1]
        u_ref[...] = u
        dgu_ref[:, :wide] = dgr
        dgu_ref[:, wide:] = dur

    @pl.when(step >= parts + own)
    def _():
        chunk(wg_far_ref, wu_far_ref, wd_far_ref)

    @pl.when(step == last)
    def _():
        out_ref[...] = out_acc[...].astype(BF16)
        dc_ref[...] = dc_acc[...].astype(BF16)


def feed(order, rank, x, dy, o_all, near, far, gain_row, ff, chunk, group, before):
    parts, rows, cols = o_all.shape
    total, width = x.shape
    own = ff // chunk
    offset = parts * cols // chunk
    others = (far.shape[1] - parts * cols) // (3 * ff)
    steps = parts + (1 + others) * own
    whole = lambda i, rank: (0, 0)
    here = lambda i, rank: (group, 0)
    early = lambda i: jnp.minimum(i, parts - 1)
    mine = lambda i: jnp.clip(i - parts, 0, own - 1)

    def near_strip(k):
        return pl.BlockSpec((width, chunk), lambda i, rank: (0, k * own + mine(i)))

    def far_strip(k):
        def place(i, rank):
            s = jnp.maximum(i - parts - own, 0)
            return (0, offset + (s // own * 3 + k) * own + s % own)

        return pl.BlockSpec((width, chunk), place)

    wide = pl.BlockSpec((rows, width), whole)
    return order.call(
        functools.partial(feed_kernel, parts, own),
        "feed",
        (steps,),
        [
            (x, pl.BlockSpec((rows, width), here)),
            (dy, pl.BlockSpec((rows, width), here)),
            (far, pl.BlockSpec((width, cols), lambda i, rank: (0, early(i)))),
            (near, near_strip(0)),
            (near, near_strip(1)),
            (near, near_strip(2)),
            (far, far_strip(0)),
            (far, far_strip(1)),
            (far, far_strip(2)),
            (gain_row, pl.BlockSpec((1, width), whole)),
        ]
        + [(o_all, pl.BlockSpec((1, rows, cols), lambda i, rank: (rank[0] ^ early(i), 0, 0)))],
        [
            ((total, width), BF16, pl.BlockSpec((rows, width), here)),
            ((total, ff), BF16, pl.BlockSpec((rows, chunk), lambda i, rank: (group, mine(i)))),
            (
                (total, 2 * ff),
                BF16,
                pl.BlockSpec((rows, 2 * chunk), lambda i, rank: (group, mine(i))),
            ),
            ((rows, width), F32, wide),
            ((rows, width), BF16, wide),
            ((rows, width), BF16, wide),
        ],
        37,
        scratch=[pltpu.VMEM((rows, width), F32), pltpu.VMEM((rows, width), F32)],
        before=before,
        scalars=(rank,),
    )


def norm_back(source, factor, gain_row, upstream):
    scaled = upstream * gain_row
    inner = jnp.mean(scaled * source, axis=-1, keepdims=True)
    return factor * scaled - source * (factor * factor * factor) * inner


def hidden_back_kernel(
    heads,
    first,
    start,
    with_old,
    dc_ref,
    dc_other_ref,
    hid_ref,
    dy_ref,
    gain_ref,
    w_ref,
    gl_ref,
    ap_ref,
    *refs,
):
    if with_old:
        old_ref, *refs = refs
    dhb_ref, dgl_ref, dh_ref, dg_ref, *dap_refs = refs
    rows, cols = gl_ref.shape
    pair = (first + pl.program_id(0)) * heads
    if with_old:

        @pl.when(pl.program_id(0) == 0)
        def _():
            dap_refs[0][...] = old_ref[...]

    hidden = hid_ref[...]
    factor = rms_factor(hidden)
    dc = dc_ref[...].astype(F32) + dc_other_ref[...].astype(F32)
    dh = dy_ref[...].astype(F32) + norm_back(hidden, factor, gain_ref[...], dc)
    dg_ref[0] = jnp.sum(dc * hidden * factor, axis=0, keepdims=True)
    dh_ref[...] = dh
    dhb = dh.astype(BF16)
    dhb_ref[...] = dhb
    gated_grad = dot(dhb, w_ref[...])
    half_low = lanes_of(STRIP) < HEAD_SIZE
    for group in range(cols // LANES):
        at = slice(group * LANES, (group + 1) * LANES)
        mixture = group_of(heads, ap_ref, pair, group, half_low)
        gate_value = jax.nn.sigmoid(gl_ref[:, at])
        grad = gated_grad[:, at]
        dgl_ref[:, at] = (grad * mixture * gate_value * (1.0 - gate_value)).astype(BF16)
        for half, packed in enumerate(pack_rows(half_low, grad * gate_value)):
            if 2 * group + half < heads:
                put_pair(dap_refs, pair + 2 * group + half, packed.astype(BF16), start=start)


def hidden_back(
    order, heads, dc, dc_other, hidden, dy, gain_row, weights, gl, packed, rows, first, places, old, before, carry
):
    total, cols = gl.shape
    group, width = dc.shape
    count = group // rows
    whole = lambda i: (0, 0)
    here = lambda i: (first + i, 0)
    part = pl.BlockSpec((rows, width), lambda i: (i, 0))
    every = lambda shape: pl.BlockSpec(shape, lambda i: (0,) * len(shape))
    sent = [(packed.shape[0], stop - start, rows // 2, LANES) for start, stop in places]
    return order.call(
        functools.partial(hidden_back_kernel, heads, first, places[0][0], bool(old)),
        "hidden_back",
        (count,),
        [
            (dc, part),
            (dc_other, part),
            (hidden, part),
            (dy, pl.BlockSpec((rows, width), here)),
            (gain_row, pl.BlockSpec((1, width), whole)),
            (weights, pl.BlockSpec((width, cols), whole)),
            (gl, pl.BlockSpec((rows, cols), here)),
            (packed, every(packed.shape)),
        ]
        + [(array, every(array.shape)) for array in old],
        [
            ((total, width), BF16, pl.BlockSpec((rows, width), here)),
            ((total, cols), BF16, pl.BlockSpec((rows, cols), here)),
            ((group, width), F32, part),
            ((count, 1, width), F32, pl.BlockSpec((1, 1, width), lambda i: (i, 0, 0))),
        ]
        + [(shape, BF16, every(shape)) for shape in sent],
        4 * count,
        before=before,
        carry=carry,
    )


def project_back_kernel(
    heads,
    first,
    arrays,
    upper_ref,
    raw_ref,
    x_ref,
    dgl_ref,
    w_ref,
    gq_ref,
    gk_ref,
    *refs,
):
    g_refs = refs[:arrays]
    grads_ref, *da_refs, sums_ref, all_ref, da_ref = refs[arrays:]
    first_pair = (first + pl.program_id(0)) * heads
    rows, cols = dgl_ref.shape
    width = x_ref.shape[1]
    lane = lanes_of(rows)
    low = lane < HEAD_SIZE
    zero = jnp.zeros(lane.shape, F32)
    sums = [jnp.zeros((1, LANES), F32), jnp.zeros((1, LANES), F32)]

    def head_back(raw, upstream, gain_row, which):
        factor = lax.rsqrt(per_head(low, raw * raw) + EPSILON)
        scaled = upstream * gain_row
        inner = per_head(low, scaled * raw)
        sums[which] += jnp.sum(upstream * raw * factor, axis=0, keepdims=True)
        return factor * scaled - raw * (factor * factor * factor) * inner

    forget = zero
    for group in range(cols // LANES):
        at = group * LANES
        here = slice(at, at + LANES)
        pair = (2 * group, 2 * group + 1)
        held = [take_pair(g_refs, first_pair + h).astype(F32) if h < heads else None for h in pair]
        both = [zero if block is None else block[:, :LANES] for block in held]
        rest = [zero if block is None else block[:, LANES:] for block in held]
        query = head_back(raw_ref[:, here], merge_pair(low, *both), gq_ref[...], 0)
        key = head_back(
            raw_ref[:, cols + at : cols + at + LANES],
            merge_swapped(low, *both),
            gk_ref[...],
            1,
        )
        all_ref[:, here] = query.astype(BF16)
        all_ref[:, cols + at : cols + at + LANES] = key.astype(BF16)
        value = merge_pair(low, *rest)
        all_ref[:, 2 * cols + at : 2 * cols + at + LANES] = value.astype(BF16)
        for h, block in zip(pair, rest):
            if h < heads:
                forget = jnp.where(lane == h, block[:, 64:65], forget)
    all_ref[:, 3 * cols : 4 * cols] = dgl_ref[...]
    all_ref[:, 4 * cols :] = forget.astype(BF16)
    grads_ref[:, : 3 * cols] = all_ref[:, : 3 * cols]
    grads_ref[:, 3 * cols :] = all_ref[:, 4 * cols :]
    da = dot(all_ref[...], w_ref[...], NT)
    if len(da_refs) == 1:
        da_refs[0][...] = da.astype(BF16)
    else:
        da_ref[...] = da
        half = rows // 2
        upper = upper_ref[0]
        for ref, part in zip(da_refs, (upper, 1 - upper)):
            ref[0] = da_ref[pl.ds(pl.multiple_of(part * half, half), half), :].astype(BF16)

    x = x_ref[...].astype(F32)
    sums_ref[0, :, :width] = jnp.sum(da * x * rms_factor(x), axis=0, keepdims=True)
    sums_ref[0, :, width : width + LANES] = sums[0]
    sums_ref[0, :, width + LANES : width + 2 * LANES] = sums[1]
    sums_ref[0, :, width + 2 * LANES :] = jnp.sum(forget, axis=0, keepdims=True)


def project_back(
    order, heads, upper, returned, raw, x, dgl, weights, gq_row, gk_row, rows, first, count, halves, before, after, carry
):
    total, cols = dgl.shape
    width, wide = weights.shape
    half = rows // 2
    whole = lambda i, upper: (0, 0)
    here = lambda i, upper: (first + i, 0)
    row = pl.BlockSpec((1, LANES), whole)
    sums = width + 3 * LANES
    if halves:
        da = [((count, half, width), BF16, pl.BlockSpec((1, half, width), lambda i, upper: (i, 0, 0)))] * 2
    else:
        da = [((count * rows, width), BF16, pl.BlockSpec((rows, width), lambda i, upper: (i, 0)))]
    return order.call(
        functools.partial(project_back_kernel, heads, first, len(returned)),
        "project_back",
        (count,),
        [
            (raw, pl.BlockSpec((rows, 2 * cols), here)),
            (x, pl.BlockSpec((rows, width), here)),
            (dgl, pl.BlockSpec((rows, cols), here)),
            (weights, pl.BlockSpec((width, wide), whole)),
            (gq_row, row),
            (gk_row, row),
        ]
        + [(array, pl.BlockSpec(array.shape, lambda i, upper: (0, 0, 0, 0))) for array in returned],
        [((total, wide - cols), BF16, pl.BlockSpec((rows, wide - cols), here))]
        + da
        + [((count, 1, sums), F32, pl.BlockSpec((1, 1, sums), lambda i, upper: (i, 0, 0)))],
        6 * count,
        scratch=[pltpu.VMEM((rows, wide), BF16), pltpu.VMEM((rows, width), F32)],
        before=before,
        scalars=(upper,),
        after=after,
        carry=carry,
    )


def input_back_kernel(rank_ref, x_ref, dh_ref, gain_ref, own_ref, *refs):
    *passed, out_ref = refs
    rank, count = rank_ref[0], len(passed) + 1
    da = own_ref[...].astype(F32)
    for t, ref in enumerate(passed):
        taken = jnp.where(pl.program_id(0) == 0, rank == t + 1, rank == count - 2 - t)
        da = jnp.where(taken, ref[...].astype(F32), da)
    x = x_ref[...].astype(F32)
    out_ref[...] = dh_ref[...] + norm_back(x, rms_factor(x), gain_ref[...], da)


def input_back(order, rank, summed, place, x, dh, dh_place, gain_row, rows, micro, before, after):
    total, width = x.shape
    half = rows // 2
    here = pl.BlockSpec((half, width), lambda i, rank: (2 * micro + i, 0))
    one = pl.BlockSpec((half, width), lambda i, rank: (2 * place + i, 0))
    mine = pl.BlockSpec((half, width), lambda i, rank: (2 * dh_place + i, 0))
    passing = pl.BlockSpec((half, width), lambda i, rank: (0, 0))
    return order.call(
        input_back_kernel,
        "input_back",
        (2,),
        [(x, here), (dh, mine), (gain_row, pl.BlockSpec((1, width), lambda i, rank: (0, 0)))]
        + [(block, one if len(summed) == 1 else passing) for block in summed],
        [((total, width), F32, here)],
        4,
        before=before,
        scalars=(rank,),
        after=after,
    )


def layer_out_kernel(hid_ref, part_ref, other_ref, out_ref):
    total = hid_ref[...] + (part_ref[...].astype(F32) + other_ref[...].astype(F32))
    out_ref[...] = total.astype(BF16)


def layer_output(order, hidden, part, other, group, total, before, after):
    rows, width = hidden.shape
    tiles = 4
    tile = rows // tiles
    one = pl.BlockSpec((tile, width), lambda i: (i, 0))
    return order.call(
        layer_out_kernel,
        "layer_out",
        (tiles,),
        [(hidden, one), (part, one), (other, one)],
        [((total, width), BF16, pl.BlockSpec((tile, width), lambda i: (tiles * group + i, 0)))],
        4,
        before=before,
        after=after,
    )


def pad_to(array, size, axis):
    missing = size - array.shape[axis]
    if missing == 0:
        return array
    widths = [(0, missing if i == axis else 0) for i in range(array.ndim)]
    return jnp.pad(array, widths)


def turned_kernel(*refs):
    out_ref, at = refs[-1], 0
    for left_ref, right_ref in zip(refs[:-1:2], refs[1:-1:2]):
        wide = right_ref.shape[1]
        product = lax.dot_general(
            left_ref[...], right_ref[...], (((0,), (0,)), ((), ())), preferred_element_type=F32
        )
        out_ref[:, at : at + wide] = product.astype(BF16)
        at += wide


def turned_products(order, pairs, us):
    height = pairs[0][0].shape[1]
    tile = 256
    ins, wide = [], 0
    for left, right in pairs:
        ins.append((left, pl.BlockSpec((left.shape[0], tile), lambda i: (0, i))))
        ins.append((right, pl.BlockSpec(right.shape, lambda i: (0, 0))))
        wide += right.shape[1]
    return order.call(
        turned_kernel,
        "turned_products",
        (height // tile,),
        ins,
        [((height, wide), BF16, pl.BlockSpec((tile, wide), lambda i: (i, 0)))],
        us,
    )[0]


def owned_kernel(own, left_ref, right_ref, sums_ref, out_ref):
    product = lax.dot_general(
        left_ref[...], right_ref[...], (((0,), (0,)), ((), ())), preferred_element_type=F32
    ).astype(BF16)
    for i in range(out_ref.shape[0]):
        out_ref[i, :own] = product[i * own : (i + 1) * own]
        out_ref[i, own:] = sums_ref[i]


def owned_product(order, left, right, sums, us, carry):
    rows, height = left.shape
    owners, extra, wide = sums.shape
    own = height // owners
    step = 1
    while own * step % LANES:
        step += 1
    return order.call(
        functools.partial(owned_kernel, own),
        "owned_product",
        (owners // step,),
        [
            (left, pl.BlockSpec((rows, own * step), lambda i: (0, i))),
            (right, pl.BlockSpec((rows, wide), lambda i: (0, 0))),
            (sums, pl.BlockSpec((step, extra, wide), lambda i: (i, 0, 0))),
        ],
        [((owners, own + extra, wide), BF16, pl.BlockSpec((step, own + extra, wide), lambda i: (i, 0, 0)))],
        us,
        carry=carry,
    )


def line_steps(count):
    return [((t - 1, t), (count - t, count - 1 - t)) for t in range(1, count)]


def line_sum(kept, sent, axis):
    count = lax.axis_size(axis)
    steps = line_steps(count)
    moving = sent
    for t, hops in enumerate(steps):
        arrived = lax.ppermute(moving, axis, hops)
        moving = arrived + (sent if t + 2 <= count // 2 else kept)
    passed = [moving]
    for hops in steps:
        passed.append(lax.ppermute(passed[-1], axis, hops))
    return passed


def exchanged(array, axis, flip):
    count = lax.axis_size(axis)
    return lax.ppermute(array, axis, [(i, i ^ flip) for i in range(count)])


def to_all(array, axis):
    return lax.all_to_all(array, axis, 0, 0, tiled=True)


def small_sum(row, axis):
    flip = 1
    while flip < lax.axis_size(axis):
        row = row + exchanged(row, axis, flip)
        flip *= 2
    return row


def shards(
    inputs,
    cotangent,
    tail_keys,
    tail_values,
    tail_forget,
    gain_one,
    gain_two,
    w_query,
    w_key,
    w_value,
    w_forget,
    forget_bias,
    query_gain,
    key_gain,
    w_outgate,
    w_out,
    w_gate,
    w_up,
    w_down,
):
    micros, rows, width = inputs.shape
    total = micros * rows
    own_cols = w_query.shape[1]
    heads = w_forget.shape[1]
    ff = w_gate.shape[1]
    seq_count = lax.axis_size("seq")
    head_count = lax.axis_size("head")
    seq_rank = lax.axis_index("seq")
    head_rank = lax.axis_index("head")
    cols = -(-own_cols // LANES) * LANES
    pair_total = micros * heads
    pairs = -(-pair_total // seq_count)
    padded_pairs = pairs * seq_count
    tail_length = tail_keys.shape[1]

    x = inputs.reshape(total, width)
    dy = cotangent.reshape(total, width)

    small = jnp.concatenate([w_forget, gain_one[:, None], gain_two[:, None]], axis=1)
    first_shard = jnp.concatenate(
        [pad_to(w, cols, 1) for w in (w_query, w_key, w_value, w_outgate)]
        + [pad_to(small, LANES, 1)],
        axis=1,
    )
    first = lax.all_gather(first_shard, "seq", axis=0, tiled=True)
    near_shard = jnp.concatenate([w_gate, w_up, w_down.T], axis=1)
    near = lax.all_gather(near_shard, "seq", axis=0, tiled=True)
    split = 3 * ff // 2
    outs, units, early = [pad_to(w_out.T, cols, 1)], [(near_shard[:, :split], near_shard[:, split:])], []
    flip = 1
    while flip < head_count:
        outs.append(exchanged(jnp.concatenate(outs, axis=1), "head", flip))
        if flip == 1:
            early.append(outs[-1])
        else:
            units += [tuple(exchanged(part, "head", flip) for part in unit) for unit in units]
        flip *= 2
    far_parts = outs + [part for unit in units[1:] for part in unit]
    rank = head_rank.astype(jnp.int32)[None]
    upper = (rank >= head_count // 2).astype(jnp.int32)
    order = Order()
    gain_one_row = first[:, 4 * cols + heads].astype(F32)[None, :]
    gain_two_row = first[:, 4 * cols + heads + 1].astype(F32)[None, :]
    bias_here = lax.dynamic_slice_in_dim(forget_bias, head_rank * heads, heads, 0)
    bias_row = pad_to(bias_here[None, :], LANES, 1)
    gq_row = jnp.tile(query_gain.astype(F32), 2)[None, :]
    gk_row = jnp.tile(key_gain.astype(F32), 2)[None, :]

    tail_key_parts, tail_value_parts = [], []
    for j in range(pairs):
        p = jnp.minimum(j * seq_count + seq_rank, pair_total - 1)
        m, h = p // heads, p % heads
        tail_of = lambda array, wide: lax.dynamic_slice(
            array, (m, 0, h * wide), (1, tail_length, wide)
        )[0]
        forget = tail_of(tail_forget, 1)
        decay = jnp.cumsum(forget, axis=0) - jnp.sum(forget, axis=0, keepdims=True)
        high = lax.reduce_precision(decay, 8, 7)
        middle = lax.reduce_precision(decay - high, 8, 7)
        least = decay - high - middle
        ones = jnp.ones((tail_length, 3), BF16)
        parts = jnp.concatenate([-high, -middle, -least], axis=1).astype(BF16)
        tail_key_parts.append(
            pad_to(jnp.concatenate([tail_of(tail_keys, HEAD_SIZE), ones, parts], axis=1), LANES, 1)
        )
        tail_value_parts.append(
            pad_to(jnp.concatenate([tail_of(tail_values, HEAD_SIZE), ones], axis=1), LANES, 1)
        )
    tail_key, tail_value = jnp.stack(tail_key_parts), jnp.stack(tail_value_parts)

    a, raw, gl, *pays = project(
        order, heads, cols, seq_count, x, first, bias_row, gain_one_row, gq_row, gk_row, micros, early
    )
    pays = [to_all(pay, "seq") for pay in pays]
    kept, returned = [], []
    most = max(pairs - 1, 1)
    for j, pay in enumerate(pays):
        in_most = j < most
        packed, *saved = attend(
            order,
            pay,
            tail_key,
            tail_value,
            j,
            most if in_most else pairs - most,
            j if in_most else j - most,
            (packed,) if 0 < j < most else (),
        )
        kept.append((saved, pay, 0))
        if j >= most - 1:
            returned.append(to_all(packed, "seq"))
        if j == 0:
            far = lax.all_gather(pack(order, far_parts), "seq", axis=0, tiled=True)
    packed = jnp.concatenate(returned, axis=1)

    size = 2 if micros % 2 == 0 else 1
    groups = micros // size
    chunk = min(512, ff)
    gated, o_alls = (), []
    for g in range(groups):
        enough = (g + 1) * size * heads <= most * seq_count
        *gated, sent = gate(
            order, heads, returned[0] if enough else packed, gl, rows, g * size, size, head_count, gated
        )
        o_alls.append(to_all(sent, "head"))
    o = gated[0]

    hiddens, out_parts, dc_parts, dc_others = [], [], [], []
    dhs, gains_two = [], []
    late, carried = (), None
    early_places = size * heads // seq_count if groups > 1 else 0
    fed, backed = (), ()

    def back_to_heads(g, carry=()):
        nonlocal backed, late, carried
        places = [(early_places, pairs)]
        if g == 0 and early_places > 0:
            places = [(0, early_places)] + places
        *results, out_parts[g] = hidden_back(
            order,
            heads,
            dc_parts[g],
            dc_others[g],
            hiddens[g],
            dy,
            gain_two_row,
            far,
            gl,
            packed,
            rows,
            g * size,
            places,
            late,
            backed,
            carry + (out_parts[g],),
        )
        if carry:
            carried = results.pop()
        dhb, dgl, dh, gain, *sent = results
        backed, late = (dhb, dgl), (sent[-1],)
        dhs.append(dh)
        gains_two.append(gain)
        return sent[0]

    def scattered(grad):
        return lax.psum_scatter(grad, "seq", scatter_dimension=0, tiled=True)

    for g in range(groups):
        *fed, hidden, out_part, dc_part = feed(
            order, rank, x, dy, o_alls[g], near, far, gain_two_row, ff, chunk, g, fed
        )
        hiddens.append(hidden)
        out_parts.append(out_part)
        dc_parts.append(dc_part)
        dc_others.append(exchanged(dc_part, "head", 1))
        if g > 0:
            early_grads = back_to_heads(g - 1)
    c, u, dgu = fed
    unit_grads = scattered(turned_products(order, [(c, dgu), (dy, u)], 13))

    layer_out = ()

    def put_out(g, after=()):
        nonlocal layer_out
        other = exchanged(out_parts[g], "head", 1)
        layer_out = layer_output(order, hiddens[g], out_parts[g], other, g, total, layer_out, after)

    if early_places > 0:
        early_grads = to_all(early_grads, "seq")
    returned = []
    mixed, grad = (), ()
    for j in range(pairs):
        if j == early_places:
            back_to_heads(groups - 1)
            mixed = (turned_products(order, [(backed[0], o), (a, backed[1])], 8),)
            late_grads = to_all(late[0], "seq")
        sent = (early_grads, j) if j < early_places else (late_grads, j - early_places)
        saved, pay, place = kept[j]
        grad, *mixed = attend_back(
            order,
            saved[1:],
            tail_key,
            tail_value,
            saved[0],
            sent[0],
            pay,
            j,
            place,
            sent[1],
            most if j < most else pairs - most,
            j if j < most else j - most,
            (grad,) if 0 < j < most else (),
            tuple(mixed),
            (),
        )
        if j >= most - 1:
            returned.append(to_all(grad, "seq"))

    put_out(0)

    grads, da_sums, gains_one = (), [], []
    for g in range(groups):
        last = g == groups - 1
        results = project_back(
            order,
            heads,
            upper,
            returned[:1] if (g + 1) * size * heads <= most * seq_count else returned,
            raw,
            x,
            backed[1],
            first,
            gq_row,
            gk_row,
            rows,
            g * size,
            size,
            last,
            grads,
            (unit_grads,) if g == 0 else (),
            mixed,
        )
        count = 2 if last else 1
        grads, da, gain, mixed = results[:1], results[1 : 1 + count], results[1 + count], results[2 + count :]
        gains_one.append(gain)
        if last:
            da_sums += [(line_sum(da[0][i], da[1][i], "head"), 0) for i in range(size)]
        else:
            total_da = lax.psum(da[0], "head")
            da_sums += [([total_da], i) for i in range(size)]

    one_sums = jnp.sum(jnp.concatenate(gains_one, axis=0), axis=0)
    two_sums = jnp.sum(jnp.concatenate(gains_two, axis=0), axis=0) * (1.0 / head_count)
    own_rows = gain_one.shape[0]
    shared = pad_to(one_sums[:, width:], 3 * LANES, 1)
    owned_sums = jnp.concatenate(
        [
            one_sums[:, :width].reshape(seq_count, own_rows),
            two_sums.reshape(seq_count, own_rows),
            jnp.broadcast_to(shared, (seq_count, 3 * LANES)),
        ],
        axis=1,
    ).astype(BF16)
    owned_sums = jnp.pad(owned_sums[:, None], ((0, 0), (0, 15), (0, grads[0].shape[1] - owned_sums.shape[1])))
    head_grads, *mixed = owned_product(order, a, grads[0], owned_sums, 9, mixed)
    mixed_grads = scattered(mixed[0]) if mixed else mixed_grads
    for out in range(1, groups):
        put_out(out)

    head_grads = jnp.sum(to_all(head_grads, "seq").astype(F32), axis=0)
    sums = head_grads[own_rows : own_rows + 1]
    head_grads = head_grads[:own_rows]
    unit_grads, mixed_grads = unit_grads.astype(F32), mixed_grads.astype(F32)
    strips = [unit_grads[:, i * chunk : (i + 1) * chunk] for i in range(2 * ff // chunk)]
    grad_gate = jnp.concatenate(strips[0::2], axis=1)
    grad_up = jnp.concatenate(strips[1::2], axis=1)
    grad_down = unit_grads[:, 2 * ff :].T
    grad_out = mixed_grads[:, :own_cols].T

    gain_lanes = 2 * own_rows
    bias_at = gain_lanes + 2 * LANES
    bias_full = lax.dynamic_update_slice(
        jnp.zeros((1, forget_bias.shape[0]), F32), sums[:, bias_at : bias_at + heads], (0, head_rank * heads)
    )
    sums = small_sum(jnp.concatenate([sums[:, :bias_at], bias_full], axis=1), "head")[0]
    halves = sums[gain_lanes:bias_at].reshape(4, HEAD_SIZE)
    gq_total, gk_total = halves[0] + halves[1], halves[2] + halves[3]
    bias_total = sums[bias_at:]

    input_grad = ()
    for m in range(micros):
        summed, place = da_sums[m]
        input_grad = input_back(
            order, rank, summed, place, x, dhs[m // size], m % size, gain_one_row, rows, m, input_grad, ()
        )

    input_grad, layer_out = input_grad[0], layer_out[0]
    shape = inputs.shape
    return (
        layer_out.reshape(shape),
        input_grad.reshape(shape),
        sums[:own_rows],
        sums[own_rows:gain_lanes],
        head_grads[:, :own_cols],
        head_grads[:, cols : cols + own_cols],
        head_grads[:, 2 * cols : 2 * cols + own_cols],
        head_grads[:, 3 * cols : 3 * cols + heads],
        bias_total,
        gq_total,
        gk_total,
        mixed_grads[:, cols : cols + own_cols],
        grad_out,
        grad_gate,
        grad_up,
        grad_down,
    )


def solution(mesh):
    by_rows = P("seq", "head")
    by_cols = P("head", "seq")
    placed = (
        P(None, "seq", None),
        P(None, "seq", None),
        P(None, None, "head"),
        P(None, None, "head"),
        P(None, None, "head"),
        P("seq"),
        P("seq"),
        by_rows,
        by_rows,
        by_rows,
        by_rows,
        P(),
        P(),
        P(),
        by_rows,
        by_cols,
        by_rows,
        by_rows,
        by_cols,
    )
    return jax.shard_map(
        shards,
        mesh=mesh,
        in_specs=placed,
        out_specs=(
            P(None, "seq", None),
            P(None, "seq", None),
            P("seq"),
            P("seq"),
            by_rows,
            by_rows,
            by_rows,
            by_rows,
            P(),
            P(),
            P(),
            by_rows,
            by_cols,
            by_rows,
            by_rows,
            by_cols,
        ),
        check_vma=False,
    )
```

```python
import functools

import jax
import jax.numpy as jnp
from jax import lax
from jax.experimental import pallas as pl
from jax.experimental.pallas import tpu as pltpu
from jax.sharding import PartitionSpec as P

HEAD_SIZE = 64
LANES = 128
EPSILON = 1e-06
F32 = jnp.float32
BF16 = jnp.bfloat16
NN = (((1,), (0,)), ((), ()))
NT = (((1,), (1,)), ((), ()))
HIDE = -1e30
SCALE = HEAD_SIZE**-0.5
STRIP = 64
MIB = 1024 * 1024


def dot(left, right, dims=NN):
    return lax.dot_general(left, right, dims, preferred_element_type=F32)


def params():
    return pltpu.CompilerParams(vmem_limit_bytes=60 * MIB)


def linked(kernel, inputs, extra, outputs, carried):
    def body(*refs):
        first = inputs + extra
        token = refs[first + outputs + carried]
        token[...] = jnp.zeros_like(token)
        kernel(*refs[:inputs], *refs[first : first + outputs], *refs[first + outputs + carried + 1 :])

    return body


class Order:
    def __init__(self):
        self.tokens = []

    def call(
        self, kernel, name, grid, ins, outs, us, scratch=(), before=(), scalars=(), after=(), carry=()
    ):
        arrays = list(scalars) + [array for array, _ in ins]
        extra = list(before) + list(carry) + list(after) + self.tokens
        count = len(arrays)
        whole = lambda *at: (0, 0)
        anywhere = pl.BlockSpec(memory_space=pl.ANY)
        out_specs = [spec for _, _, spec in outs] + [anywhere] * len(carry)
        out_specs.append(pl.BlockSpec((8, LANES), whole))
        out_shape = [jax.ShapeDtypeStruct(shape, kind) for shape, kind, _ in outs]
        out_shape += [jax.ShapeDtypeStruct(array.shape, array.dtype) for array in carry]
        out_shape.append(jax.ShapeDtypeStruct((8, LANES), F32))
        aliases = {count + i: i for i in range(len(before))}
        for i in range(len(carry)):
            aliases[count + len(before) + i] = len(outs) + i
        *results, token = pl.pallas_call(
            linked(kernel, count, len(extra), len(outs), len(carry)),
            grid_spec=pltpu.PrefetchScalarGridSpec(
                num_scalar_prefetch=len(scalars),
                grid=grid,
                in_specs=[spec for _, spec in ins] + [anywhere] * len(extra),
                out_specs=out_specs,
                scratch_shapes=list(scratch),
            ),
            out_shape=out_shape,
            input_output_aliases=aliases,
            compiler_params=params(),
            cost_estimate=pl.CostEstimate(flops=int(us * 8e9), bytes_accessed=0, transcendentals=0),
            name=name,
        )(*arrays, *extra)
        self.tokens = [token]
        return results


def lanes_of(rows):
    return lax.broadcasted_iota(jnp.int32, (rows, LANES), 1)


def swap_halves(block):
    return pltpu.roll(block, HEAD_SIZE, 1)


def in_three(value):
    high = value.astype(BF16).astype(F32)
    rest = value - high
    middle = rest.astype(BF16).astype(F32)
    return high, middle, rest - middle


def at_lanes(lane, first, parts, base):
    for place, part in enumerate(parts):
        base = jnp.where(lane == first + place, part, base)
    return base


def triangle(rows, lower):
    down = lax.broadcasted_iota(jnp.int32, (rows, rows), 0)
    across = lax.broadcasted_iota(jnp.int32, (rows, rows), 1)
    return jnp.where(down >= across if lower else down <= across, 1.0, 0.0).astype(BF16)


def running_sum(tri, column, lane):
    spread = at_lanes(lane, 0, in_three(column), jnp.zeros(lane.shape, F32))
    sums = dot(tri, spread.astype(BF16))
    return sums[:, 0:1] + sums[:, 1:2] + sums[:, 2:3]


def forget_column(tail_block):
    return tail_block[:, 64:65] + tail_block[:, 65:66] + tail_block[:, 66:67]


def per_head(low, values):
    first = jnp.sum(jnp.where(low, values, 0.0), axis=-1, keepdims=True)
    second = jnp.sum(jnp.where(low, 0.0, values), axis=-1, keepdims=True)
    return jnp.where(low, first, second) * (1.0 / HEAD_SIZE)


def rms_factor(values):
    return lax.rsqrt(jnp.mean(values * values, axis=-1, keepdims=True) + EPSILON)


def merge_pair(low, first, second):
    return jnp.where(low, first, swap_halves(second))


def merge_swapped(low, first, second):
    return jnp.where(low, swap_halves(first), second)


def put_pair(refs, pair, block, column=0, start=0):
    owners = refs[0].shape[0]
    owner, place = lax.rem(pair, owners), lax.div(pair, owners)
    width = block.shape[1]
    for ref in refs:
        stop = start + ref.shape[1]

        @pl.when((place >= start) & (place < stop))
        def _(ref=ref, start=start):
            ref[owner, place - start, :, column : column + width] = block

        start = stop


def unpack_rows(low_half, first, second):
    strip = low_half.shape[0]
    rows = []
    for at in range(0, first.shape[0], strip):
        one, two = first[at : at + strip], second[at : at + strip]
        rows.append(jnp.where(low_half, one, swap_halves(two)))
        rows.append(jnp.where(low_half, swap_halves(one), two))
    return jnp.concatenate(rows, axis=0)


def pack_rows(low_half, block):
    strip = low_half.shape[0]
    first, second = [], []
    for at in range(0, block.shape[0], 2 * strip):
        top, bottom = block[at : at + strip], block[at + strip : at + 2 * strip]
        first.append(jnp.where(low_half, top, swap_halves(bottom)))
        second.append(jnp.where(low_half, swap_halves(top), bottom))
    return jnp.concatenate(first, axis=0), jnp.concatenate(second, axis=0)


def project_kernel(
    heads, idle, x_ref, w_ref, bias_ref, gain_ref, gq_ref, gk_ref, a_ref, raw_ref, gl_ref, *pay_refs
):
    x = x_ref[...].astype(F32)
    rows = x.shape[0]
    cols = gl_ref.shape[1]
    a = (x * rms_factor(x) * gain_ref[...]).astype(BF16)
    a_ref[...] = a
    proj = dot(a, w_ref[...])
    raw_ref[...] = proj[:, : 2 * cols]
    gl_ref[...] = proj[:, 3 * cols : 4 * cols]
    logit = proj[:, 4 * cols :] + bias_ref[...]
    lane = lanes_of(rows)
    low = lane < HEAD_SIZE
    for group in range(cols // LANES):
        at = group * LANES
        query = proj[:, at : at + LANES]
        key = proj[:, cols + at : cols + at + LANES]
        value = proj[:, 2 * cols + at : 2 * cols + at + LANES]
        query = query * lax.rsqrt(per_head(low, query * query) + EPSILON) * gq_ref[...]
        key = key * lax.rsqrt(per_head(low, key * key) + EPSILON) * gk_ref[...]
        for half in range(2):
            head = 2 * group + half
            if head >= heads:
                continue
            zl = at_lanes(lane, 64, in_three(logit[:, head : head + 1]), jnp.zeros(lane.shape, F32))
            if half == 0:
                both = merge_pair(low, query, key)
                rest = jnp.where(low, value, zl)
            else:
                both = merge_swapped(low, query, key)
                rest = jnp.where(low, swap_halves(value), zl)
            pair = pl.program_id(0) * heads + head
            put_pair(pay_refs, pair, both.astype(BF16))
            put_pair(pay_refs, pair, rest.astype(BF16), LANES)

    @pl.when(pl.program_id(0) == 0)
    def _():
        for pair in idle:
            put_pair(pay_refs, pair, jnp.zeros((rows, 2 * LANES), BF16))


def project(order, heads, cols, owners, x, weights, bias_row, gain_row, gq_row, gk_row, micros, after):
    total, width = x.shape
    rows = total // micros
    wide = weights.shape[1]
    whole = lambda m: (0, 0)
    part = lambda m: (m, 0)
    row = pl.BlockSpec((1, LANES), whole)
    pairs = -(-micros * heads // owners)
    idle = range(micros * heads, pairs * owners)
    parts = [1] * pairs
    sent = [(owners, part, rows, 2 * LANES) for part in parts]
    return order.call(
        functools.partial(project_kernel, heads, idle),
        "project",
        (micros,),
        [
            (x, pl.BlockSpec((rows, width), part)),
            (weights, pl.BlockSpec((width, wide), whole)),
            (bias_row, row),
            (gain_row, pl.BlockSpec((1, width), whole)),
            (gq_row, row),
            (gk_row, row),
        ],
        [
            ((total, width), BF16, pl.BlockSpec((rows, width), part)),
            ((total, 2 * cols), F32, pl.BlockSpec((rows, 2 * cols), part)),
            ((total, cols), F32, pl.BlockSpec((rows, cols), part)),
        ]
        + [(shape, BF16, pl.BlockSpec(shape, lambda m: (0, 0, 0, 0))) for shape in sent],
        13,
        after=after,
    )


def attend_kernel(size, pay_ref, tk_ref, tv_ref, ap_ref, af_ref, q_ref, k_ref, v_ref):
    blocks, _, rows, _ = pay_ref.shape
    length = blocks * rows
    lane = lanes_of(rows)
    low = lane < HEAD_SIZE
    tri = triangle(rows, True)
    zero = jnp.zeros(lane.shape, F32)

    def build(b, carry):
        at = pl.ds(pl.multiple_of(b * rows, rows), rows)
        both = pay_ref[b, 0, :, :LANES].astype(F32)
        rest = pay_ref[b, 0, :, LANES:].astype(F32)
        logit = forget_column(rest)
        log_forget = jnp.minimum(logit, 0.0) - jnp.log1p(jnp.exp(-jnp.abs(logit)))
        decay = running_sum(tri, log_forget, lane) + carry
        high, middle, least = in_three(decay)
        query_side = at_lanes(lane, 64, (high, middle, least, 1.0, 1.0, 1.0), zero)
        key_side = at_lanes(lane, 64, (1.0, 1.0, 1.0, -high, -middle, -least), zero)
        value_side = at_lanes(lane, 64, (1.0, 1.0, 1.0), zero)
        q_ref[0, at, :] = jnp.where(low, both * SCALE, query_side).astype(BF16)
        k_ref[0, at, :] = jnp.where(low, swap_halves(both), key_side).astype(BF16)
        v_ref[0, at, :] = jnp.where(low, rest, value_side).astype(BF16)
        return decay[rows - 1 :, :]

    lax.fori_loop(0, blocks, build, jnp.zeros((1, 1), F32))

    tail_length = tk_ref.shape[1]
    visible = lax.broadcasted_iota(jnp.int32, (size, size), 0) >= lax.broadcasted_iota(
        jnp.int32, (size, size), 1
    )
    half_low = lanes_of(STRIP) < HEAD_SIZE
    lane_here = lanes_of(size)

    def one_block(qi):
        at = pl.ds(qi * size, size)
        query = q_ref[0, at, :]

        def absorb(key, value, total, masked=False):
            scores = dot(query, key, NT)
            if masked:
                scores = jnp.where(visible, scores, HIDE)
            return total + dot(jnp.exp(scores).astype(BF16), value)

        total = jnp.zeros((size, LANES), F32)
        for t in range(tail_length // size):
            here = pl.ds(t * size, size)
            total = absorb(tk_ref[0, here, :], tv_ref[0, here, :], total)

        for ki in range(qi):
            here = pl.ds(ki * size, size)
            total = absorb(k_ref[0, here, :], v_ref[0, here, :], total)
        total = absorb(k_ref[0, at, :], v_ref[0, at, :], total, True)
        weight = total[:, 64:65]
        mixture = total / weight
        af_ref[0, at, :] = mixture
        for piece in range(size // rows):
            block = mixture[piece * rows : (piece + 1) * rows]
            packed, _ = pack_rows(half_low, block)
            ap_ref[qi * (size // rows) + piece, 0] = packed.astype(BF16)
        old = query.astype(F32)
        shifted = forget_column(old) - jnp.log(weight)
        q_ref[0, at, :] = at_lanes(lane_here, 64, in_three(shifted), old).astype(BF16)

    for qi in range(length // size):
        one_block(qi)


def attend(order, pay, tail_key, tail_value, first, out_places, out_place, before):
    blocks, pairs, rows, _ = pay.shape
    length = blocks * rows
    tail_length = tail_key.shape[1]
    size = min(512, length)
    pair = lambda j: (j, 0, 0)
    across = lambda j: (0, j, 0, 0)
    tail = pl.BlockSpec((1, tail_length, LANES), lambda j: (first + j, 0, 0))
    whole = pl.BlockSpec((1, length, LANES), pair)
    return order.call(
        functools.partial(attend_kernel, size),
        "attend",
        (pairs,),
        [
            (pay, pl.BlockSpec((blocks, 1, rows, 2 * LANES), across)),
            (tail_key, tail),
            (tail_value, tail),
        ],
        [
            (
                (blocks, out_places, rows // 2, LANES),
                BF16,
                pl.BlockSpec((blocks, 1, rows // 2, LANES), lambda j: (0, out_place, 0, 0)),
            ),
            ((pairs, length, LANES), F32, whole),
            ((pairs, length, LANES), BF16, whole),
            ((pairs, length, LANES), BF16, whole),
            ((pairs, length, LANES), BF16, whole),
        ],
        14 * pairs,
        before=before,
    )


def attend_back_kernel(
    size,
    q_ref,
    k_ref,
    v_ref,
    tk_ref,
    tv_ref,
    af_ref,
    dap_ref,
    rest_ref,
    g_ref,
    da_ref,
    dqt_ref,
    sums_ref,
):
    blocks, _, rows, _ = rest_ref.shape
    length = blocks * rows
    lane = lanes_of(rows)
    low = lane < HEAD_SIZE
    zero = jnp.zeros(lane.shape, F32)

    def build(b, carry):
        at = pl.ds(pl.multiple_of(b * rows, rows), rows)
        packed = dap_ref[b, 0].astype(F32)
        strips = []
        for strip in range(0, packed.shape[0], STRIP):
            strips += [packed[strip : strip + STRIP], swap_halves(packed[strip : strip + STRIP])]
        grad = jnp.where(low, jnp.concatenate(strips, axis=0), 0.0)
        delta = jnp.sum(grad * af_ref[0, at, :], axis=-1, keepdims=True)
        da_ref[at, :] = at_lanes(lane, 64, in_three(-delta), grad).astype(BF16)
        return carry

    lax.fori_loop(0, blocks, build, 0)

    across = lax.broadcasted_iota(jnp.int32, (size, size), 1)
    down = lax.broadcasted_iota(jnp.int32, (size, size), 0)
    visible = across >= down
    count = length // size

    def block_at(i):
        return pl.ds(i * size, size)

    def pieces(key, value, at, masked=False):
        scores = dot(key, q_ref[0, at, :], NT)
        if masked:
            scores = jnp.where(visible, scores, HIDE)
        prob = jnp.exp(scores)
        score_grad = prob * dot(value, da_ref[at, :], NT)
        return prob.astype(BF16), score_grad.astype(BF16)

    tail_length = tk_ref.shape[1]
    tail_count = tail_length // size

    for qi in range(count):
        at = block_at(qi)
        total = jnp.zeros((LANES, size), F32)
        for t in range(tail_count):
            key = tk_ref[0, pl.ds(t * size, size), :]
            _, score_grad = pieces(key, tv_ref[0, pl.ds(t * size, size), :], at)
            total = total + dot(key.T, score_grad)
        dqt_ref[:, at] = total

    lane_here = lanes_of(size)
    low_here = lane_here < HEAD_SIZE

    for ki in range(count):
        own = block_at(ki)
        key = k_ref[0, own, :]
        value = v_ref[0, own, :]
        key_turned = key.T

        def one(at, sums, masked=False, key=key, value=value, key_turned=key_turned):
            key_sum, value_sum = sums
            prob, score_grad = pieces(key, value, at, masked)
            dqt_ref[:, at] += dot(key_turned, score_grad)
            return (
                key_sum + dot(score_grad, q_ref[0, at, :]),
                value_sum + dot(prob, da_ref[at, :]),
            )

        start = (jnp.zeros((size, LANES), F32), jnp.zeros((size, LANES), F32))
        sums = one(own, start, True)
        for qi in range(ki + 1, count):
            sums = one(block_at(qi), sums)
        key_sum, value_sum = sums
        sums_ref[own, :] = key_sum
        for piece in range(size // rows):
            here = slice(piece * rows, (piece + 1) * rows)
            g_ref[ki * (size // rows) + piece, 0, :, LANES:] = value_sum[here].astype(BF16)

    tri = triangle(rows, False)

    def finish(i, carry):
        b = blocks - 1 - i
        at = pl.ds(pl.multiple_of(b * rows, rows), rows)
        query = dqt_ref[:, at].T
        key = sums_ref[at, :]
        decay_grad = query[:, 64:65] - key[:, 67:68]
        suffix = running_sum(tri, decay_grad, lane) + carry
        logit = forget_column(rest_ref[b, 0].astype(F32))
        forget_grad = suffix / (1.0 + jnp.exp(logit))
        both = jnp.where(low, query * SCALE, swap_halves(key))
        rest = jnp.where(low, g_ref[b, 0, :, LANES:].astype(F32), jnp.where(lane == 64, forget_grad, 0.0))
        g_ref[b, 0, :, :LANES] = both.astype(BF16)
        g_ref[b, 0, :, LANES:] = rest.astype(BF16)
        return suffix[0:1, :]

    lax.fori_loop(0, blocks, finish, jnp.zeros((1, 1), F32))


def attend_back(
    order, saved, tail_key, tail_value, mixture, packed_grad, pay, place, saved_place, grad_place, out_places, out_place, before, carry, after
):
    blocks, _, rows, _ = pay.shape
    length = blocks * rows
    tail_length = tail_key.shape[1]
    size = min(512, length)
    pair = lambda j: (place, 0, 0)
    tail = pl.BlockSpec((1, tail_length, LANES), pair)
    whole = pl.BlockSpec((1, length, LANES), lambda j: (saved_place, 0, 0))
    grad = pl.BlockSpec((blocks, 1, rows // 2, LANES), lambda j: (0, grad_place, 0, 0))
    sent = (blocks, out_places, rows, 2 * LANES)
    out = pl.BlockSpec((blocks, 1, rows, 2 * LANES), lambda j: (0, out_place, 0, 0))
    return order.call(
        functools.partial(attend_back_kernel, size),
        "attend_back",
        (1,),
        [(array, whole) for array in saved]
        + [
            (tail_key, tail),
            (tail_value, tail),
            (mixture, whole),
            (packed_grad, grad),
            (pay, pl.BlockSpec((blocks, 1, rows, LANES), lambda j: (0, saved_place, 0, 1))),
        ],
        [(sent, BF16, out)],
        22,
        scratch=[
            pltpu.VMEM((length, LANES), BF16),
            pltpu.VMEM((LANES, length), F32),
            pltpu.VMEM((length, LANES), F32),
        ],
        before=before,
        carry=carry,
        after=after,
    )


def take_pair(refs, pair):
    owners = refs[0].shape[0]
    owner, place = lax.rem(pair, owners), lax.div(pair, owners)
    block, start = None, 0
    for ref in refs:
        here = ref[owner, jnp.clip(place - start, 0, ref.shape[1] - 1)]
        block = here if block is None else jnp.where(place >= start, here, block)
        start += ref.shape[1]
    return block


def group_of(heads, ref, first_pair, group, low_half):
    owners = ref.shape[0]

    def packed(head):
        if head >= heads:
            return jnp.zeros(ref.shape[2:], F32)
        pair = first_pair + head
        if isinstance(pair, int):
            return ref[pair % owners, pair // owners].astype(F32)
        return ref[lax.rem(pair, owners), lax.div(pair, owners)].astype(F32)

    return unpack_rows(low_half, packed(2 * group), packed(2 * group + 1))


def gate_kernel(heads, first, ap_ref, gl_ref, o_ref, sent_ref):
    rows, cols = o_ref.shape
    half_low = lanes_of(STRIP) < HEAD_SIZE
    pair = (first + pl.program_id(0)) * heads
    for group in range(cols // LANES):
        at = slice(group * LANES, (group + 1) * LANES)
        mixture = group_of(heads, ap_ref, pair, group, half_low)
        gated = (mixture * jax.nn.sigmoid(gl_ref[:, at])).astype(BF16)
        o_ref[:, at] = gated
        for z in range(sent_ref.shape[0]):
            sent_ref[z, :, at] = gated


def gate(order, heads, packed, gl, rows, first, count, copies, before):
    total, cols = gl.shape
    here = pl.BlockSpec((rows, cols), lambda i: (first + i, 0))
    return order.call(
        functools.partial(gate_kernel, heads, first),
        "gate",
        (count,),
        [(packed, pl.BlockSpec(packed.shape, lambda i: (0, 0, 0, 0))), (gl, here)],
        [
            ((total, cols), BF16, here),
            (
                (copies, count * rows, cols),
                BF16,
                pl.BlockSpec((copies, rows, cols), lambda i: (0, i, 0)),
            ),
        ],
        2 * count,
        before=before,
    )


def pack_kernel(*refs):
    out_ref, at = refs[-1], 0
    for ref in refs[:-1]:
        wide = ref.shape[1]
        out_ref[:, at : at + wide] = ref[...]
        at += wide


def pack(order, arrays):
    rows = arrays[0].shape[0]
    wide = sum(array.shape[1] for array in arrays)
    whole = lambda i: (0, 0)
    return order.call(
        pack_kernel,
        "pack",
        (1,),
        [(array, pl.BlockSpec(array.shape, whole)) for array in arrays],
        [((rows, wide), BF16, pl.BlockSpec((rows, wide), whole))],
        2,
    )[0]


def feed_kernel(
    parts,
    own,
    rank_ref,
    x_ref,
    dy_ref,
    wo_ref,
    wg_ref,
    wu_ref,
    wd_ref,
    wg_far_ref,
    wu_far_ref,
    wd_far_ref,
    gain_ref,
    *refs,
):
    o_ref, c_ref, u_ref, dgu_ref, hid_ref, out_ref, dc_ref, out_acc, dc_acc = refs
    step = pl.program_id(0)
    last = pl.num_programs(0) - 1

    def attended():
        return dot(o_ref[0], wo_ref[...], NT)

    @pl.when(step == 0)
    def _():
        hid_ref[...] = x_ref[...].astype(F32) + attended()

    @pl.when((step > 0) & (step < parts))
    def _():
        hid_ref[...] += attended()

    @pl.when(step == parts - 1)
    def _():
        hidden = hid_ref[...]
        c_ref[...] = (hidden * rms_factor(hidden) * gain_ref[...]).astype(BF16)
        out_acc[...] = jnp.zeros_like(out_acc)
        dc_acc[...] = jnp.zeros_like(dc_acc)

    def chunk(w_gate, w_up, w_down):
        c = c_ref[...]
        gr = dot(c, w_gate[...])
        ur = dot(c, w_up[...])
        sig = jax.nn.sigmoid(gr)
        silu = gr * sig
        u = (silu * ur).astype(BF16)
        du = dot(dy_ref[...], w_down[...])
        dgr = (du * ur * sig * (1.0 + gr * (1.0 - sig))).astype(BF16)
        dur = (du * silu).astype(BF16)
        out_acc[...] += dot(u, w_down[...], NT)
        dc_acc[...] += dot(dgr, w_gate[...], NT) + dot(dur, w_up[...], NT)
        return u, dgr, dur

    @pl.when((step >= parts) & (step < parts + own))
    def _():
        u, dgr, dur = chunk(wg_ref, wu_ref, wd_ref)
        wide = u.shape[1]
        u_ref[...] = u
        dgu_ref[:, :wide] = dgr
        dgu_ref[:, wide:] = dur

    @pl.when(step >= parts + own)
    def _():
        chunk(wg_far_ref, wu_far_ref, wd_far_ref)

    @pl.when(step == last)
    def _():
        out_ref[...] = out_acc[...].astype(BF16)
        dc_ref[...] = dc_acc[...].astype(BF16)


def feed(order, rank, x, dy, o_all, near, far, gain_row, ff, chunk, group, before):
    parts, rows, cols = o_all.shape
    total, width = x.shape
    own = ff // chunk
    offset = parts * cols // chunk
    others = (far.shape[1] - parts * cols) // (3 * ff)
    steps = parts + (1 + others) * own
    whole = lambda i, rank: (0, 0)
    here = lambda i, rank: (group, 0)
    early = lambda i: jnp.minimum(i, parts - 1)
    mine = lambda i: jnp.clip(i - parts, 0, own - 1)

    def near_strip(k):
        return pl.BlockSpec((width, chunk), lambda i, rank: (0, k * own + mine(i)))

    def far_strip(k):
        def place(i, rank):
            s = jnp.maximum(i - parts - own, 0)
            return (0, offset + (s // own * 3 + k) * own + s % own)

        return pl.BlockSpec((width, chunk), place)

    wide = pl.BlockSpec((rows, width), whole)
    return order.call(
        functools.partial(feed_kernel, parts, own),
        "feed",
        (steps,),
        [
            (x, pl.BlockSpec((rows, width), here)),
            (dy, pl.BlockSpec((rows, width), here)),
            (far, pl.BlockSpec((width, cols), lambda i, rank: (0, early(i)))),
            (near, near_strip(0)),
            (near, near_strip(1)),
            (near, near_strip(2)),
            (far, far_strip(0)),
            (far, far_strip(1)),
            (far, far_strip(2)),
            (gain_row, pl.BlockSpec((1, width), whole)),
        ]
        + [(o_all, pl.BlockSpec((1, rows, cols), lambda i, rank: (rank[0] ^ early(i), 0, 0)))],
        [
            ((total, width), BF16, pl.BlockSpec((rows, width), here)),
            ((total, ff), BF16, pl.BlockSpec((rows, chunk), lambda i, rank: (group, mine(i)))),
            (
                (total, 2 * ff),
                BF16,
                pl.BlockSpec((rows, 2 * chunk), lambda i, rank: (group, mine(i))),
            ),
            ((rows, width), F32, wide),
            ((rows, width), BF16, wide),
            ((rows, width), BF16, wide),
        ],
        37,
        scratch=[pltpu.VMEM((rows, width), F32), pltpu.VMEM((rows, width), F32)],
        before=before,
        scalars=(rank,),
    )


def norm_back(source, factor, gain_row, upstream):
    scaled = upstream * gain_row
    inner = jnp.mean(scaled * source, axis=-1, keepdims=True)
    return factor * scaled - source * (factor * factor * factor) * inner


def hidden_back_kernel(
    heads,
    first,
    start,
    with_old,
    dc_ref,
    dc_other_ref,
    hid_ref,
    dy_ref,
    gain_ref,
    w_ref,
    gl_ref,
    ap_ref,
    *refs,
):
    if with_old:
        old_ref, *refs = refs
    dhb_ref, dgl_ref, dh_ref, dg_ref, *dap_refs = refs
    rows, cols = gl_ref.shape
    pair = (first + pl.program_id(0)) * heads
    if with_old:

        @pl.when(pl.program_id(0) == 0)
        def _():
            dap_refs[0][...] = old_ref[...]

    hidden = hid_ref[...]
    factor = rms_factor(hidden)
    dc = dc_ref[...].astype(F32) + dc_other_ref[...].astype(F32)
    dh = dy_ref[...].astype(F32) + norm_back(hidden, factor, gain_ref[...], dc)
    dg_ref[0] = jnp.sum(dc * hidden * factor, axis=0, keepdims=True)
    dh_ref[...] = dh
    dhb = dh.astype(BF16)
    dhb_ref[...] = dhb
    gated_grad = dot(dhb, w_ref[...])
    half_low = lanes_of(STRIP) < HEAD_SIZE
    for group in range(cols // LANES):
        at = slice(group * LANES, (group + 1) * LANES)
        mixture = group_of(heads, ap_ref, pair, group, half_low)
        gate_value = jax.nn.sigmoid(gl_ref[:, at])
        grad = gated_grad[:, at]
        dgl_ref[:, at] = (grad * mixture * gate_value * (1.0 - gate_value)).astype(BF16)
        for half, packed in enumerate(pack_rows(half_low, grad * gate_value)):
            if 2 * group + half < heads:
                put_pair(dap_refs, pair + 2 * group + half, packed.astype(BF16), start=start)


def hidden_back(
    order, heads, dc, dc_other, hidden, dy, gain_row, weights, gl, packed, rows, first, places, old, before, carry
):
    total, cols = gl.shape
    group, width = dc.shape
    count = group // rows
    whole = lambda i: (0, 0)
    here = lambda i: (first + i, 0)
    part = pl.BlockSpec((rows, width), lambda i: (i, 0))
    every = lambda shape: pl.BlockSpec(shape, lambda i: (0,) * len(shape))
    sent = [(packed.shape[0], stop - start, rows // 2, LANES) for start, stop in places]
    return order.call(
        functools.partial(hidden_back_kernel, heads, first, places[0][0], bool(old)),
        "hidden_back",
        (count,),
        [
            (dc, part),
            (dc_other, part),
            (hidden, part),
            (dy, pl.BlockSpec((rows, width), here)),
            (gain_row, pl.BlockSpec((1, width), whole)),
            (weights, pl.BlockSpec((width, cols), whole)),
            (gl, pl.BlockSpec((rows, cols), here)),
            (packed, every(packed.shape)),
        ]
        + [(array, every(array.shape)) for array in old],
        [
            ((total, width), BF16, pl.BlockSpec((rows, width), here)),
            ((total, cols), BF16, pl.BlockSpec((rows, cols), here)),
            ((group, width), F32, part),
            ((count, 1, width), F32, pl.BlockSpec((1, 1, width), lambda i: (i, 0, 0))),
        ]
        + [(shape, BF16, every(shape)) for shape in sent],
        4 * count,
        before=before,
        carry=carry,
    )


def project_back_kernel(
    heads,
    first,
    arrays,
    upper_ref,
    raw_ref,
    x_ref,
    dgl_ref,
    w_ref,
    gq_ref,
    gk_ref,
    *refs,
):
    g_refs = refs[:arrays]
    grads_ref, *da_refs, sums_ref, all_ref, da_ref = refs[arrays:]
    first_pair = (first + pl.program_id(0)) * heads
    rows, cols = dgl_ref.shape
    width = x_ref.shape[1]
    lane = lanes_of(rows)
    low = lane < HEAD_SIZE
    zero = jnp.zeros(lane.shape, F32)
    sums = [jnp.zeros((1, LANES), F32), jnp.zeros((1, LANES), F32)]

    def head_back(raw, upstream, gain_row, which):
        factor = lax.rsqrt(per_head(low, raw * raw) + EPSILON)
        scaled = upstream * gain_row
        inner = per_head(low, scaled * raw)
        sums[which] += jnp.sum(upstream * raw * factor, axis=0, keepdims=True)
        return factor * scaled - raw * (factor * factor * factor) * inner

    forget = zero
    for group in range(cols // LANES):
        at = group * LANES
        here = slice(at, at + LANES)
        pair = (2 * group, 2 * group + 1)
        held = [take_pair(g_refs, first_pair + h).astype(F32) if h < heads else None for h in pair]
        both = [zero if block is None else block[:, :LANES] for block in held]
        rest = [zero if block is None else block[:, LANES:] for block in held]
        query = head_back(raw_ref[:, here], merge_pair(low, *both), gq_ref[...], 0)
        key = head_back(
            raw_ref[:, cols + at : cols + at + LANES],
            merge_swapped(low, *both),
            gk_ref[...],
            1,
        )
        all_ref[:, here] = query.astype(BF16)
        all_ref[:, cols + at : cols + at + LANES] = key.astype(BF16)
        value = merge_pair(low, *rest)
        all_ref[:, 2 * cols + at : 2 * cols + at + LANES] = value.astype(BF16)
        for h, block in zip(pair, rest):
            if h < heads:
                forget = jnp.where(lane == h, block[:, 64:65], forget)
    all_ref[:, 3 * cols : 4 * cols] = dgl_ref[...]
    all_ref[:, 4 * cols :] = forget.astype(BF16)
    grads_ref[:, : 3 * cols] = all_ref[:, : 3 * cols]
    grads_ref[:, 3 * cols :] = all_ref[:, 4 * cols :]
    da = dot(all_ref[...], w_ref[...], NT)
    da_ref[...] = da
    half = rows // 2
    upper = upper_ref[0]
    for ref, part in zip(da_refs, (upper, 1 - upper)):
        ref[0] = da_ref[pl.ds(pl.multiple_of(part * half, half), half), :].astype(BF16)
    x = x_ref[...].astype(F32)
    sums_ref[0, :, :width] = jnp.sum(da * x * rms_factor(x), axis=0, keepdims=True)
    sums_ref[0, :, width : width + LANES] = sums[0]
    sums_ref[0, :, width + LANES : width + 2 * LANES] = sums[1]
    sums_ref[0, :, width + 2 * LANES :] = jnp.sum(forget, axis=0, keepdims=True)


def project_back(
    order, heads, upper, returned, raw, x, dgl, weights, gq_row, gk_row, rows, first, count, before, after, carry
):
    total, cols = dgl.shape
    width, wide = weights.shape
    half = rows // 2
    whole = lambda i, upper: (0, 0)
    here = lambda i, upper: (first + i, 0)
    row = pl.BlockSpec((1, LANES), whole)
    sums = width + 3 * LANES
    da = [((count, half, width), BF16, pl.BlockSpec((1, half, width), lambda i, upper: (i, 0, 0)))] * 2
    return order.call(
        functools.partial(project_back_kernel, heads, first, len(returned)),
        "project_back",
        (count,),
        [
            (raw, pl.BlockSpec((rows, 2 * cols), here)),
            (x, pl.BlockSpec((rows, width), here)),
            (dgl, pl.BlockSpec((rows, cols), here)),
            (weights, pl.BlockSpec((width, wide), whole)),
            (gq_row, row),
            (gk_row, row),
        ]
        + [(array, pl.BlockSpec(array.shape, lambda i, upper: (0, 0, 0, 0))) for array in returned],
        [((total, wide - cols), BF16, pl.BlockSpec((rows, wide - cols), here))]
        + da
        + [((count, 1, sums), F32, pl.BlockSpec((1, 1, sums), lambda i, upper: (i, 0, 0)))],
        6 * count,
        scratch=[pltpu.VMEM((rows, wide), BF16), pltpu.VMEM((rows, width), F32)],
        before=before,
        scalars=(upper,),
        after=after,
        carry=carry,
    )


def input_back_kernel(rank_ref, x_ref, dh_ref, gain_ref, own_ref, *refs):
    *passed, out_ref = refs
    rank, count = rank_ref[0], len(passed) + 1
    da = own_ref[0].astype(F32)
    for t, ref in enumerate(passed):
        taken = jnp.where(pl.program_id(1) == 0, rank == t + 1, rank == count - 2 - t)
        da = jnp.where(taken, ref[0].astype(F32), da)
    x = x_ref[...].astype(F32)
    out_ref[...] = dh_ref[...] + norm_back(x, rms_factor(x), gain_ref[...], da)


def input_back(order, rank, summed, x, dh, gain_row, rows, first, before, after):
    total, width = x.shape
    size, half, _ = summed[0].shape
    here = pl.BlockSpec((half, width), lambda m, i, rank: (2 * (first + m) + i, 0))
    one = pl.BlockSpec((half, width), lambda m, i, rank: (2 * m + i, 0))
    passing = pl.BlockSpec((1, half, width), lambda m, i, rank: (m, 0, 0))
    return order.call(
        input_back_kernel,
        "input_back",
        (size, 2),
        [(x, here), (dh, one), (gain_row, pl.BlockSpec((1, width), lambda m, i, rank: (0, 0)))]
        + [(block, passing) for block in summed],
        [((total, width), F32, here)],
        4 * size,
        before=before,
        scalars=(rank,),
        after=after,
    )


def layer_out_kernel(hid_ref, part_ref, other_ref, out_ref):
    total = hid_ref[...] + (part_ref[...].astype(F32) + other_ref[...].astype(F32))
    out_ref[...] = total.astype(BF16)


def layer_output(order, hidden, part, other, group, total, before, after):
    rows, width = hidden.shape
    tiles = 4
    tile = rows // tiles
    one = pl.BlockSpec((tile, width), lambda i: (i, 0))
    return order.call(
        layer_out_kernel,
        "layer_out",
        (tiles,),
        [(hidden, one), (part, one), (other, one)],
        [((total, width), BF16, pl.BlockSpec((tile, width), lambda i: (tiles * group + i, 0)))],
        4,
        before=before,
        after=after,
    )


def pad_to(array, size, axis):
    missing = size - array.shape[axis]
    if missing == 0:
        return array
    widths = [(0, missing if i == axis else 0) for i in range(array.ndim)]
    return jnp.pad(array, widths)


def turned_kernel(*refs):
    out_ref, at = refs[-1], 0
    for left_ref, right_ref in zip(refs[:-1:2], refs[1:-1:2]):
        wide = right_ref.shape[1]
        product = lax.dot_general(
            left_ref[...], right_ref[...], (((0,), (0,)), ((), ())), preferred_element_type=F32
        )
        out_ref[:, at : at + wide] = product.astype(BF16)
        at += wide


def turned_products(order, pairs, us):
    height = pairs[0][0].shape[1]
    tile = 256
    ins, wide = [], 0
    for left, right in pairs:
        ins.append((left, pl.BlockSpec((left.shape[0], tile), lambda i: (0, i))))
        ins.append((right, pl.BlockSpec(right.shape, lambda i: (0, 0))))
        wide += right.shape[1]
    return order.call(
        turned_kernel,
        "turned_products",
        (height // tile,),
        ins,
        [((height, wide), BF16, pl.BlockSpec((tile, wide), lambda i: (i, 0)))],
        us,
    )[0]


def owned_kernel(own, left_ref, right_ref, sums_ref, out_ref):
    product = lax.dot_general(
        left_ref[...], right_ref[...], (((0,), (0,)), ((), ())), preferred_element_type=F32
    ).astype(BF16)
    for i in range(out_ref.shape[0]):
        out_ref[i, :own] = product[i * own : (i + 1) * own]
        out_ref[i, own:] = sums_ref[i]


def owned_product(order, left, right, sums, us, carry):
    rows, height = left.shape
    owners, extra, wide = sums.shape
    own = height // owners
    step = 1
    while own * step % LANES:
        step += 1
    return order.call(
        functools.partial(owned_kernel, own),
        "owned_product",
        (owners // step,),
        [
            (left, pl.BlockSpec((rows, own * step), lambda i: (0, i))),
            (right, pl.BlockSpec((rows, wide), lambda i: (0, 0))),
            (sums, pl.BlockSpec((step, extra, wide), lambda i: (i, 0, 0))),
        ],
        [((owners, own + extra, wide), BF16, pl.BlockSpec((step, own + extra, wide), lambda i: (i, 0, 0)))],
        us,
        carry=carry,
    )


def line_steps(count):
    return [((t - 1, t), (count - t, count - 1 - t)) for t in range(1, count)]


def fold_kernel(*refs):
    count = len(refs) // 3
    for i in range(count):
        total = refs[2 * i][...].astype(F32) + refs[2 * i + 1][...].astype(F32)
        refs[2 * count + i][...] = total.astype(BF16)


def fold(order, pairs, after):
    size, rows, width = pairs[0][0].shape
    block = pl.BlockSpec((1, rows, width), lambda i: (i, 0, 0))
    return order.call(
        fold_kernel,
        "fold",
        (size,),
        [(array, block) for pair in pairs for array in pair],
        [((size, rows, width), BF16, block) for _ in pairs],
        0.2 * len(pairs),
        after=after,
    )


def exchanged(array, axis, flip):
    count = lax.axis_size(axis)
    return lax.ppermute(array, axis, [(i, i ^ flip) for i in range(count)])


def to_all(array, axis):
    return lax.all_to_all(array, axis, 0, 0, tiled=True)


def small_sum(row, axis):
    flip = 1
    while flip < lax.axis_size(axis):
        row = row + exchanged(row, axis, flip)
        flip *= 2
    return row


def shards(
    inputs,
    cotangent,
    tail_keys,
    tail_values,
    tail_forget,
    gain_one,
    gain_two,
    w_query,
    w_key,
    w_value,
    w_forget,
    forget_bias,
    query_gain,
    key_gain,
    w_outgate,
    w_out,
    w_gate,
    w_up,
    w_down,
):
    micros, rows, width = inputs.shape
    total = micros * rows
    own_cols = w_query.shape[1]
    heads = w_forget.shape[1]
    ff = w_gate.shape[1]
    seq_count = lax.axis_size("seq")
    head_count = lax.axis_size("head")
    seq_rank = lax.axis_index("seq")
    head_rank = lax.axis_index("head")
    cols = -(-own_cols // LANES) * LANES
    pair_total = micros * heads
    pairs = -(-pair_total // seq_count)
    padded_pairs = pairs * seq_count
    tail_length = tail_keys.shape[1]

    x = inputs.reshape(total, width)
    dy = cotangent.reshape(total, width)

    small = jnp.concatenate([w_forget, gain_one[:, None], gain_two[:, None]], axis=1)
    first_shard = jnp.concatenate(
        [pad_to(w, cols, 1) for w in (w_query, w_key, w_value, w_outgate)]
        + [pad_to(small, LANES, 1)],
        axis=1,
    )
    first = lax.all_gather(first_shard, "seq", axis=0, tiled=True)
    near_shard = jnp.concatenate([w_gate, w_up, w_down.T], axis=1)
    near = lax.all_gather(near_shard, "seq", axis=0, tiled=True)
    split = 3 * ff // 2
    outs, units, early = [pad_to(w_out.T, cols, 1)], [(near_shard[:, :split], near_shard[:, split:])], []
    flip = 1
    while flip < head_count:
        outs.append(exchanged(jnp.concatenate(outs, axis=1), "head", flip))
        if flip == 1:
            early.append(outs[-1])
        else:
            units += [tuple(exchanged(part, "head", flip) for part in unit) for unit in units]
        flip *= 2
    far_parts = outs + [part for unit in units[1:] for part in unit]
    rank = head_rank.astype(jnp.int32)[None]
    upper = (rank >= head_count // 2).astype(jnp.int32)
    order = Order()
    gain_one_row = first[:, 4 * cols + heads].astype(F32)[None, :]
    gain_two_row = first[:, 4 * cols + heads + 1].astype(F32)[None, :]
    bias_here = lax.dynamic_slice_in_dim(forget_bias, head_rank * heads, heads, 0)
    bias_row = pad_to(bias_here[None, :], LANES, 1)
    gq_row = jnp.tile(query_gain.astype(F32), 2)[None, :]
    gk_row = jnp.tile(key_gain.astype(F32), 2)[None, :]

    tail_key_parts, tail_value_parts = [], []
    for j in range(pairs):
        p = jnp.minimum(j * seq_count + seq_rank, pair_total - 1)
        m, h = p // heads, p % heads
        tail_of = lambda array, wide: lax.dynamic_slice(
            array, (m, 0, h * wide), (1, tail_length, wide)
        )[0]
        forget = tail_of(tail_forget, 1)
        decay = jnp.cumsum(forget, axis=0) - jnp.sum(forget, axis=0, keepdims=True)
        high = lax.reduce_precision(decay, 8, 7)
        middle = lax.reduce_precision(decay - high, 8, 7)
        least = decay - high - middle
        ones = jnp.ones((tail_length, 3), BF16)
        parts = jnp.concatenate([-high, -middle, -least], axis=1).astype(BF16)
        tail_key_parts.append(
            pad_to(jnp.concatenate([tail_of(tail_keys, HEAD_SIZE), ones, parts], axis=1), LANES, 1)
        )
        tail_value_parts.append(
            pad_to(jnp.concatenate([tail_of(tail_values, HEAD_SIZE), ones], axis=1), LANES, 1)
        )
    tail_key, tail_value = jnp.stack(tail_key_parts), jnp.stack(tail_value_parts)

    a, raw, gl, *pays = project(
        order, heads, cols, seq_count, x, first, bias_row, gain_one_row, gq_row, gk_row, micros, early
    )
    pays = [to_all(pay, "seq") for pay in pays]
    kept, returned = [], []
    most = max(pairs - 1, 1)
    for j, pay in enumerate(pays):
        in_most = j < most
        packed, *saved = attend(
            order,
            pay,
            tail_key,
            tail_value,
            j,
            most if in_most else pairs - most,
            j if in_most else j - most,
            (packed,) if 0 < j < most else (),
        )
        kept.append((saved, pay, 0))
        if j >= most - 1:
            returned.append(to_all(packed, "seq"))
        if j == 0:
            far = lax.all_gather(pack(order, far_parts), "seq", axis=0, tiled=True)
    packed = jnp.concatenate(returned, axis=1)

    size = 2 if micros % 2 == 0 else 1
    groups = micros // size
    chunk = min(512, ff)
    gated, o_alls = (), []
    for g in range(groups):
        enough = (g + 1) * size * heads <= most * seq_count
        *gated, sent = gate(
            order, heads, returned[0] if enough else packed, gl, rows, g * size, size, head_count, gated
        )
        o_alls.append(to_all(sent, "head"))
    o = gated[0]

    hiddens, out_parts, dc_parts, dc_others = [], [], [], []
    dhs, gains_two = [], []
    late, carried = (), None
    early_places = size * heads // seq_count if groups > 1 else 0
    fed, backed = (), ()

    def back_to_heads(g, carry=()):
        nonlocal backed, late, carried
        places = [(early_places, pairs)]
        if g == 0 and early_places > 0:
            places = [(0, early_places)] + places
        *results, out_parts[g] = hidden_back(
            order,
            heads,
            dc_parts[g],
            dc_others[g],
            hiddens[g],
            dy,
            gain_two_row,
            far,
            gl,
            packed,
            rows,
            g * size,
            places,
            late,
            backed,
            carry + (out_parts[g],),
        )
        if carry:
            carried = results.pop()
        dhb, dgl, dh, gain, *sent = results
        backed, late = (dhb, dgl), (sent[-1],)
        dhs.append(dh)
        gains_two.append(gain)
        return sent[0]

    def scattered(grad):
        return lax.psum_scatter(grad, "seq", scatter_dimension=0, tiled=True)

    for g in range(groups):
        *fed, hidden, out_part, dc_part = feed(
            order, rank, x, dy, o_alls[g], near, far, gain_two_row, ff, chunk, g, fed
        )
        hiddens.append(hidden)
        out_parts.append(out_part)
        dc_parts.append(dc_part)
        dc_others.append(exchanged(dc_part, "head", 1))
        if g > 0:
            early_grads = back_to_heads(g - 1)
    c, u, dgu = fed
    unit_grads = scattered(turned_products(order, [(c, dgu), (dy, u)], 13))

    layer_out = ()

    def put_out(g, after=()):
        nonlocal layer_out
        other = exchanged(out_parts[g], "head", 1)
        layer_out = layer_output(order, hiddens[g], out_parts[g], other, g, total, layer_out, after)

    if early_places > 0:
        early_grads = to_all(early_grads, "seq")
    returned = []
    mixed, grad = (), ()
    for j in range(pairs):
        if j == early_places:
            back_to_heads(groups - 1)
            mixed = (turned_products(order, [(backed[0], o), (a, backed[1])], 8),)
            late_grads = to_all(late[0], "seq")
        sent = (early_grads, j) if j < early_places else (late_grads, j - early_places)
        saved, pay, place = kept[j]
        grad, *mixed = attend_back(
            order,
            saved[1:],
            tail_key,
            tail_value,
            saved[0],
            sent[0],
            pay,
            j,
            place,
            sent[1],
            most if j < most else pairs - most,
            j if j < most else j - most,
            (grad,) if 0 < j < most else (),
            tuple(mixed),
            (),
        )
        if j >= most - 1:
            returned.append(to_all(grad, "seq"))

    for out in range(groups):
        put_out(out)

    grads, streams, gains_one = (), [], []
    for g in range(groups):
        results = project_back(
            order,
            heads,
            upper,
            returned[:1] if (g + 1) * size * heads <= most * seq_count else returned,
            raw,
            x,
            backed[1],
            first,
            gq_row,
            gk_row,
            rows,
            g * size,
            size,
            grads,
            (unit_grads,) if g == 0 else (),
            mixed,
        )
        grads, da, gain, mixed = results[:1], results[1:3], results[3], results[4:]
        gains_one.append(gain)
        streams.append(da)

    hops = line_steps(head_count)
    moving = [sent for _, sent in streams]
    passed = [[] for _ in streams]
    for step in range(1, head_count + groups - 1):
        active = [(g, step - g) for g in range(groups) if 1 <= step - g < head_count]
        terms = []
        for g, t in active:
            kept, sent = streams[g]
            terms.append((lax.ppermute(moving[g], "head", hops[t - 1]), sent if t < head_count // 2 else kept))
        waited = tuple(blocks[-1] for blocks in passed if len(blocks) > 1)
        for (g, t), total_now in zip(active, fold(order, terms, waited)):
            moving[g] = total_now
            if t == head_count - 1:
                passed[g].append(total_now)
        if step == 1:
            one_sums = jnp.sum(jnp.concatenate(gains_one, axis=0), axis=0)
            two_sums = jnp.sum(jnp.concatenate(gains_two, axis=0), axis=0) * (1.0 / head_count)
            own_rows = gain_one.shape[0]
            shared = pad_to(one_sums[:, width:], 3 * LANES, 1)
            owned_sums = jnp.concatenate(
                [
                    one_sums[:, :width].reshape(seq_count, own_rows),
                    two_sums.reshape(seq_count, own_rows),
                    jnp.broadcast_to(shared, (seq_count, 3 * LANES)),
                ],
                axis=1,
            ).astype(BF16)
            owned_sums = jnp.pad(owned_sums[:, None], ((0, 0), (0, 15), (0, grads[0].shape[1] - owned_sums.shape[1])))
            head_grads, *mixed = owned_product(order, a, grads[0], owned_sums, 9, mixed)
            mixed_grads = scattered(mixed[0]) if mixed else mixed_grads
        for g in range(groups):
            if passed[g] and len(passed[g]) <= head_count - 1:
                passed[g].append(lax.ppermute(passed[g][-1], "head", hops[len(passed[g]) - 1]))
    for blocks in passed:
        while len(blocks) < head_count:
            blocks.append(lax.ppermute(blocks[-1], "head", hops[len(blocks) - 1]))

    head_grads = jnp.sum(to_all(head_grads, "seq").astype(F32), axis=0)
    sums = head_grads[own_rows : own_rows + 1]
    head_grads = head_grads[:own_rows]
    unit_grads, mixed_grads = unit_grads.astype(F32), mixed_grads.astype(F32)
    strips = [unit_grads[:, i * chunk : (i + 1) * chunk] for i in range(2 * ff // chunk)]
    grad_gate = jnp.concatenate(strips[0::2], axis=1)
    grad_up = jnp.concatenate(strips[1::2], axis=1)
    grad_down = unit_grads[:, 2 * ff :].T
    grad_out = mixed_grads[:, :own_cols].T

    gain_lanes = 2 * own_rows
    bias_at = gain_lanes + 2 * LANES
    bias_full = lax.dynamic_update_slice(
        jnp.zeros((1, forget_bias.shape[0]), F32), sums[:, bias_at : bias_at + heads], (0, head_rank * heads)
    )
    sums = small_sum(jnp.concatenate([sums[:, :bias_at], bias_full], axis=1), "head")[0]
    halves = sums[gain_lanes:bias_at].reshape(4, HEAD_SIZE)
    gq_total, gk_total = halves[0] + halves[1], halves[2] + halves[3]
    bias_total = sums[bias_at:]

    input_grad = ()
    for g in range(groups):
        input_grad = input_back(
            order,
            rank,
            passed[g],
            x,
            dhs[g],
            gain_one_row,
            rows,
            g * size,
            input_grad,
            (sums[None],) if g == groups - 1 else (),
        )

    input_grad, layer_out = input_grad[0], layer_out[0]
    shape = inputs.shape
    return (
        layer_out.reshape(shape),
        input_grad.reshape(shape),
        sums[:own_rows],
        sums[own_rows:gain_lanes],
        head_grads[:, :own_cols],
        head_grads[:, cols : cols + own_cols],
        head_grads[:, 2 * cols : 2 * cols + own_cols],
        head_grads[:, 3 * cols : 3 * cols + heads],
        bias_total,
        gq_total,
        gk_total,
        mixed_grads[:, cols : cols + own_cols],
        grad_out,
        grad_gate,
        grad_up,
        grad_down,
    )


def solution(mesh):
    by_rows = P("seq", "head")
    by_cols = P("head", "seq")
    placed = (
        P(None, "seq", None),
        P(None, "seq", None),
        P(None, None, "head"),
        P(None, None, "head"),
        P(None, None, "head"),
        P("seq"),
        P("seq"),
        by_rows,
        by_rows,
        by_rows,
        by_rows,
        P(),
        P(),
        P(),
        by_rows,
        by_cols,
        by_rows,
        by_rows,
        by_cols,
    )
    return jax.shard_map(
        shards,
        mesh=mesh,
        in_specs=placed,
        out_specs=(
            P(None, "seq", None),
            P(None, "seq", None),
            P("seq"),
            P("seq"),
            by_rows,
            by_rows,
            by_rows,
            by_rows,
            P(),
            P(),
            P(),
            by_rows,
            by_cols,
            by_rows,
            by_rows,
            by_cols,
        ),
        check_vma=False,
    )
```

```python
import functools

import jax
import jax.numpy as jnp
from jax import lax
from jax.experimental import pallas as pl
from jax.experimental.pallas import tpu as pltpu
from jax.sharding import PartitionSpec as P

HEAD_SIZE = 64
LANES = 128
EPSILON = 1e-06
F32 = jnp.float32
BF16 = jnp.bfloat16
NN = (((1,), (0,)), ((), ()))
NT = (((1,), (1,)), ((), ()))
HIDE = -1e30
SCALE = HEAD_SIZE**-0.5
STRIP = 64
MIB = 1024 * 1024


def dot(left, right, dims=NN):
    return lax.dot_general(left, right, dims, preferred_element_type=F32)


def params():
    return pltpu.CompilerParams(vmem_limit_bytes=60 * MIB)


def linked(kernel, inputs, extra, outputs, carried):
    def body(*refs):
        first = inputs + extra
        token = refs[first + outputs + carried]
        token[...] = jnp.zeros_like(token)
        kernel(*refs[:inputs], *refs[first : first + outputs], *refs[first + outputs + carried + 1 :])

    return body


class Order:
    def __init__(self):
        self.tokens = []

    def call(
        self, kernel, name, grid, ins, outs, us, scratch=(), before=(), scalars=(), after=(), carry=()
    ):
        arrays = list(scalars) + [array for array, _ in ins]
        extra = list(before) + list(carry) + list(after) + self.tokens
        count = len(arrays)
        whole = lambda *at: (0, 0)
        anywhere = pl.BlockSpec(memory_space=pl.ANY)
        out_specs = [spec for _, _, spec in outs] + [anywhere] * len(carry)
        out_specs.append(pl.BlockSpec((8, LANES), whole))
        out_shape = [jax.ShapeDtypeStruct(shape, kind) for shape, kind, _ in outs]
        out_shape += [jax.ShapeDtypeStruct(array.shape, array.dtype) for array in carry]
        out_shape.append(jax.ShapeDtypeStruct((8, LANES), F32))
        aliases = {count + i: i for i in range(len(before))}
        for i in range(len(carry)):
            aliases[count + len(before) + i] = len(outs) + i
        *results, token = pl.pallas_call(
            linked(kernel, count, len(extra), len(outs), len(carry)),
            grid_spec=pltpu.PrefetchScalarGridSpec(
                num_scalar_prefetch=len(scalars),
                grid=grid,
                in_specs=[spec for _, spec in ins] + [anywhere] * len(extra),
                out_specs=out_specs,
                scratch_shapes=list(scratch),
            ),
            out_shape=out_shape,
            input_output_aliases=aliases,
            compiler_params=params(),
            cost_estimate=pl.CostEstimate(flops=int(us * 8e9), bytes_accessed=0, transcendentals=0),
            name=name,
        )(*arrays, *extra)
        self.tokens = [token]
        return results


def lanes_of(rows):
    return lax.broadcasted_iota(jnp.int32, (rows, LANES), 1)


def swap_halves(block):
    return pltpu.roll(block, HEAD_SIZE, 1)


def in_three(value):
    high = value.astype(BF16).astype(F32)
    rest = value - high
    middle = rest.astype(BF16).astype(F32)
    return high, middle, rest - middle


def at_lanes(lane, first, parts, base):
    for place, part in enumerate(parts):
        base = jnp.where(lane == first + place, part, base)
    return base


def triangle(rows, lower):
    down = lax.broadcasted_iota(jnp.int32, (rows, rows), 0)
    across = lax.broadcasted_iota(jnp.int32, (rows, rows), 1)
    return jnp.where(down >= across if lower else down <= across, 1.0, 0.0).astype(BF16)


def running_sum(tri, column, lane):
    spread = at_lanes(lane, 0, in_three(column), jnp.zeros(lane.shape, F32))
    sums = dot(tri, spread.astype(BF16))
    return sums[:, 0:1] + sums[:, 1:2] + sums[:, 2:3]


def forget_column(tail_block):
    return tail_block[:, 64:65] + tail_block[:, 65:66] + tail_block[:, 66:67]


def per_head(low, values):
    first = jnp.sum(jnp.where(low, values, 0.0), axis=-1, keepdims=True)
    second = jnp.sum(jnp.where(low, 0.0, values), axis=-1, keepdims=True)
    return jnp.where(low, first, second) * (1.0 / HEAD_SIZE)


def rms_factor(values):
    return lax.rsqrt(jnp.mean(values * values, axis=-1, keepdims=True) + EPSILON)


def merge_pair(low, first, second):
    return jnp.where(low, first, swap_halves(second))


def merge_swapped(low, first, second):
    return jnp.where(low, swap_halves(first), second)


def put_pair(refs, pair, block, column=0, start=0):
    owners = refs[0].shape[0]
    owner, place = lax.rem(pair, owners), lax.div(pair, owners)
    width = block.shape[1]
    for ref in refs:
        stop = start + ref.shape[1]

        @pl.when((place >= start) & (place < stop))
        def _(ref=ref, start=start):
            ref[owner, place - start, :, column : column + width] = block

        start = stop


def unpack_rows(low_half, first, second):
    strip = low_half.shape[0]
    rows = []
    for at in range(0, first.shape[0], strip):
        one, two = first[at : at + strip], second[at : at + strip]
        rows.append(jnp.where(low_half, one, swap_halves(two)))
        rows.append(jnp.where(low_half, swap_halves(one), two))
    return jnp.concatenate(rows, axis=0)


def pack_rows(low_half, block):
    strip = low_half.shape[0]
    first, second = [], []
    for at in range(0, block.shape[0], 2 * strip):
        top, bottom = block[at : at + strip], block[at + strip : at + 2 * strip]
        first.append(jnp.where(low_half, top, swap_halves(bottom)))
        second.append(jnp.where(low_half, swap_halves(top), bottom))
    return jnp.concatenate(first, axis=0), jnp.concatenate(second, axis=0)


def project_kernel(
    heads, idle, x_ref, w_ref, bias_ref, gain_ref, gq_ref, gk_ref, a_ref, raw_ref, gl_ref, *pay_refs
):
    x = x_ref[...].astype(F32)
    rows = x.shape[0]
    cols = gl_ref.shape[1]
    a = (x * rms_factor(x) * gain_ref[...]).astype(BF16)
    a_ref[...] = a
    proj = dot(a, w_ref[...])
    raw_ref[...] = proj[:, : 2 * cols]
    gl_ref[...] = proj[:, 3 * cols : 4 * cols]
    logit = proj[:, 4 * cols :] + bias_ref[...]
    lane = lanes_of(rows)
    low = lane < HEAD_SIZE
    for group in range(cols // LANES):
        at = group * LANES
        query = proj[:, at : at + LANES]
        key = proj[:, cols + at : cols + at + LANES]
        value = proj[:, 2 * cols + at : 2 * cols + at + LANES]
        query = query * lax.rsqrt(per_head(low, query * query) + EPSILON) * gq_ref[...]
        key = key * lax.rsqrt(per_head(low, key * key) + EPSILON) * gk_ref[...]
        for half in range(2):
            head = 2 * group + half
            if head >= heads:
                continue
            zl = at_lanes(lane, 64, in_three(logit[:, head : head + 1]), jnp.zeros(lane.shape, F32))
            if half == 0:
                both = merge_pair(low, query, key)
                rest = jnp.where(low, value, zl)
            else:
                both = merge_swapped(low, query, key)
                rest = jnp.where(low, swap_halves(value), zl)
            pair = pl.program_id(0) * heads + head
            put_pair(pay_refs, pair, jnp.concatenate([both, rest], axis=1).astype(BF16))

    @pl.when(pl.program_id(0) == 0)
    def _():
        for pair in idle:
            put_pair(pay_refs, pair, jnp.zeros((rows, 2 * LANES), BF16))


def project(order, heads, cols, owners, x, weights, bias_row, gain_row, gq_row, gk_row, micros, after):
    total, width = x.shape
    rows = total // micros
    wide = weights.shape[1]
    whole = lambda m: (0, 0)
    part = lambda m: (m, 0)
    row = pl.BlockSpec((1, LANES), whole)
    pairs = -(-micros * heads // owners)
    idle = range(micros * heads, pairs * owners)
    parts = [1] * pairs
    sent = [(owners, part, rows, 2 * LANES) for part in parts]
    return order.call(
        functools.partial(project_kernel, heads, idle),
        "project",
        (micros,),
        [
            (x, pl.BlockSpec((rows, width), part)),
            (weights, pl.BlockSpec((width, wide), whole)),
            (bias_row, row),
            (gain_row, pl.BlockSpec((1, width), whole)),
            (gq_row, row),
            (gk_row, row),
        ],
        [
            ((total, width), BF16, pl.BlockSpec((rows, width), part)),
            ((total, 2 * cols), F32, pl.BlockSpec((rows, 2 * cols), part)),
            ((total, cols), F32, pl.BlockSpec((rows, cols), part)),
        ]
        + [(shape, BF16, pl.BlockSpec(shape, lambda m: (0, 0, 0, 0))) for shape in sent],
        13,
        after=after,
    )


def attend_kernel(size, pay_ref, tk_ref, tv_ref, ap_ref, af_ref, q_ref, k_ref, v_ref):
    blocks, _, rows, _ = pay_ref.shape
    length = blocks * rows
    lane = lanes_of(rows)
    low = lane < HEAD_SIZE
    tri = triangle(rows, True)
    zero = jnp.zeros(lane.shape, F32)

    def build(b, carry):
        at = pl.ds(pl.multiple_of(b * rows, rows), rows)
        both = pay_ref[b, 0, :, :LANES].astype(F32)
        rest = pay_ref[b, 0, :, LANES:].astype(F32)
        logit = forget_column(rest)
        log_forget = jnp.minimum(logit, 0.0) - jnp.log1p(jnp.exp(-jnp.abs(logit)))
        decay = running_sum(tri, log_forget, lane) + carry
        high, middle, least = in_three(decay)
        query_side = at_lanes(lane, 64, (high, middle, least, 1.0, 1.0, 1.0), zero)
        key_side = at_lanes(lane, 64, (1.0, 1.0, 1.0, -high, -middle, -least), zero)
        value_side = at_lanes(lane, 64, (1.0, 1.0, 1.0), zero)
        q_ref[0, at, :] = jnp.where(low, both * SCALE, query_side).astype(BF16)
        k_ref[0, at, :] = jnp.where(low, swap_halves(both), key_side).astype(BF16)
        v_ref[0, at, :] = jnp.where(low, rest, value_side).astype(BF16)
        return decay[rows - 1 :, :]

    lax.fori_loop(0, blocks, build, jnp.zeros((1, 1), F32))

    tail_length = tk_ref.shape[1]
    visible = lax.broadcasted_iota(jnp.int32, (size, size), 0) >= lax.broadcasted_iota(
        jnp.int32, (size, size), 1
    )
    half_low = lanes_of(STRIP) < HEAD_SIZE
    lane_here = lanes_of(size)

    def one_block(qi):
        at = pl.ds(qi * size, size)
        query = q_ref[0, at, :]

        def absorb(key, value, total, masked=False):
            scores = dot(query, key, NT)
            if masked:
                scores = jnp.where(visible, scores, HIDE)
            return total + dot(jnp.exp(scores).astype(BF16), value)

        total = jnp.zeros((size, LANES), F32)
        for t in range(tail_length // size):
            here = pl.ds(t * size, size)
            total = absorb(tk_ref[0, here, :], tv_ref[0, here, :], total)

        for ki in range(qi):
            here = pl.ds(ki * size, size)
            total = absorb(k_ref[0, here, :], v_ref[0, here, :], total)
        total = absorb(k_ref[0, at, :], v_ref[0, at, :], total, True)
        weight = total[:, 64:65]
        mixture = total / weight
        af_ref[0, at, :] = mixture
        for piece in range(size // rows):
            block = mixture[piece * rows : (piece + 1) * rows]
            packed, _ = pack_rows(half_low, block)
            ap_ref[qi * (size // rows) + piece, 0] = packed.astype(BF16)
        old = query.astype(F32)
        shifted = forget_column(old) - jnp.log(weight)
        q_ref[0, at, :] = at_lanes(lane_here, 64, in_three(shifted), old).astype(BF16)

    for qi in range(length // size):
        one_block(qi)


def attend(order, pay, tail_key, tail_value, first, out_places, out_place, before):
    blocks, pairs, rows, _ = pay.shape
    length = blocks * rows
    tail_length = tail_key.shape[1]
    size = min(512, length)
    pair = lambda j: (j, 0, 0)
    across = lambda j: (0, j, 0, 0)
    tail = pl.BlockSpec((1, tail_length, LANES), lambda j: (first + j, 0, 0))
    whole = pl.BlockSpec((1, length, LANES), pair)
    return order.call(
        functools.partial(attend_kernel, size),
        "attend",
        (pairs,),
        [
            (pay, pl.BlockSpec((blocks, 1, rows, 2 * LANES), across)),
            (tail_key, tail),
            (tail_value, tail),
        ],
        [
            (
                (blocks, out_places, rows // 2, LANES),
                BF16,
                pl.BlockSpec((blocks, 1, rows // 2, LANES), lambda j: (0, out_place, 0, 0)),
            ),
            ((pairs, length, LANES), F32, whole),
            ((pairs, length, LANES), BF16, whole),
            ((pairs, length, LANES), BF16, whole),
            ((pairs, length, LANES), BF16, whole),
        ],
        14 * pairs,
        before=before,
    )


def attend_back_kernel(
    size,
    q_ref,
    k_ref,
    v_ref,
    tk_ref,
    tv_ref,
    af_ref,
    dap_ref,
    rest_ref,
    g_ref,
    da_ref,
    dqt_ref,
    sums_ref,
):
    blocks, _, rows, _ = rest_ref.shape
    length = blocks * rows
    lane = lanes_of(rows)
    low = lane < HEAD_SIZE
    zero = jnp.zeros(lane.shape, F32)

    def build(b, carry):
        at = pl.ds(pl.multiple_of(b * rows, rows), rows)
        packed = dap_ref[b, 0].astype(F32)
        strips = []
        for strip in range(0, packed.shape[0], STRIP):
            strips += [packed[strip : strip + STRIP], swap_halves(packed[strip : strip + STRIP])]
        grad = jnp.where(low, jnp.concatenate(strips, axis=0), 0.0)
        delta = jnp.sum(grad * af_ref[0, at, :], axis=-1, keepdims=True)
        da_ref[at, :] = at_lanes(lane, 64, in_three(-delta), grad).astype(BF16)
        return carry

    lax.fori_loop(0, blocks, build, 0)

    across = lax.broadcasted_iota(jnp.int32, (size, size), 1)
    down = lax.broadcasted_iota(jnp.int32, (size, size), 0)
    visible = across >= down
    count = length // size

    def block_at(i):
        return pl.ds(i * size, size)

    def pieces(key, value, at, masked=False):
        scores = dot(key, q_ref[0, at, :], NT)
        if masked:
            scores = jnp.where(visible, scores, HIDE)
        prob = jnp.exp(scores)
        score_grad = prob * dot(value, da_ref[at, :], NT)
        return prob.astype(BF16), score_grad.astype(BF16)

    tail_length = tk_ref.shape[1]

    for qi in range(count):
        at = block_at(qi)
        total = jnp.zeros((LANES, size), F32)
        for t in range(0, tail_length, 2 * size):
            here = pl.ds(t, min(2 * size, tail_length - t))
            key = tk_ref[0, here, :]
            _, score_grad = pieces(key, tv_ref[0, here, :], at)
            total = total + dot(key.T, score_grad)
        dqt_ref[:, at] = total

    lane_here = lanes_of(size)
    low_here = lane_here < HEAD_SIZE

    for ki in range(count):
        own = block_at(ki)
        key = k_ref[0, own, :]
        value = v_ref[0, own, :]
        key_turned = key.T

        def one(at, sums, masked=False, key=key, value=value, key_turned=key_turned):
            key_sum, value_sum = sums
            prob, score_grad = pieces(key, value, at, masked)
            dqt_ref[:, at] += dot(key_turned, score_grad)
            return (
                key_sum + dot(score_grad, q_ref[0, at, :]),
                value_sum + dot(prob, da_ref[at, :]),
            )

        start = (jnp.zeros((size, LANES), F32), jnp.zeros((size, LANES), F32))
        sums = one(own, start, True)
        for qi in range(ki + 1, count):
            sums = one(block_at(qi), sums)
        key_sum, value_sum = sums
        sums_ref[own, :] = key_sum
        for piece in range(size // rows):
            here = slice(piece * rows, (piece + 1) * rows)
            g_ref[ki * (size // rows) + piece, 0, :, LANES:] = value_sum[here].astype(BF16)

    tri = triangle(rows, False)

    def finish(i, carry):
        b = blocks - 1 - i
        at = pl.ds(pl.multiple_of(b * rows, rows), rows)
        query = dqt_ref[:, at].T
        key = sums_ref[at, :]
        decay_grad = query[:, 64:65] - key[:, 67:68]
        suffix = running_sum(tri, decay_grad, lane) + carry
        logit = forget_column(rest_ref[b, 0].astype(F32))
        forget_grad = suffix / (1.0 + jnp.exp(logit))
        both = jnp.where(low, query * SCALE, swap_halves(key))
        rest = jnp.where(low, g_ref[b, 0, :, LANES:].astype(F32), jnp.where(lane == 64, forget_grad, 0.0))
        g_ref[b, 0, :, :LANES] = both.astype(BF16)
        g_ref[b, 0, :, LANES:] = rest.astype(BF16)
        return suffix[0:1, :]

    lax.fori_loop(0, blocks, finish, jnp.zeros((1, 1), F32))


def attend_back(
    order, saved, tail_key, tail_value, mixture, packed_grad, pay, place, saved_place, grad_place, out_places, out_place, before, carry, after
):
    blocks, _, rows, _ = pay.shape
    length = blocks * rows
    tail_length = tail_key.shape[1]
    size = min(512, length)
    pair = lambda j: (place, 0, 0)
    tail = pl.BlockSpec((1, tail_length, LANES), pair)
    whole = pl.BlockSpec((1, length, LANES), lambda j: (saved_place, 0, 0))
    grad = pl.BlockSpec((blocks, 1, rows // 2, LANES), lambda j: (0, grad_place, 0, 0))
    sent = (blocks, out_places, rows, 2 * LANES)
    out = pl.BlockSpec((blocks, 1, rows, 2 * LANES), lambda j: (0, out_place, 0, 0))
    return order.call(
        functools.partial(attend_back_kernel, size),
        "attend_back",
        (1,),
        [(array, whole) for array in saved]
        + [
            (tail_key, tail),
            (tail_value, tail),
            (mixture, whole),
            (packed_grad, grad),
            (pay, pl.BlockSpec((blocks, 1, rows, LANES), lambda j: (0, saved_place, 0, 1))),
        ],
        [(sent, BF16, out)],
        22,
        scratch=[
            pltpu.VMEM((length, LANES), BF16),
            pltpu.VMEM((LANES, length), F32),
            pltpu.VMEM((length, LANES), F32),
        ],
        before=before,
        carry=carry,
        after=after,
    )


def take_pair(refs, pair):
    owners = refs[0].shape[0]
    owner, place = lax.rem(pair, owners), lax.div(pair, owners)
    block, start = None, 0
    for ref in refs:
        here = ref[owner, jnp.clip(place - start, 0, ref.shape[1] - 1)]
        block = here if block is None else jnp.where(place >= start, here, block)
        start += ref.shape[1]
    return block


def group_of(heads, ref, first_pair, group, low_half):
    owners = ref.shape[0]

    def packed(head):
        if head >= heads:
            return jnp.zeros(ref.shape[2:], F32)
        pair = first_pair + head
        if isinstance(pair, int):
            return ref[pair % owners, pair // owners].astype(F32)
        return ref[lax.rem(pair, owners), lax.div(pair, owners)].astype(F32)

    return unpack_rows(low_half, packed(2 * group), packed(2 * group + 1))


def gate_kernel(heads, first, ap_ref, gl_ref, o_ref, sent_ref):
    rows, cols = o_ref.shape
    half_low = lanes_of(STRIP) < HEAD_SIZE
    pair = (first + pl.program_id(0)) * heads
    for group in range(cols // LANES):
        at = slice(group * LANES, (group + 1) * LANES)
        mixture = group_of(heads, ap_ref, pair, group, half_low)
        gated = (mixture * jax.nn.sigmoid(gl_ref[:, at])).astype(BF16)
        o_ref[:, at] = gated
        for z in range(sent_ref.shape[0]):
            sent_ref[z, :, at] = gated


def gate(order, heads, packed, gl, rows, first, count, copies, before):
    total, cols = gl.shape
    here = pl.BlockSpec((rows, cols), lambda i: (first + i, 0))
    return order.call(
        functools.partial(gate_kernel, heads, first),
        "gate",
        (count,),
        [(packed, pl.BlockSpec(packed.shape, lambda i: (0, 0, 0, 0))), (gl, here)],
        [
            ((total, cols), BF16, here),
            (
                (copies, count * rows, cols),
                BF16,
                pl.BlockSpec((copies, rows, cols), lambda i: (0, i, 0)),
            ),
        ],
        2 * count,
        before=before,
    )


def pack_kernel(*refs):
    out_ref, at = refs[-1], 0
    for ref in refs[:-1]:
        wide = ref.shape[1]
        out_ref[:, at : at + wide] = ref[...]
        at += wide


def pack(order, arrays):
    rows = arrays[0].shape[0]
    wide = sum(array.shape[1] for array in arrays)
    whole = lambda i: (0, 0)
    return order.call(
        pack_kernel,
        "pack",
        (1,),
        [(array, pl.BlockSpec(array.shape, whole)) for array in arrays],
        [((rows, wide), BF16, pl.BlockSpec((rows, wide), whole))],
        2,
    )[0]


def feed_kernel(
    parts,
    own,
    rank_ref,
    x_ref,
    dy_ref,
    wo_ref,
    wg_ref,
    wu_ref,
    wd_ref,
    wg_far_ref,
    wu_far_ref,
    wd_far_ref,
    gain_ref,
    *refs,
):
    o_ref, c_ref, u_ref, dgu_ref, hid_ref, out_ref, dc_ref, out_acc, dc_acc = refs
    step = pl.program_id(0)
    last = pl.num_programs(0) - 1

    def attended():
        return dot(o_ref[0], wo_ref[...], NT)

    @pl.when(step == 0)
    def _():
        hid_ref[...] = x_ref[...].astype(F32) + attended()

    @pl.when((step > 0) & (step < parts))
    def _():
        hid_ref[...] += attended()

    @pl.when(step == parts - 1)
    def _():
        hidden = hid_ref[...]
        c_ref[...] = (hidden * rms_factor(hidden) * gain_ref[...]).astype(BF16)
        out_acc[...] = jnp.zeros_like(out_acc)
        dc_acc[...] = jnp.zeros_like(dc_acc)

    def chunk(w_gate, w_up, w_down):
        c = c_ref[...]
        gr = dot(c, w_gate[...])
        ur = dot(c, w_up[...])
        sig = jax.nn.sigmoid(gr)
        silu = gr * sig
        u = (silu * ur).astype(BF16)
        du = dot(dy_ref[...], w_down[...])
        dgr = (du * ur * sig * (1.0 + gr * (1.0 - sig))).astype(BF16)
        dur = (du * silu).astype(BF16)
        out_acc[...] += dot(u, w_down[...], NT)
        dc_acc[...] += dot(dgr, w_gate[...], NT) + dot(dur, w_up[...], NT)
        return u, dgr, dur

    @pl.when((step >= parts) & (step < parts + own))
    def _():
        u, dgr, dur = chunk(wg_ref, wu_ref, wd_ref)
        wide = u.shape[1]
        u_ref[...] = u
        dgu_ref[:, :wide] = dgr
        dgu_ref[:, wide:] = dur

    @pl.when(step >= parts + own)
    def _():
        chunk(wg_far_ref, wu_far_ref, wd_far_ref)

    @pl.when(step == last)
    def _():
        out_ref[...] = out_acc[...].astype(BF16)
        dc_ref[...] = dc_acc[...].astype(BF16)


def feed(order, rank, x, dy, o_all, near, far, gain_row, ff, chunk, group, before):
    parts, rows, cols = o_all.shape
    total, width = x.shape
    own = ff // chunk
    offset = parts * cols // chunk
    others = (far.shape[1] - parts * cols) // (3 * ff)
    steps = parts + (1 + others) * own
    whole = lambda i, rank: (0, 0)
    here = lambda i, rank: (group, 0)
    early = lambda i: jnp.minimum(i, parts - 1)
    mine = lambda i: jnp.clip(i - parts, 0, own - 1)

    def near_strip(k):
        return pl.BlockSpec((width, chunk), lambda i, rank: (0, k * own + mine(i)))

    def far_strip(k):
        def place(i, rank):
            s = jnp.maximum(i - parts - own, 0)
            return (0, offset + (s // own * 3 + k) * own + s % own)

        return pl.BlockSpec((width, chunk), place)

    wide = pl.BlockSpec((rows, width), whole)
    return order.call(
        functools.partial(feed_kernel, parts, own),
        "feed",
        (steps,),
        [
            (x, pl.BlockSpec((rows, width), here)),
            (dy, pl.BlockSpec((rows, width), here)),
            (far, pl.BlockSpec((width, cols), lambda i, rank: (0, early(i)))),
            (near, near_strip(0)),
            (near, near_strip(1)),
            (near, near_strip(2)),
            (far, far_strip(0)),
            (far, far_strip(1)),
            (far, far_strip(2)),
            (gain_row, pl.BlockSpec((1, width), whole)),
        ]
        + [(o_all, pl.BlockSpec((1, rows, cols), lambda i, rank: (rank[0] ^ early(i), 0, 0)))],
        [
            ((total, width), BF16, pl.BlockSpec((rows, width), here)),
            ((total, ff), BF16, pl.BlockSpec((rows, chunk), lambda i, rank: (group, mine(i)))),
            (
                (total, 2 * ff),
                BF16,
                pl.BlockSpec((rows, 2 * chunk), lambda i, rank: (group, mine(i))),
            ),
            ((rows, width), F32, wide),
            ((rows, width), BF16, wide),
            ((rows, width), BF16, wide),
        ],
        37,
        scratch=[pltpu.VMEM((rows, width), F32), pltpu.VMEM((rows, width), F32)],
        before=before,
        scalars=(rank,),
    )


def norm_back(source, factor, gain_row, upstream):
    scaled = upstream * gain_row
    inner = jnp.mean(scaled * source, axis=-1, keepdims=True)
    return factor * scaled - source * (factor * factor * factor) * inner


def hidden_back_kernel(
    heads,
    first,
    start,
    with_old,
    dc_ref,
    dc_other_ref,
    hid_ref,
    dy_ref,
    gain_ref,
    w_ref,
    gl_ref,
    ap_ref,
    *refs,
):
    if with_old:
        old_ref, *refs = refs
    dhb_ref, dgl_ref, dh_ref, dg_ref, *dap_refs = refs
    rows, cols = gl_ref.shape
    pair = (first + pl.program_id(0)) * heads
    if with_old:

        @pl.when(pl.program_id(0) == 0)
        def _():
            dap_refs[0][...] = old_ref[...]

    hidden = hid_ref[...]
    factor = rms_factor(hidden)
    dc = dc_ref[...].astype(F32) + dc_other_ref[...].astype(F32)
    dh = dy_ref[...].astype(F32) + norm_back(hidden, factor, gain_ref[...], dc)
    dg_ref[0] = jnp.sum(dc * hidden * factor, axis=0, keepdims=True)
    dh_ref[...] = dh
    dhb = dh.astype(BF16)
    dhb_ref[...] = dhb
    gated_grad = dot(dhb, w_ref[...])
    half_low = lanes_of(STRIP) < HEAD_SIZE
    for group in range(cols // LANES):
        at = slice(group * LANES, (group + 1) * LANES)
        mixture = group_of(heads, ap_ref, pair, group, half_low)
        gate_value = jax.nn.sigmoid(gl_ref[:, at])
        grad = gated_grad[:, at]
        dgl_ref[:, at] = (grad * mixture * gate_value * (1.0 - gate_value)).astype(BF16)
        for half, packed in enumerate(pack_rows(half_low, grad * gate_value)):
            if 2 * group + half < heads:
                put_pair(dap_refs, pair + 2 * group + half, packed.astype(BF16), start=start)


def hidden_back(
    order, heads, dc, dc_other, hidden, dy, gain_row, weights, gl, packed, rows, first, places, old, before, carry
):
    total, cols = gl.shape
    group, width = dc.shape
    count = group // rows
    whole = lambda i: (0, 0)
    here = lambda i: (first + i, 0)
    part = pl.BlockSpec((rows, width), lambda i: (i, 0))
    every = lambda shape: pl.BlockSpec(shape, lambda i: (0,) * len(shape))
    sent = [(packed.shape[0], stop - start, rows // 2, LANES) for start, stop in places]
    return order.call(
        functools.partial(hidden_back_kernel, heads, first, places[0][0], bool(old)),
        "hidden_back",
        (count,),
        [
            (dc, part),
            (dc_other, part),
            (hidden, part),
            (dy, pl.BlockSpec((rows, width), here)),
            (gain_row, pl.BlockSpec((1, width), whole)),
            (weights, pl.BlockSpec((width, cols), whole)),
            (gl, pl.BlockSpec((rows, cols), here)),
            (packed, every(packed.shape)),
        ]
        + [(array, every(array.shape)) for array in old],
        [
            ((total, width), BF16, pl.BlockSpec((rows, width), here)),
            ((total, cols), BF16, pl.BlockSpec((rows, cols), here)),
            ((group, width), F32, part),
            ((count, 1, width), F32, pl.BlockSpec((1, 1, width), lambda i: (i, 0, 0))),
        ]
        + [(shape, BF16, every(shape)) for shape in sent],
        4 * count,
        before=before,
        carry=carry,
    )


def project_back_kernel(
    heads,
    first,
    arrays,
    upper_ref,
    raw_ref,
    x_ref,
    dgl_ref,
    w_ref,
    gq_ref,
    gk_ref,
    *refs,
):
    g_refs = refs[:arrays]
    grads_ref, *da_refs, sums_ref, all_ref, da_ref = refs[arrays:]
    first_pair = (first + pl.program_id(0)) * heads
    rows, cols = dgl_ref.shape
    width = x_ref.shape[1]
    lane = lanes_of(rows)
    low = lane < HEAD_SIZE
    zero = jnp.zeros(lane.shape, F32)
    sums = [jnp.zeros((1, LANES), F32), jnp.zeros((1, LANES), F32)]

    def head_back(raw, upstream, gain_row, which):
        factor = lax.rsqrt(per_head(low, raw * raw) + EPSILON)
        scaled = upstream * gain_row
        inner = per_head(low, scaled * raw)
        sums[which] += jnp.sum(upstream * raw * factor, axis=0, keepdims=True)
        return factor * scaled - raw * (factor * factor * factor) * inner

    forget = zero
    for group in range(cols // LANES):
        at = group * LANES
        here = slice(at, at + LANES)
        pair = (2 * group, 2 * group + 1)
        held = [take_pair(g_refs, first_pair + h).astype(F32) if h < heads else None for h in pair]
        both = [zero if block is None else block[:, :LANES] for block in held]
        rest = [zero if block is None else block[:, LANES:] for block in held]
        query = head_back(raw_ref[:, here], merge_pair(low, *both), gq_ref[...], 0)
        key = head_back(
            raw_ref[:, cols + at : cols + at + LANES],
            merge_swapped(low, *both),
            gk_ref[...],
            1,
        )
        all_ref[:, here] = query.astype(BF16)
        all_ref[:, cols + at : cols + at + LANES] = key.astype(BF16)
        value = merge_pair(low, *rest)
        all_ref[:, 2 * cols + at : 2 * cols + at + LANES] = value.astype(BF16)
        for h, block in zip(pair, rest):
            if h < heads:
                forget = jnp.where(lane == h, block[:, 64:65], forget)
    all_ref[:, 3 * cols : 4 * cols] = dgl_ref[...]
    all_ref[:, 4 * cols :] = forget.astype(BF16)
    grads_ref[:, : 3 * cols] = all_ref[:, : 3 * cols]
    grads_ref[:, 3 * cols :] = all_ref[:, 4 * cols :]
    da = dot(all_ref[...], w_ref[...], NT)
    da_ref[...] = da
    half = rows // 2
    upper = upper_ref[0]
    for ref, part in zip(da_refs, (upper, 1 - upper)):
        ref[0] = da_ref[pl.ds(pl.multiple_of(part * half, half), half), :].astype(BF16)
    x = x_ref[...].astype(F32)
    sums_ref[0, :, :width] = jnp.sum(da * x * rms_factor(x), axis=0, keepdims=True)
    sums_ref[0, :, width : width + LANES] = sums[0]
    sums_ref[0, :, width + LANES : width + 2 * LANES] = sums[1]
    sums_ref[0, :, width + 2 * LANES :] = jnp.sum(forget, axis=0, keepdims=True)


def project_back(
    order, heads, upper, returned, raw, x, dgl, weights, gq_row, gk_row, rows, first, count, before, after, carry
):
    total, cols = dgl.shape
    width, wide = weights.shape
    half = rows // 2
    whole = lambda i, upper: (0, 0)
    here = lambda i, upper: (first + i, 0)
    row = pl.BlockSpec((1, LANES), whole)
    sums = width + 3 * LANES
    da = [((count, half, width), BF16, pl.BlockSpec((1, half, width), lambda i, upper: (i, 0, 0)))] * 2
    return order.call(
        functools.partial(project_back_kernel, heads, first, len(returned)),
        "project_back",
        (count,),
        [
            (raw, pl.BlockSpec((rows, 2 * cols), here)),
            (x, pl.BlockSpec((rows, width), here)),
            (dgl, pl.BlockSpec((rows, cols), here)),
            (weights, pl.BlockSpec((width, wide), whole)),
            (gq_row, row),
            (gk_row, row),
        ]
        + [(array, pl.BlockSpec(array.shape, lambda i, upper: (0, 0, 0, 0))) for array in returned],
        [((total, wide - cols), BF16, pl.BlockSpec((rows, wide - cols), here))]
        + da
        + [((count, 1, sums), F32, pl.BlockSpec((1, 1, sums), lambda i, upper: (i, 0, 0)))],
        6 * count,
        scratch=[pltpu.VMEM((rows, wide), BF16), pltpu.VMEM((rows, width), F32)],
        before=before,
        scalars=(upper,),
        after=after,
        carry=carry,
    )


def input_back_kernel(rank_ref, x_ref, dh_ref, gain_ref, own_ref, *refs):
    *passed, out_ref = refs
    rank, count = rank_ref[0], len(passed) + 1
    da = own_ref[0].astype(F32)
    for t, ref in enumerate(passed):
        taken = jnp.where(pl.program_id(1) == 0, rank == t + 1, rank == count - 2 - t)
        da = jnp.where(taken, ref[0].astype(F32), da)
    x = x_ref[...].astype(F32)
    out_ref[...] = dh_ref[...] + norm_back(x, rms_factor(x), gain_ref[...], da)


def input_back(order, rank, summed, x, dh, gain_row, rows, first, before, after):
    total, width = x.shape
    size, half, _ = summed[0].shape
    here = pl.BlockSpec((half, width), lambda m, i, rank: (2 * (first + m) + i, 0))
    one = pl.BlockSpec((half, width), lambda m, i, rank: (2 * m + i, 0))
    passing = pl.BlockSpec((1, half, width), lambda m, i, rank: (m, 0, 0))
    return order.call(
        input_back_kernel,
        "input_back",
        (size, 2),
        [(x, here), (dh, one), (gain_row, pl.BlockSpec((1, width), lambda m, i, rank: (0, 0)))]
        + [(block, passing) for block in summed],
        [((total, width), F32, here)],
        4 * size,
        before=before,
        scalars=(rank,),
        after=after,
    )


def layer_out_kernel(hid_ref, part_ref, other_ref, out_ref):
    total = hid_ref[...] + (part_ref[...].astype(F32) + other_ref[...].astype(F32))
    out_ref[...] = total.astype(BF16)


def layer_output(order, hidden, part, other, group, total, before, after):
    rows, width = hidden.shape
    tiles = 4
    tile = rows // tiles
    one = pl.BlockSpec((tile, width), lambda i: (i, 0))
    return order.call(
        layer_out_kernel,
        "layer_out",
        (tiles,),
        [(hidden, one), (part, one), (other, one)],
        [((total, width), BF16, pl.BlockSpec((tile, width), lambda i: (tiles * group + i, 0)))],
        4,
        before=before,
        after=after,
    )


def pad_to(array, size, axis):
    missing = size - array.shape[axis]
    if missing == 0:
        return array
    widths = [(0, missing if i == axis else 0) for i in range(array.ndim)]
    return jnp.pad(array, widths)


def turned_kernel(*refs):
    out_ref, at = refs[-1], 0
    for left_ref, right_ref in zip(refs[:-1:2], refs[1:-1:2]):
        wide = right_ref.shape[1]
        product = lax.dot_general(
            left_ref[...], right_ref[...], (((0,), (0,)), ((), ())), preferred_element_type=F32
        )
        out_ref[:, at : at + wide] = product.astype(BF16)
        at += wide


def turned_products(order, pairs, us):
    height = pairs[0][0].shape[1]
    tile = 512 if height % 512 == 0 else 256
    ins, wide = [], 0
    for left, right in pairs:
        ins.append((left, pl.BlockSpec((left.shape[0], tile), lambda i: (0, i))))
        ins.append((right, pl.BlockSpec(right.shape, lambda i: (0, 0))))
        wide += right.shape[1]
    return order.call(
        turned_kernel,
        "turned_products",
        (height // tile,),
        ins,
        [((height, wide), BF16, pl.BlockSpec((tile, wide), lambda i: (i, 0)))],
        us,
    )[0]


def owned_kernel(own, left_ref, right_ref, sums_ref, out_ref):
    product = lax.dot_general(
        left_ref[...], right_ref[...], (((0,), (0,)), ((), ())), preferred_element_type=F32
    ).astype(BF16)
    for i in range(out_ref.shape[0]):
        out_ref[i, :own] = product[i * own : (i + 1) * own]
        out_ref[i, own:] = sums_ref[i]


def owned_product(order, left, right, sums, us, carry):
    rows, height = left.shape
    owners, extra, wide = sums.shape
    own = height // owners
    step = 1
    while own * step % LANES:
        step += 1
    return order.call(
        functools.partial(owned_kernel, own),
        "owned_product",
        (owners // step,),
        [
            (left, pl.BlockSpec((rows, own * step), lambda i: (0, i))),
            (right, pl.BlockSpec((rows, wide), lambda i: (0, 0))),
            (sums, pl.BlockSpec((step, extra, wide), lambda i: (i, 0, 0))),
        ],
        [((owners, own + extra, wide), BF16, pl.BlockSpec((step, own + extra, wide), lambda i: (i, 0, 0)))],
        us,
        carry=carry,
    )


def line_steps(count):
    return [((t - 1, t), (count - t, count - 1 - t)) for t in range(1, count)]


def fold_kernel(*refs):
    count = len(refs) // 3
    for i in range(count):
        total = refs[2 * i][...].astype(F32) + refs[2 * i + 1][...].astype(F32)
        refs[2 * count + i][...] = total.astype(BF16)


def fold(order, pairs, after):
    size, rows, width = pairs[0][0].shape
    block = pl.BlockSpec((1, rows, width), lambda i: (i, 0, 0))
    return order.call(
        fold_kernel,
        "fold",
        (size,),
        [(array, block) for pair in pairs for array in pair],
        [((size, rows, width), BF16, block) for _ in pairs],
        0.2 * len(pairs),
        after=after,
    )


def exchanged(array, axis, flip):
    count = lax.axis_size(axis)
    return lax.ppermute(array, axis, [(i, i ^ flip) for i in range(count)])


def to_all(array, axis):
    return lax.all_to_all(array, axis, 0, 0, tiled=True)


def small_sum(row, axis):
    flip = 1
    while flip < lax.axis_size(axis):
        row = row + exchanged(row, axis, flip)
        flip *= 2
    return row


def shards(
    inputs,
    cotangent,
    tail_keys,
    tail_values,
    tail_forget,
    gain_one,
    gain_two,
    w_query,
    w_key,
    w_value,
    w_forget,
    forget_bias,
    query_gain,
    key_gain,
    w_outgate,
    w_out,
    w_gate,
    w_up,
    w_down,
):
    micros, rows, width = inputs.shape
    total = micros * rows
    own_cols = w_query.shape[1]
    heads = w_forget.shape[1]
    ff = w_gate.shape[1]
    seq_count = lax.axis_size("seq")
    head_count = lax.axis_size("head")
    seq_rank = lax.axis_index("seq")
    head_rank = lax.axis_index("head")
    cols = -(-own_cols // LANES) * LANES
    pair_total = micros * heads
    pairs = -(-pair_total // seq_count)
    padded_pairs = pairs * seq_count
    tail_length = tail_keys.shape[1]

    x = inputs.reshape(total, width)
    dy = cotangent.reshape(total, width)

    small = jnp.concatenate([w_forget, gain_one[:, None], gain_two[:, None]], axis=1)
    first_shard = jnp.concatenate(
        [pad_to(w, cols, 1) for w in (w_query, w_key, w_value, w_outgate)]
        + [pad_to(small, LANES, 1)],
        axis=1,
    )
    first = lax.all_gather(first_shard, "seq", axis=0, tiled=True)
    near_shard = jnp.concatenate([w_gate, w_up, w_down.T], axis=1)
    near = lax.all_gather(near_shard, "seq", axis=0, tiled=True)
    split = 3 * ff // 2
    outs, units, early = [pad_to(w_out.T, cols, 1)], [(near_shard[:, :split], near_shard[:, split:])], []
    flip = 1
    while flip < head_count:
        outs.append(exchanged(jnp.concatenate(outs, axis=1), "head", flip))
        if flip == 1:
            early.append(outs[-1])
        else:
            units += [tuple(exchanged(part, "head", flip) for part in unit) for unit in units]
        flip *= 2
    far_parts = outs + [part for unit in units[1:] for part in unit]
    rank = head_rank.astype(jnp.int32)[None]
    upper = (rank >= head_count // 2).astype(jnp.int32)
    order = Order()
    gain_one_row = first[:, 4 * cols + heads].astype(F32)[None, :]
    gain_two_row = first[:, 4 * cols + heads + 1].astype(F32)[None, :]
    bias_here = lax.dynamic_slice_in_dim(forget_bias, head_rank * heads, heads, 0)
    bias_row = pad_to(bias_here[None, :], LANES, 1)
    gq_row = jnp.tile(query_gain.astype(F32), 2)[None, :]
    gk_row = jnp.tile(key_gain.astype(F32), 2)[None, :]

    tail_key_parts, tail_value_parts = [], []
    for j in range(pairs):
        p = jnp.minimum(j * seq_count + seq_rank, pair_total - 1)
        m, h = p // heads, p % heads
        tail_of = lambda array, wide: lax.dynamic_slice(
            array, (m, 0, h * wide), (1, tail_length, wide)
        )[0]
        forget = tail_of(tail_forget, 1)
        decay = jnp.cumsum(forget, axis=0) - jnp.sum(forget, axis=0, keepdims=True)
        high = lax.reduce_precision(decay, 8, 7)
        middle = lax.reduce_precision(decay - high, 8, 7)
        least = decay - high - middle
        ones = jnp.ones((tail_length, 3), BF16)
        parts = jnp.concatenate([-high, -middle, -least], axis=1).astype(BF16)
        tail_key_parts.append(
            pad_to(jnp.concatenate([tail_of(tail_keys, HEAD_SIZE), ones, parts], axis=1), LANES, 1)
        )
        tail_value_parts.append(
            pad_to(jnp.concatenate([tail_of(tail_values, HEAD_SIZE), ones], axis=1), LANES, 1)
        )
    tail_key, tail_value = jnp.stack(tail_key_parts), jnp.stack(tail_value_parts)

    a, raw, gl, *pays = project(
        order, heads, cols, seq_count, x, first, bias_row, gain_one_row, gq_row, gk_row, micros, early
    )
    pays = [to_all(pay, "seq") for pay in pays]
    kept, returned = [], []
    most = max(pairs - 1, 1)
    for j, pay in enumerate(pays):
        in_most = j < most
        packed, *saved = attend(
            order,
            pay,
            tail_key,
            tail_value,
            j,
            most if in_most else pairs - most,
            j if in_most else j - most,
            (packed,) if 0 < j < most else (),
        )
        kept.append((saved, pay, 0))
        if j >= most - 1:
            returned.append(to_all(packed, "seq"))
        if j == 0:
            far = lax.all_gather(pack(order, far_parts), "seq", axis=0, tiled=True)
    packed = jnp.concatenate(returned, axis=1)

    size = 2 if micros % 2 == 0 else 1
    groups = micros // size
    chunk = min(512, ff)
    gated, o_alls = (), []
    for g in range(groups):
        enough = (g + 1) * size * heads <= most * seq_count
        *gated, sent = gate(
            order, heads, returned[0] if enough else packed, gl, rows, g * size, size, head_count, gated
        )
        o_alls.append(to_all(sent, "head"))
    o = gated[0]

    hiddens, out_parts, dc_parts, dc_others = [], [], [], []
    dhs, gains_two = [], []
    late, carried = (), None
    early_places = size * heads // seq_count if groups > 1 else 0
    fed, backed = (), ()

    def back_to_heads(g, carry=()):
        nonlocal backed, late, carried
        places = [(early_places, pairs)]
        if g == 0 and early_places > 0:
            places = [(0, early_places)] + places
        *results, out_parts[g] = hidden_back(
            order,
            heads,
            dc_parts[g],
            dc_others[g],
            hiddens[g],
            dy,
            gain_two_row,
            far,
            gl,
            packed,
            rows,
            g * size,
            places,
            late,
            backed,
            carry + (out_parts[g],),
        )
        if carry:
            carried = results.pop()
        dhb, dgl, dh, gain, *sent = results
        backed, late = (dhb, dgl), (sent[-1],)
        dhs.append(dh)
        gains_two.append(gain)
        return sent[0]

    def scattered(grad):
        return lax.psum_scatter(grad, "seq", scatter_dimension=0, tiled=True)

    for g in range(groups):
        *fed, hidden, out_part, dc_part = feed(
            order, rank, x, dy, o_alls[g], near, far, gain_two_row, ff, chunk, g, fed
        )
        hiddens.append(hidden)
        out_parts.append(out_part)
        dc_parts.append(dc_part)
        dc_others.append(exchanged(dc_part, "head", 1))
        if g > 0:
            early_grads = back_to_heads(g - 1)
    c, u, dgu = fed
    unit_grads = scattered(turned_products(order, [(c, dgu), (dy, u)], 13))

    layer_out = ()

    def put_out(g, after=()):
        nonlocal layer_out
        other = exchanged(out_parts[g], "head", 1)
        layer_out = layer_output(order, hiddens[g], out_parts[g], other, g, total, layer_out, after)

    if early_places > 0:
        early_grads = to_all(early_grads, "seq")
    returned = []
    mixed, grad = (), ()
    for j in range(pairs):
        if j == early_places:
            back_to_heads(groups - 1)
            mixed = (turned_products(order, [(backed[0], o), (a, backed[1])], 8),)
            late_grads = to_all(late[0], "seq")
        sent = (early_grads, j) if j < early_places else (late_grads, j - early_places)
        saved, pay, place = kept[j]
        grad, *mixed = attend_back(
            order,
            saved[1:],
            tail_key,
            tail_value,
            saved[0],
            sent[0],
            pay,
            j,
            place,
            sent[1],
            most if j < most else pairs - most,
            j if j < most else j - most,
            (grad,) if 0 < j < most else (),
            tuple(mixed),
            (),
        )
        if j >= most - 1:
            returned.append(to_all(grad, "seq"))

    for out in range(groups):
        put_out(out)

    grads, streams, gains_one = (), [], []
    for g in range(groups):
        results = project_back(
            order,
            heads,
            upper,
            returned[:1] if (g + 1) * size * heads <= most * seq_count else returned,
            raw,
            x,
            backed[1],
            first,
            gq_row,
            gk_row,
            rows,
            g * size,
            size,
            grads,
            (unit_grads,) if g == 0 else (),
            mixed,
        )
        grads, da, gain, mixed = results[:1], results[1:3], results[3], results[4:]
        gains_one.append(gain)
        streams.append(da)

    hops = line_steps(head_count)
    moving = [sent for _, sent in streams]
    passed = [[] for _ in streams]
    for step in range(1, head_count + groups - 1):
        active = [(g, step - g) for g in range(groups) if 1 <= step - g < head_count]
        terms = []
        for g, t in active:
            kept, sent = streams[g]
            terms.append((lax.ppermute(moving[g], "head", hops[t - 1]), sent if t < head_count // 2 else kept))
        waited = tuple(blocks[-1] for blocks in passed if len(blocks) > 1)
        for (g, t), total_now in zip(active, fold(order, terms, waited)):
            moving[g] = total_now
            if t == head_count - 1:
                passed[g].append(total_now)
        if step == 1:
            one_sums = jnp.sum(jnp.concatenate(gains_one, axis=0), axis=0)
            two_sums = jnp.sum(jnp.concatenate(gains_two, axis=0), axis=0) * (1.0 / head_count)
            own_rows = gain_one.shape[0]
            shared = pad_to(one_sums[:, width:], 3 * LANES, 1)
            owned_sums = jnp.concatenate(
                [
                    one_sums[:, :width].reshape(seq_count, own_rows),
                    two_sums.reshape(seq_count, own_rows),
                    jnp.broadcast_to(shared, (seq_count, 3 * LANES)),
                ],
                axis=1,
            ).astype(BF16)
            owned_sums = jnp.pad(owned_sums[:, None], ((0, 0), (0, 15), (0, grads[0].shape[1] - owned_sums.shape[1])))
            head_grads, *mixed = owned_product(order, a, grads[0], owned_sums, 9, mixed)
            mixed_grads = scattered(mixed[0]) if mixed else mixed_grads
        for g in range(groups):
            if passed[g] and len(passed[g]) <= head_count - 1:
                passed[g].append(lax.ppermute(passed[g][-1], "head", hops[len(passed[g]) - 1]))
    for blocks in passed:
        while len(blocks) < head_count:
            blocks.append(lax.ppermute(blocks[-1], "head", hops[len(blocks) - 1]))

    head_grads = jnp.sum(to_all(head_grads, "seq").astype(F32), axis=0)
    sums = head_grads[own_rows : own_rows + 1]
    head_grads = head_grads[:own_rows]
    unit_grads, mixed_grads = unit_grads.astype(F32), mixed_grads.astype(F32)
    strips = [unit_grads[:, i * chunk : (i + 1) * chunk] for i in range(2 * ff // chunk)]
    grad_gate = jnp.concatenate(strips[0::2], axis=1)
    grad_up = jnp.concatenate(strips[1::2], axis=1)
    grad_down = unit_grads[:, 2 * ff :].T
    grad_out = mixed_grads[:, :own_cols].T

    gain_lanes = 2 * own_rows
    bias_at = gain_lanes + 2 * LANES
    bias_full = lax.dynamic_update_slice(
        jnp.zeros((1, forget_bias.shape[0]), F32), sums[:, bias_at : bias_at + heads], (0, head_rank * heads)
    )
    sums = small_sum(jnp.concatenate([sums[:, :bias_at], bias_full], axis=1), "head")[0]
    halves = sums[gain_lanes:bias_at].reshape(4, HEAD_SIZE)
    gq_total, gk_total = halves[0] + halves[1], halves[2] + halves[3]
    bias_total = sums[bias_at:]

    input_grad = ()
    for g in range(groups):
        input_grad = input_back(
            order,
            rank,
            passed[g],
            x,
            dhs[g],
            gain_one_row,
            rows,
            g * size,
            input_grad,
            (sums[None],) if g == groups - 1 else (),
        )

    input_grad, layer_out = input_grad[0], layer_out[0]
    shape = inputs.shape
    return (
        layer_out.reshape(shape),
        input_grad.reshape(shape),
        sums[:own_rows],
        sums[own_rows:gain_lanes],
        head_grads[:, :own_cols],
        head_grads[:, cols : cols + own_cols],
        head_grads[:, 2 * cols : 2 * cols + own_cols],
        head_grads[:, 3 * cols : 3 * cols + heads],
        bias_total,
        gq_total,
        gk_total,
        mixed_grads[:, cols : cols + own_cols],
        grad_out,
        grad_gate,
        grad_up,
        grad_down,
    )


def solution(mesh):
    by_rows = P("seq", "head")
    by_cols = P("head", "seq")
    placed = (
        P(None, "seq", None),
        P(None, "seq", None),
        P(None, None, "head"),
        P(None, None, "head"),
        P(None, None, "head"),
        P("seq"),
        P("seq"),
        by_rows,
        by_rows,
        by_rows,
        by_rows,
        P(),
        P(),
        P(),
        by_rows,
        by_cols,
        by_rows,
        by_rows,
        by_cols,
    )
    return jax.shard_map(
        shards,
        mesh=mesh,
        in_specs=placed,
        out_specs=(
            P(None, "seq", None),
            P(None, "seq", None),
            P("seq"),
            P("seq"),
            by_rows,
            by_rows,
            by_rows,
            by_rows,
            P(),
            P(),
            P(),
            by_rows,
            by_cols,
            by_rows,
            by_rows,
            by_cols,
        ),
        check_vma=False,
    )
```
